32 devices in a mesh: grp: 2 (over x), pool: 8 (over z, y), tp: 2 (over core).
Axes of the slice: x: 2, y: 2, z: 4, core: 2. Of those that a mesh axis runs over, the one named last changes fastest.
Arguments:
- hidden_states: bfloat16 [6144, 5120], P(('grp', 'pool'), 'tp'), parts along dimension 0, may hold values from -6 to 6
- kv_weight: bfloat16 [5120, 4, 256], P('tp'), may hold values from -0.078125 to 0.078125
- shrink_factors: bfloat16 [16, 5120, 64], P(('grp', 'pool'), 'tp'), parts along dimension 0, may hold values from -0.078125 to 0.078125
- expand_factors: bfloat16 [16, 64, 4, 256], P(('grp', 'pool')), parts along dimension 0, may hold values from -0.75 to 0.75
- adapter_ids: int32 [128], P(('grp', 'pool')), parts along dimension 0, may hold values from 0 to 7, as said below
- cache_lengths: int32 [128], P(('grp', 'pool')), parts along dimension 0, may hold values from 2 to 128, as said below
- tree_parents: int32 [128, 48], P(('grp', 'pool')), parts along dimension 0, may hold values from 0 to 46, as said below
- queries: bfloat16 [6144, 32, 128], P(('grp', 'pool'), 'tp'), parts along dimension 0, may hold values from -120 to 120
- cache_keys: bfloat16 [128, 128, 4, 128], P(('grp', 'pool'), None, 'tp'), parts along dimension 0, may hold values from -6 to 6
- cache_values: bfloat16 [128, 128, 4, 128], P(('grp', 'pool'), None, 'tp'), parts along dimension 0, may hold values from -6 to 6
- key_gain: float32 [128], replicated, may hold values from 0.1 to 1.9
Outputs:
- attention: bfloat16 [6144, 32, 128], P(('grp', 'pool'), 'tp'), parts along dimension 0
- tree_cache: bfloat16 [6144, 4, 256], P(('grp', 'pool'), 'tp'), parts along dimension 0
The draws below stay inside these ranges and needn't reach their ends.
There are 2 independent parts, one for each index of `grp`. The reference program is written for one: setup_inputs(seed, part) draws one part's arguments, and reference() takes and returns one part's arrays. A program takes and returns all parts, laid end to end along the dimension named above; an argument that names none is the same for every part. Nothing has to cross between parts.
Inputs may be any that keep to these rules, and one draw needn't show every extreme that they name: `adapter_ids`: the 8 requests on one index of pool name adapters of 8 different owners, the owner of adapter a being a; some owner's adapters are named by exactly one request of every index of pool. `cache_lengths`: some request holds exactly 128 positions. tree_parents[r, 0] = 0 and tree_parents[r, i] < i for i >= 1.
All inputs are finite; a program needn't handle non-finite values.
Results may differ from the reference program's by a relative error of at most 0.0054.
Values may be sent and summed in bfloat16 or wider, within the bound.
No kernel may reach another device: no remote copies, remote signals or barrier semaphores. Data moves between devices by JAX's collectives and lax.ppermute only.
A program may use at most 128 MiB of HBM per device.

```python
import math
import jax
import jax.numpy as jnp
from jax import lax

D = 5120
QH = 32
KVH = 4
HD = 128
RANK = 64
TREE = 48
CTX = 128
REQ_DEV = 8
ADP_DEV = 1
REQUESTS = 64
TOKENS = 3072
ADAPTERS = 8
N_POOL = 8


def cache_base(key):
    return jnp.clip(jax.random.normal(key, (REQUESTS, CTX, KVH, HD), jnp.float32), -6.0, 6.0)


def draw_cache_keys(key, part):
    base_keys = cache_base(key)
    return base_keys.astype(jnp.bfloat16)


def draw_queries(key, part):
    key = jax.random.fold_in(key, 31)
    drawn = jnp.clip(jax.random.normal(key, (REQUESTS, TREE, QH, HD), jnp.float32), -6.0, 6.0)
    return drawn.reshape(TOKENS, QH, HD).astype(jnp.bfloat16)


def draw_adapter_ids(key, part):
    key = jax.random.fold_in(key, 11)
    key_hot, key_score, key_local, key_order = jax.random.split(key, 4)
    hot_owner = jax.random.randint(key_hot, (), 0, N_POOL)
    owner_ids = jnp.arange(N_POOL, dtype=jnp.int32)
    scores = jax.random.randint(key_score, (N_POOL, N_POOL), 0, 1 << 20) * N_POOL + owner_ids[None, :]
    scores = jnp.where(owner_ids[None, :] == hot_owner, 1 << 30, scores)
    unused, owners = lax.top_k(scores, REQ_DEV)
    owners = jax.random.permutation(key_order, owners, axis=1, independent=True)
    local_index = jax.random.randint(key_local, (N_POOL, REQ_DEV), 0, ADP_DEV)
    return (owners * ADP_DEV + local_index).reshape(REQUESTS).astype(jnp.int32)


def draw_cache_lengths(key, part):
    key = jax.random.fold_in(key, 51)
    key_len, key_spot = jax.random.split(key)
    lengths = jax.random.randint(key_len, (REQUESTS,), 2, CTX + 1)
    chosen_request = jax.random.randint(key_spot, (), 0, REQUESTS)
    return jnp.where(jnp.arange(REQUESTS) == chosen_request, CTX, lengths).astype(jnp.int32)


def draw_tree_parents(key, part):
    key = jax.random.fold_in(key, 41)
    node_ids = jnp.arange(TREE, dtype=jnp.int32)
    drawn_parents = jax.random.randint(key, (REQUESTS, TREE), 0, jnp.maximum(node_ids, 1)[None, :])
    return jnp.where(node_ids[None, :] == 0, 0, drawn_parents).astype(jnp.int32)


def block_levels(stream_key, dims, cuts, smallest, top_value):
    def one(dim, shards_of):
        draws = jax.random.uniform(jax.random.fold_in(jax.random.fold_in(stream_key, 6), dim), (shards_of,), jnp.float32, smallest / len(cuts), top_value / len(cuts))
        return jnp.repeat(jnp.exp(draws), dims[dim] // shards_of).reshape((-1,) + (1,) * (len(dims) - dim - 1))

    loudness = one(*cuts[0])
    for cut in cuts[1:]:
        loudness = loudness * one(*cut)
    return loudness


def normal_values(rng, extent, spread, bound, cuts=(), held_as=jnp.bfloat16):
    factor_of = block_levels(rng, extent, cuts, -0.22, 0.18) if cuts else 1.0
    array = jax.random.normal(rng, extent, jnp.float32) * spread * factor_of
    return jnp.minimum(jnp.maximum(array, -bound), bound).astype(held_as)


def setup_inputs(seed: int = 0, part: int = 0) -> dict:
    keys = jax.random.split(jax.random.key(seed), 12)
    own_keys = jax.random.split(jax.random.fold_in(keys[11], part), 12)
    return {
        "hidden_states": normal_values(own_keys[0], (TOKENS, D), 1.0, 6.0, ((0, 8), (1, 2))),
        "kv_weight": normal_values(keys[1], (D, KVH, 2 * HD), D ** -0.5, 0.078125, ((0, 2),)),
        "shrink_factors": normal_values(own_keys[2], (ADAPTERS, D, RANK), D ** -0.5, 0.078125, ((0, 8), (1, 2))),
        "expand_factors": normal_values(own_keys[3], (ADAPTERS, RANK, KVH, 2 * HD), RANK ** -0.5, 0.75, ((0, 8),)),
        "adapter_ids": draw_adapter_ids(jax.random.fold_in(jax.random.fold_in(keys[11], part), 71), part),
        "cache_lengths": draw_cache_lengths(jax.random.fold_in(jax.random.fold_in(keys[11], part), 71), part),
        "tree_parents": draw_tree_parents(jax.random.fold_in(jax.random.fold_in(keys[11], part), 71), part),
        "queries": draw_queries(jax.random.fold_in(jax.random.fold_in(keys[11], part), 71), part),
        "cache_keys": draw_cache_keys(jax.random.fold_in(jax.random.fold_in(keys[11], part), 71), part),
        "cache_values": normal_values(own_keys[9], (REQUESTS, CTX, KVH, HD), 1.0, 6.0, ((0, 8), (2, 2))),
        "key_gain": jnp.clip(1.0 + 0.18 * jax.random.normal(keys[10], (HD,), jnp.float32), 0.1, 1.9),
    }


def ancestry(tree_parents):
    node_count = tree_parents.shape[-1]
    node_ids = jnp.arange(node_count, dtype=jnp.int32)
    parent_hot = (tree_parents[..., :, None] == node_ids).astype(jnp.float32)
    identity_mat = (node_ids[:, None] == node_ids[None, :]).astype(jnp.float32)
    reach = jnp.minimum(parent_hot + identity_mat, 1.0)
    span_now = 1
    while span_now < node_count:
        reach = jnp.minimum(jnp.einsum('...ij,...jk->...ik', reach, reach, precision=lax.Precision.HIGHEST), 1.0)
        span_now = span_now * 2
    return reach

def rotary(vectors, positions):
    head_size = vectors.shape[-1]
    half_size = head_size // 2
    frequency = jnp.exp(jnp.arange(half_size, dtype=jnp.float32) * (-2.0 * math.log(1000000.0) / head_size))
    angles = positions[..., None] * frequency
    cosine = jnp.cos(angles)
    sine_part = jnp.sin(angles)
    front_half = vectors[..., :half_size]
    back_half = vectors[..., half_size:]
    return jnp.concatenate([front_half * cosine - back_half * sine_part, back_half * cosine + front_half * sine_part], -1)

def prepare(projected, key_gain, positions, head_size):
    key_part = projected[..., :head_size]
    value_part = projected[..., head_size:]
    norm_scale = lax.rsqrt(lax.optimization_barrier(jnp.mean(key_part * key_part, -1, keepdims=True)) + 1e-06)
    key_part = rotary(key_part * norm_scale * key_gain, positions)
    return jnp.concatenate([key_part, value_part], -1).astype(jnp.bfloat16)

def attend(query_rows, cache_keys, cache_values, tree_cache, length, reach):
    tree_size, head_count, head_size = query_rows.shape
    context = cache_keys.shape[0]
    groups = cache_keys.shape[1]
    per_group = head_count // groups
    query_blocks = query_rows.astype(jnp.float32).reshape(tree_size, groups, per_group, head_size)
    score_scale = 1.0 / math.sqrt(head_size)
    tree_keys = tree_cache[..., :head_size].astype(jnp.float32)
    tree_values = tree_cache[..., head_size:].astype(jnp.float32)
    cache_scores = jnp.einsum('tgpd,cgd->gptc', query_blocks, cache_keys.astype(jnp.float32), precision=lax.Precision.HIGHEST) * score_scale
    tree_scores = jnp.einsum('tgpd,jgd->gptj', query_blocks, tree_keys, precision=lax.Precision.HIGHEST) * score_scale
    cache_scores = jnp.where(jnp.arange(context) < length, cache_scores, -1e+30)
    tree_scores = jnp.where(reach > 0.5, tree_scores, -1e+30)
    scores = jnp.concatenate([cache_scores, tree_scores], -1)
    row_max = lax.optimization_barrier(jnp.max(scores, -1, keepdims=True))
    exponent = jnp.exp(scores - row_max)
    rounded = (exponent / lax.optimization_barrier(jnp.sum(exponent, -1, keepdims=True))).astype(jnp.bfloat16)
    weights = lax.optimization_barrier(rounded).astype(jnp.float32)
    output = jnp.einsum('gptc,cgd->tgpd', weights[..., :context], cache_values.astype(jnp.float32), precision=lax.Precision.HIGHEST)
    output = output + jnp.einsum('gptj,jgd->tgpd', weights[..., context:], tree_values, precision=lax.Precision.HIGHEST)
    return output.reshape(tree_size, head_count, head_size).astype(jnp.bfloat16)

def reference(hidden_states, kv_weight, shrink_factors, expand_factors, adapter_ids, cache_lengths, tree_parents, queries, cache_keys, cache_values, key_gain):
    flat_weight = kv_weight.reshape(D, KVH * 2 * HD)

    def per_request(pieces):
        row_block, adapter, length, parent_row, query_rows, key_rows, value_rows = pieces
        base_part = jnp.dot(row_block, flat_weight, preferred_element_type=jnp.float32)
        shrunk = jnp.dot(row_block, shrink_factors[adapter], preferred_element_type=jnp.float32)
        delta = jnp.dot(shrunk, expand_factors[adapter].reshape(RANK, KVH * 2 * HD).astype(jnp.float32), precision=lax.Precision.HIGHEST)
        projected = (base_part + delta).reshape(TREE, KVH, 2 * HD)
        reach = ancestry(parent_row)
        positions = length.astype(jnp.float32) + lax.optimization_barrier(jnp.sum(reach, -1)) - 1.0
        tree_cache = prepare(projected, key_gain, positions[:, None], HD)
        output = attend(query_rows, key_rows, value_rows, tree_cache, length, reach)
        return (output, tree_cache)
    attention, tree_cache = lax.map(per_request, (hidden_states.reshape(REQUESTS, TREE, D), adapter_ids, cache_lengths, tree_parents, queries.reshape(REQUESTS, TREE, QH, HD), cache_keys, cache_values))
    return (attention.reshape(TOKENS, QH, HD), tree_cache.reshape(TOKENS, KVH, 2 * HD))
```

```python
import math

import jax
import jax.numpy as jnp
import numpy as np
from jax import lax
from jax.experimental import pallas as pl
from jax.experimental.pallas import tpu as pltpu
from jax.sharding import PartitionSpec as P

F32 = jnp.float32
BF16 = jnp.bfloat16


def ring_order(count):
    if count == 8:
        return list(range(0, count, 2)) + list(range(count - 1, 0, -2))
    return list(range(count))


def ancestry(tree_parents):
    node_count = tree_parents.shape[-1]
    node_ids = jnp.arange(node_count, dtype=jnp.int32)
    parent_hot = tree_parents[..., :, None] == node_ids
    identity_mat = node_ids[:, None] == node_ids[None, :]
    reach = (parent_hot | identity_mat).astype(BF16)
    span_now = 1
    while span_now < node_count:
        product = jnp.einsum("...ij,...jk->...ik", reach, reach, preferred_element_type=F32)
        reach = jnp.minimum(product, 1.0).astype(BF16)
        span_now = span_now * 2
    return reach.astype(F32)


def finish_kernel(
    request_ref,
    base_ref,
    shrunk_ref,
    expand_ref,
    cosine_ref,
    sine_ref,
    gain_ref,
    bias_ref,
    query_ref,
    key_ref,
    value_ref,
    *rest,
):
    attention_ref, cache_ref = rest[-2:]
    tree_size, heads, head_size = query_ref.shape
    kv_heads = key_ref.shape[1]
    context = key_ref.shape[2]
    per_group = heads // kv_heads
    score_scale = math.log2(math.e) / math.sqrt(head_size)
    expand = expand_ref[0]
    shrunk = shrunk_ref[0]
    high = shrunk.astype(BF16)
    left = shrunk - high.astype(F32)
    middle = left.astype(BF16)
    low = (left - middle.astype(F32)).astype(BF16)
    delta = (
        jnp.dot(low, expand, preferred_element_type=F32)
        + jnp.dot(middle, expand, preferred_element_type=F32)
        + jnp.dot(high, expand, preferred_element_type=F32)
    )
    projected = base_ref[...] + delta
    cosine = cosine_ref[...]
    sine = sine_ref[...]
    gain = gain_ref[...]
    queries = query_ref[...].astype(F32)
    bias = bias_ref[...]
    bias = jnp.broadcast_to(bias[:, None, :], (tree_size, per_group, bias.shape[1])).reshape(
        tree_size * per_group, bias.shape[1]
    )
    pad = jnp.zeros((bias.shape[1] - context - tree_size, head_size), BF16)
    outputs = []
    caches = []
    for g in range(kv_heads):
        at = 2 * head_size * g
        key = projected[:, at : at + head_size]
        value = projected[:, at + head_size : at + 2 * head_size]
        norm = lax.rsqrt(jnp.mean(key * key, -1, keepdims=True) + 1e-06)
        key = key * norm * gain
        key = key * cosine + pltpu.roll(key, head_size // 2, 1) * sine
        caches.append(jnp.concatenate([key, value], -1))
        keys = jnp.concatenate([key_ref[0, g], key.astype(BF16), pad], 0)
        values = jnp.concatenate([value_ref[0, g], value.astype(BF16), pad], 0)
        rows = queries[:, per_group * g : per_group * (g + 1), :].reshape(
            tree_size * per_group, head_size
        )
        scores = lax.dot_general(
            rows.astype(BF16), keys, (((1,), (1,)), ((), ())), preferred_element_type=F32
        )
        scores = scores + bias
        row_max = jnp.max(scores, -1, keepdims=True)
        exponent = jnp.exp2((scores - row_max) * score_scale)
        total = jnp.sum(exponent, -1, keepdims=True)
        weights = (exponent * (1.0 / total)).astype(BF16)
        output = jnp.dot(weights, values, preferred_element_type=F32)
        outputs.append(output.reshape(tree_size, per_group, head_size))
    attention_ref[...] = jnp.concatenate(outputs, 1).astype(BF16)
    cache_ref[...] = jnp.stack(caches, 1).astype(BF16)


def finish(batch, shared, previous):
    request_ids, shrunk, expand = batch
    base, cosine, sine, gain, bias, queries, keys, values = shared
    count, tree_size, rank_size = shrunk.shape
    rows, heads, head_size = queries.shape
    columns = base.shape[1]
    kv_heads, context = keys.shape[1], keys.shape[2]
    row_block = lambda width: pl.BlockSpec((tree_size, width), lambda i, ids: (ids[i], 0))
    in_specs = [
        row_block(columns),
        pl.BlockSpec((1, tree_size, rank_size), lambda i, ids: (i, 0, 0)),
        pl.BlockSpec((1, rank_size, columns), lambda i, ids: (i, 0, 0)),
        row_block(head_size),
        row_block(head_size),
        pl.BlockSpec((1, head_size), lambda i, ids: (0, 0)),
        row_block(bias.shape[1]),
        pl.BlockSpec((tree_size, heads, head_size), lambda i, ids: (ids[i], 0, 0)),
        pl.BlockSpec((1, kv_heads, context, head_size), lambda i, ids: (ids[i], 0, 0, 0)),
        pl.BlockSpec((1, kv_heads, context, head_size), lambda i, ids: (ids[i], 0, 0, 0)),
    ]
    operands = [request_ids, base, shrunk, expand, cosine, sine, gain, bias, queries, keys, values]
    aliases = {}
    if previous is not None:
        aliases = {len(operands): 0, len(operands) + 1: 1}
        operands += list(previous)
        in_specs += [pl.BlockSpec(memory_space=pl.ANY)] * 2
    return pl.pallas_call(
        finish_kernel,
        grid_spec=pltpu.PrefetchScalarGridSpec(
            num_scalar_prefetch=1,
            grid=(count,),
            in_specs=in_specs,
            out_specs=[
                pl.BlockSpec((tree_size, heads, head_size), lambda i, ids: (ids[i], 0, 0)),
                pl.BlockSpec((tree_size, kv_heads, 2 * head_size), lambda i, ids: (ids[i], 0, 0)),
            ],
        ),
        out_shape=[
            jax.ShapeDtypeStruct((rows, heads, head_size), BF16),
            jax.ShapeDtypeStruct((rows, kv_heads, 2 * head_size), BF16),
        ],
        input_output_aliases=aliases,
        compiler_params=pltpu.CompilerParams(vmem_limit_bytes=32 * 1024 * 1024),
        cost_estimate=pl.CostEstimate(
            flops=count * 80_000_000, bytes_accessed=count * 900_000, transcendentals=count * 200_000
        ),
    )(*operands)


def per_device(
    hidden_states,
    kv_weight,
    shrink_factors,
    expand_factors,
    adapter_ids,
    cache_lengths,
    tree_parents,
    queries,
    cache_keys,
    cache_values,
    key_gain,
):
    requests, tree_size = tree_parents.shape
    row_count, half_width = hidden_states.shape
    kv_heads, kv_width = (kv_weight.shape[1], kv_weight.shape[2])
    head_size = kv_width // 2
    rank_size = shrink_factors.shape[2]
    context = cache_keys.shape[1]
    pool_count = lax.axis_size("pool")
    heads_here = kv_heads // lax.axis_size("tp")
    columns = heads_here * kv_width
    me = lax.axis_index("pool")
    core = lax.axis_index("tp")
    swap = [(0, 1), (1, 0)]

    shrink = shrink_factors[0].T
    expand = lax.dynamic_slice_in_dim(expand_factors[0], core * heads_here, heads_here, 1)
    cut = (half_width + columns) // 2 - columns
    first = jnp.concatenate([expand.reshape(rank_size, columns), shrink[:, :cut]], 1)
    second = shrink[:, cut:]

    order = ring_order(pool_count)
    onward = [(order[i], order[(i + 1) % pool_count]) for i in range(pool_count)]
    backward = [(b, a) for a, b in onward]
    order_array = jnp.asarray(np.array(order, np.int32))
    place_array = jnp.asarray(np.argsort(np.array(order)).astype(np.int32))
    place = place_array[me]

    def owner_at(offset):
        return order_array[(place + offset + pool_count) % pool_count]

    arrivals = [[(owner_at(0), first, second)]]
    front = rear = (first, second)
    for step in range(1, pool_count // 2):
        front = tuple(lax.ppermute(piece, "pool", onward) for piece in front)
        rear = tuple(lax.ppermute(piece, "pool", backward) for piece in rear)
        arrivals.append([(owner_at(-step), *front), (owner_at(step), *rear)])
    arrivals.append(
        [
            (
                owner_at(pool_count // 2),
                lax.ppermute(front[0], "pool", onward),
                lax.ppermute(rear[1], "pool", backward),
            )
        ]
    )

    base_part = jnp.dot(
        hidden_states,
        kv_weight.reshape(half_width, kv_heads * kv_width),
        preferred_element_type=F32,
    )
    base_away = lax.dynamic_slice_in_dim(base_part, (1 - core) * columns, columns, 1)
    base_here = lax.dynamic_slice_in_dim(base_part, core * columns, columns, 1)
    base = base_here + lax.ppermute(base_away, "tp", swap)

    reach = ancestry(tree_parents)
    positions = cache_lengths.astype(F32)[:, None] + jnp.sum(reach, -1) - 1.0
    half_size = head_size // 2
    frequency = jnp.exp(
        jnp.arange(half_size, dtype=F32) * (-2.0 * math.log(1000000.0) / head_size)
    )
    angles = positions.reshape(row_count, 1) * frequency
    cosine = jnp.cos(angles)
    sine = jnp.sin(angles)
    cosine = jnp.concatenate([cosine, cosine], 1)
    sine = jnp.concatenate([-sine, sine], 1)
    cache_valid = jnp.arange(context)[None, :] < cache_lengths[:, None]
    cache_valid = jnp.broadcast_to(cache_valid[:, None, :], (requests, tree_size, context))
    span = -(-(context + tree_size) // 128) * 128
    spare = jnp.zeros((requests, tree_size, span - context - tree_size), bool)
    allowed = jnp.concatenate([cache_valid, reach > 0.5, spare], -1)
    bias = jnp.where(allowed, 0.0, -1e30).astype(F32).reshape(row_count, span)
    keys = cache_keys.transpose(0, 2, 1, 3)
    values = cache_values.transpose(0, 2, 1, 3)
    shared = (base, cosine, sine, key_gain.reshape(1, head_size), bias, queries, keys, values)

    def shrunk_of(owner, one, two):
        hot = adapter_ids == owner
        request = jnp.argmax(hot).astype(jnp.int32)
        rows = lax.dynamic_slice_in_dim(hidden_states, request * tree_size, tree_size, 0)
        partial = lax.dot_general(
            rows[:, :cut], one[:, columns:], (((1,), (1,)), ((), ())), preferred_element_type=F32
        ) + lax.dot_general(
            rows[:, cut:], two, (((1,), (1,)), ((), ())), preferred_element_type=F32
        )
        return request, partial, one[:, :columns]

    if pool_count == requests:
        groups = [sum(arrivals, [])]
    else:
        groups = None
    if groups is not None:
        outputs = None
        for group in groups:
            found = [shrunk_of(*arrival) for arrival in group]
            request_ids = jnp.stack([item[0] for item in found])
            partial = jnp.stack([item[1] for item in found])
            shrunk = partial + lax.ppermute(partial, "tp", swap)
            batch = (request_ids, shrunk, jnp.stack([item[2] for item in found]))
            outputs = finish(batch, shared, outputs)
    else:
        flat = sum(arrivals, [])
        owners = jnp.stack([arrival[0] for arrival in flat])
        found = [shrunk_of(*arrival) for arrival in flat]
        slot = jnp.argmax(adapter_ids[:, None] == owners[None, :], 1)
        partial = jnp.stack([item[1] for item in found])[slot]
        shrunk = partial + lax.ppermute(partial, "tp", swap)
        batch = (
            jnp.arange(requests, dtype=jnp.int32),
            shrunk,
            jnp.stack([item[2] for item in found])[slot],
        )
        outputs = finish(batch, shared, None)
    return tuple(outputs)


def solution(mesh):
    placed = (
        P(("grp", "pool"), "tp"),
        P("tp", None, None),
        P(("grp", "pool"), "tp", None),
        P(("grp", "pool"), None, None, None),
        P(("grp", "pool")),
        P(("grp", "pool")),
        P(("grp", "pool"), None),
        P(("grp", "pool"), "tp", None),
        P(("grp", "pool"), None, "tp", None),
        P(("grp", "pool"), None, "tp", None),
        P(),
    )
    return jax.shard_map(
        per_device,
        mesh=mesh,
        in_specs=placed,
        out_specs=(P(("grp", "pool"), "tp", None), P(("grp", "pool"), "tp", None)),
        check_vma=False,
    )
```

```python
import functools
import math

import jax
import jax.numpy as jnp
import numpy as np
from jax import lax
from jax.experimental import pallas as pl
from jax.experimental.pallas import tpu as pltpu
from jax.sharding import PartitionSpec as P

F32 = jnp.float32
BF16 = jnp.bfloat16


def ring_order(count):
    if count == 8:
        return list(range(0, count, 2)) + list(range(count - 1, 0, -2))
    return list(range(count))


def sorting_matrix(rows, columns, inner, source_inner):
    row = lax.broadcasted_iota(jnp.int32, (rows, columns), 0)
    column = lax.broadcasted_iota(jnp.int32, (rows, columns), 1)
    return (column == (row % inner) * source_inner + row // inner).astype(F32).astype(BF16)


def pack_kernel(core_ref, shrink_ref, expand_ref, first_ref, second_ref, *, cut, heads_here):
    rank_size = shrink_ref.shape[0]
    groups = expand_ref.shape[0] // rank_size
    heads = groups // 2
    ranks = 256 // groups
    row = lax.broadcasted_iota(jnp.int32, (2 * heads_here * ranks, 256), 0)
    column = lax.broadcasted_iota(jnp.int32, (2 * heads_here * ranks, 256), 1)
    group = row // ranks
    head = core_ref[0] * heads_here + group // 2
    pick = (column == (row % ranks) * groups + (group % 2) * heads + head).astype(F32).astype(BF16)
    columns = 2 * heads_here * 128
    for block in range(rank_size // ranks):
        sorted_rows = jnp.dot(
            pick, expand_ref[256 * block : 256 * (block + 1), :], preferred_element_type=F32
        ).astype(BF16)
        for g in range(2 * heads_here):
            first_ref[ranks * block : ranks * (block + 1), 128 * g : 128 * (g + 1)] = sorted_rows[
                ranks * g : ranks * (g + 1), :
            ]
    first_ref[:, columns:] = shrink_ref[:, :cut]
    second_ref[...] = shrink_ref[:, cut:]


def pack(core, shrink, expand_rows, cut, heads_here):
    rank_size, half_width = shrink.shape
    columns = 2 * heads_here * 128
    return pl.pallas_call(
        functools.partial(pack_kernel, cut=cut, heads_here=heads_here),
        grid_spec=pltpu.PrefetchScalarGridSpec(
            num_scalar_prefetch=1,
            grid=(1,),
            in_specs=[
                pl.BlockSpec(shrink.shape, lambda i, c: (0, 0)),
                pl.BlockSpec(expand_rows.shape, lambda i, c: (0, 0)),
            ],
            out_specs=[
                pl.BlockSpec((rank_size, columns + cut), lambda i, c: (0, 0)),
                pl.BlockSpec((rank_size, half_width - cut), lambda i, c: (0, 0)),
            ],
        ),
        out_shape=[
            jax.ShapeDtypeStruct((rank_size, columns + cut), BF16),
            jax.ShapeDtypeStruct((rank_size, half_width - cut), BF16),
        ],
        name="pack",
    )(core, shrink, expand_rows)


def base_kernel(core_ref, hidden_ref, weight_ref, here_ref, away_ref, total_ref, sorted_ref):
    step = pl.program_id(0)
    depth, width = sorted_ref.shape
    groups = weight_ref.shape[0] // depth
    heads = groups // 2
    span = 256 // groups
    order = sorting_matrix(256, 256, span, groups)
    for block in range(depth // (2 * span)):
        at = 512 * block
        pair = jnp.concatenate(
            [weight_ref[at : at + 256, :], weight_ref[at + 256 : at + 512, :]], 1
        )
        rows = jnp.dot(order, pair, preferred_element_type=F32).astype(BF16)
        for group in range(groups):
            tile, head = group // heads, group % heads
            lanes = slice(256 * head + 128 * tile, 256 * head + 128 * (tile + 1))
            for half in range(2):
                top = 2 * span * block + span * half
                sorted_ref[top : top + span, lanes] = rows[
                    span * group : span * (group + 1), 128 * half : 128 * (half + 1)
                ]
    product = jnp.dot(hidden_ref[...], sorted_ref[...], preferred_element_type=F32)

    @pl.when(step == 0)
    def _():
        total_ref[...] = product

    @pl.when(step > 0)
    def _():
        total_ref[...] += product

    @pl.when(step == pl.num_programs(0) - 1)
    def _():
        columns = here_ref.shape[1]

        @pl.when(core_ref[0] == 0)
        def _():
            here_ref[...] = total_ref[:, :columns]
            away_ref[...] = total_ref[:, columns:]

        @pl.when(core_ref[0] == 1)
        def _():
            here_ref[...] = total_ref[:, columns:]
            away_ref[...] = total_ref[:, :columns]


def base_product(core, hidden_states, weight_rows, width):
    rows, half_width = hidden_states.shape
    groups = weight_rows.shape[0] // half_width
    depth = 512
    return pl.pallas_call(
        base_kernel,
        grid_spec=pltpu.PrefetchScalarGridSpec(
            num_scalar_prefetch=1,
            grid=(half_width // depth,),
            in_specs=[
                pl.BlockSpec((rows, depth), lambda i, c: (0, i)),
                pl.BlockSpec((depth * groups, 128), lambda i, c: (i, 0)),
            ],
            out_specs=[
                pl.BlockSpec((rows, width // 2), lambda i, c: (0, 0)),
                pl.BlockSpec((rows, width // 2), lambda i, c: (0, 0)),
            ],
            scratch_shapes=[pltpu.VMEM((rows, width), F32), pltpu.VMEM((depth, width), BF16)],
        ),
        out_shape=[jax.ShapeDtypeStruct((rows, width // 2), F32)] * 2,
        compiler_params=pltpu.CompilerParams(vmem_limit_bytes=24 * 1024 * 1024),
        cost_estimate=pl.CostEstimate(
            flops=4_000_000_000, bytes_accessed=9_000_000, transcendentals=0
        ),
        name="base",
    )(core, hidden_states, weight_rows)


def tree_kernel(length_ref, parent_ref, frequency_ref, *rest, context):
    cosine_ref, sine_ref, bias_ref = rest[-3:]
    requests, nodes = parent_ref.shape
    span = bias_ref.shape[1]
    node = lax.broadcasted_iota(jnp.int32, (nodes, nodes), 0)
    same = node == lax.broadcasted_iota(jnp.int32, (nodes, nodes), 1)
    parents = parent_ref[...]
    below = [
        (same | (parents[r : r + 1, :] == node)).astype(F32).astype(BF16) for r in range(requests)
    ]
    reached = 1
    while 2 * reached < nodes:
        below = [
            jnp.minimum(jnp.dot(b, b, preferred_element_type=F32), 1.0).astype(BF16) for b in below
        ]
        reached = 2 * reached
    lane = lax.broadcasted_iota(jnp.int32, (nodes, 128), 1)
    sign = jnp.where(lane < 64, -1.0, 1.0)
    cache_lane = lax.broadcasted_iota(jnp.int32, (nodes, context), 1)
    spare = jnp.full((nodes, span - context - nodes), -1e30, F32)
    for r in range(requests):
        b = below[r]
        product = lax.dot_general(b, b, (((0,), (1,)), ((), ())), preferred_element_type=F32)
        reach = jnp.minimum(product, 1.0)
        length = length_ref[r]
        positions = length.astype(F32) + jnp.sum(reach, -1, keepdims=True) - 1.0
        angles = positions * frequency_ref[...]
        rows = slice(nodes * r, nodes * (r + 1))
        cosine_ref[rows, :] = jnp.cos(angles)
        sine_ref[rows, :] = jnp.sin(angles) * sign
        bias_ref[rows, :] = jnp.concatenate(
            [
                jnp.where(cache_lane < length, 0.0, -1e30),
                jnp.where(reach > 0.5, 0.0, -1e30),
                spare,
            ],
            1,
        )


def tree_tables(cache_lengths, tree_parents, head_size, context, after):
    requests, nodes = tree_parents.shape
    span = -(-(context + nodes) // 128) * 128
    half_size = head_size // 2
    frequency = jnp.exp(
        jnp.arange(half_size, dtype=F32) * (-2.0 * math.log(1000000.0) / head_size)
    )
    frequency = jnp.concatenate([frequency, frequency]).reshape(1, head_size)
    whole = lambda shape: pl.BlockSpec(shape, lambda i, n: (0,) * len(shape))
    rows = requests * nodes
    return pl.pallas_call(
        functools.partial(tree_kernel, context=context),
        grid_spec=pltpu.PrefetchScalarGridSpec(
            num_scalar_prefetch=1,
            grid=(1,),
            in_specs=[whole(tree_parents.shape), whole((1, head_size))]
            + [pl.BlockSpec(memory_space=pl.ANY)] * len(after),
            out_specs=[whole((rows, head_size)), whole((rows, head_size)), whole((rows, span))],
        ),
        out_shape=[
            jax.ShapeDtypeStruct((rows, head_size), F32),
            jax.ShapeDtypeStruct((rows, head_size), F32),
            jax.ShapeDtypeStruct((rows, span), F32),
        ],
        cost_estimate=pl.CostEstimate(
            flops=50_000_000, bytes_accessed=8_000_000, transcendentals=100_000
        ),
        name="tree",
    )(cache_lengths, tree_parents, frequency, *after)


def shrink_kernel(request_ref, *refs, columns, cut):
    output_ref = refs[-1]
    contract = (((1,), (1,)), ((), ()))
    for b in range(output_ref.shape[0]):
        hidden_ref, one_ref, two_ref = refs[3 * b : 3 * b + 3]
        output_ref[b] = lax.dot_general(
            hidden_ref[:, :cut], one_ref[:, columns:], contract, preferred_element_type=F32
        ) + lax.dot_general(hidden_ref[:, cut:], two_ref[...], contract, preferred_element_type=F32)


def shrink_rows(request_ids, hidden_states, pieces, tree_size, columns, cut):
    rank_size = pieces[0][0].shape[0]
    in_specs, operands = [], []
    for b, (one, two) in enumerate(pieces):
        in_specs += [
            pl.BlockSpec((tree_size, hidden_states.shape[1]), lambda i, ids, b=b: (ids[b], 0)),
            pl.BlockSpec(one.shape, lambda i, ids: (0, 0)),
            pl.BlockSpec(two.shape, lambda i, ids: (0, 0)),
        ]
        operands += [hidden_states, one, two]
    count = len(pieces)
    return pl.pallas_call(
        functools.partial(shrink_kernel, columns=columns, cut=cut),
        grid_spec=pltpu.PrefetchScalarGridSpec(
            num_scalar_prefetch=1,
            grid=(1,),
            in_specs=in_specs,
            out_specs=pl.BlockSpec((count, tree_size, rank_size), lambda i, ids: (0, 0, 0)),
        ),
        out_shape=jax.ShapeDtypeStruct((count, tree_size, rank_size), F32),
        compiler_params=pltpu.CompilerParams(vmem_limit_bytes=24 * 1024 * 1024),
        cost_estimate=pl.CostEstimate(
            flops=count * 100_000_000, bytes_accessed=count * 1_500_000, transcendentals=0
        ),
        name="shrink",
    )(request_ids, *operands)


def finish_kernel(
    request_ref,
    here_ref,
    there_ref,
    shrunk_here_ref,
    shrunk_there_ref,
    cosine_ref,
    sine_ref,
    gain_ref,
    bias_ref,
    query_ref,
    key_ref,
    value_ref,
    *rest,
    count,
):
    expand_refs = rest[:count]
    attention_ref, cache_ref, expand_ref = rest[-3:]
    tree_size, heads, head_size = query_ref.shape
    kv_heads = cache_ref.shape[0] // (2 * tree_size)
    context = key_ref.shape[0] // kv_heads
    per_group = heads // kv_heads
    score_scale = math.log2(math.e) / math.sqrt(head_size)
    if count == 1:
        expand = expand_refs[0][...]
    else:
        for b in range(count):

            @pl.when(pl.program_id(0) == b)
            def _():
                expand_ref[...] = expand_refs[b][...]

        expand = expand_ref[...]
    shrunk = shrunk_here_ref[0] + shrunk_there_ref[0]
    high = shrunk.astype(BF16)
    left = shrunk - high.astype(F32)
    middle = left.astype(BF16)
    low = (left - middle.astype(F32)).astype(BF16)
    delta = (
        jnp.dot(low, expand, preferred_element_type=F32)
        + jnp.dot(middle, expand, preferred_element_type=F32)
        + jnp.dot(high, expand, preferred_element_type=F32)
    )
    projected = (here_ref[...] + there_ref[...]) + delta
    cosine = cosine_ref[...]
    sine = sine_ref[...]
    gain = gain_ref[...]
    cached = jnp.dot(
        sorting_matrix(kv_heads * context, kv_heads * context, context, kv_heads),
        jnp.concatenate([key_ref[...], value_ref[...]], 1),
        preferred_element_type=F32,
    ).astype(BF16)
    queries = query_ref[...].astype(F32)
    bias = bias_ref[...]
    bias = jnp.broadcast_to(bias[:, None, :], (tree_size, per_group, bias.shape[1])).reshape(
        tree_size * per_group, bias.shape[1]
    )
    pad = jnp.zeros((bias.shape[1] - context - tree_size, head_size), BF16)
    outputs, new_keys, new_values = [], [], []
    for g in range(kv_heads):
        at = 2 * head_size * g
        key = projected[:, at : at + head_size]
        value = projected[:, at + head_size : at + 2 * head_size].astype(BF16)
        norm = lax.rsqrt(jnp.mean(key * key, -1, keepdims=True) + 1e-06)
        key = key * norm * gain
        key = (key * cosine + pltpu.roll(key, head_size // 2, 1) * sine).astype(BF16)
        new_keys.append(key)
        new_values.append(value)
        keys = jnp.concatenate([cached[context * g : context * (g + 1), :head_size], key, pad], 0)
        values = jnp.concatenate(
            [cached[context * g : context * (g + 1), head_size:], value, pad], 0
        )
        rows = queries[:, per_group * g : per_group * (g + 1), :].reshape(
            tree_size * per_group, head_size
        )
        scores = lax.dot_general(
            rows.astype(BF16), keys, (((1,), (1,)), ((), ())), preferred_element_type=F32
        )
        scores = scores + bias
        row_max = jnp.max(scores, -1, keepdims=True)
        exponent = jnp.exp2((scores - row_max) * score_scale)
        total = jnp.sum(exponent, -1, keepdims=True)
        weights = (exponent * (1.0 / total)).astype(BF16)
        output = jnp.dot(weights, values, preferred_element_type=F32)
        outputs.append(output.reshape(tree_size, per_group, head_size))
    attention_ref[...] = jnp.concatenate(outputs, 1).astype(BF16)
    stacked = jnp.concatenate(new_keys + new_values, 0)
    size = stacked.shape[0]
    cache_ref[...] = jnp.dot(
        sorting_matrix(size, size, size // tree_size, tree_size),
        stacked,
        preferred_element_type=F32,
    ).astype(BF16)


def finish(batch, shared, previous):
    request_ids, shrunk_here, shrunk_there, pieces = batch
    here, there, cosine, sine, gain, bias, queries, key_rows, value_rows, context = shared
    count, tree_size, rank_size = shrunk_here.shape
    rows, heads, head_size = queries.shape
    columns = here.shape[1]
    kv_heads = columns // (2 * head_size)
    row_block = lambda width: pl.BlockSpec((tree_size, width), lambda i, ids: (ids[i], 0))
    shrunk_block = pl.BlockSpec((1, tree_size, rank_size), lambda i, ids: (i, 0, 0))
    cached_block = pl.BlockSpec((kv_heads * context, head_size), lambda i, ids: (ids[i], 0))
    in_specs = [
        row_block(columns),
        row_block(columns),
        shrunk_block,
        shrunk_block,
        row_block(head_size),
        row_block(head_size),
        pl.BlockSpec((1, head_size), lambda i, ids: (0, 0)),
        row_block(bias.shape[1]),
        pl.BlockSpec((tree_size, heads, head_size), lambda i, ids: (ids[i], 0, 0)),
        cached_block,
        cached_block,
    ] + [pl.BlockSpec((rank_size, columns), lambda i, ids: (0, 0))] * count
    operands = [
        request_ids,
        here,
        there,
        shrunk_here,
        shrunk_there,
        cosine,
        sine,
        gain,
        bias,
        queries,
        key_rows,
        value_rows,
        *pieces,
    ]
    aliases = {}
    if previous is not None:
        aliases = {len(operands): 0, len(operands) + 1: 1}
        operands += list(previous)
        in_specs += [pl.BlockSpec(memory_space=pl.ANY)] * 2
    cache_rows = 2 * kv_heads * tree_size
    return pl.pallas_call(
        functools.partial(finish_kernel, count=count),
        grid_spec=pltpu.PrefetchScalarGridSpec(
            num_scalar_prefetch=1,
            grid=(count,),
            in_specs=in_specs,
            out_specs=[
                pl.BlockSpec((tree_size, heads, head_size), lambda i, ids: (ids[i], 0, 0)),
                pl.BlockSpec((cache_rows, head_size), lambda i, ids: (ids[i], 0)),
            ],
            scratch_shapes=[pltpu.VMEM((rank_size, columns), BF16)],
        ),
        out_shape=[
            jax.ShapeDtypeStruct((rows, heads, head_size), BF16),
            jax.ShapeDtypeStruct((rows * 2 * kv_heads, head_size), BF16),
        ],
        input_output_aliases=aliases,
        compiler_params=pltpu.CompilerParams(vmem_limit_bytes=24 * 1024 * 1024),
        cost_estimate=pl.CostEstimate(
            flops=count * 500_000_000, bytes_accessed=count * 3_000_000, transcendentals=count * 200_000
        ),
        name="finish",
    )(*operands)


def per_device(
    hidden_states,
    kv_weight,
    shrink_factors,
    expand_factors,
    adapter_ids,
    cache_lengths,
    tree_parents,
    queries,
    cache_keys,
    cache_values,
    key_gain,
):
    requests, tree_size = tree_parents.shape
    row_count, half_width = hidden_states.shape
    kv_heads, kv_width = (kv_weight.shape[1], kv_weight.shape[2])
    head_size = kv_width // 2
    rank_size = shrink_factors.shape[2]
    context = cache_keys.shape[1]
    pool_count = lax.axis_size("pool")
    heads_here = kv_heads // lax.axis_size("tp")
    columns = heads_here * kv_width
    me = lax.axis_index("pool")
    core = lax.axis_index("tp").astype(jnp.int32).reshape(1)
    swap = [(0, 1), (1, 0)]

    def tile_rows(array):
        lead, heads = array.shape[0], array.shape[1]
        return array.reshape(lead, heads, 2, 128).transpose(0, 2, 1, 3).reshape(-1, 128)

    cut = (half_width + columns) // 2 - columns
    first, second = pack(
        core, shrink_factors[0].T, tile_rows(expand_factors[0]), cut, heads_here
    )

    order = ring_order(pool_count)
    onward = [(order[i], order[(i + 1) % pool_count]) for i in range(pool_count)]
    backward = [(b, a) for a, b in onward]
    half = pool_count // 2
    offsets = [[0]] + [[-step, step] for step in range(1, half)] + [[half]]
    flat_offsets = sum(offsets, [])
    owners = np.zeros((pool_count, pool_count), np.int32)
    for spot, index in enumerate(order):
        owners[index] = [order[(spot + offset) % pool_count] for offset in flat_offsets]
    owners_here = lax.dynamic_index_in_dim(jnp.asarray(owners), me, 0, keepdims=False)

    arrivals = [[(first, second)]]
    front = rear = (first, second)
    for step in range(1, half):
        front = tuple(lax.ppermute(piece, "pool", onward) for piece in front)
        rear = tuple(lax.ppermute(piece, "pool", backward) for piece in rear)
        arrivals.append([front, rear])
    arrivals.append(
        [(lax.ppermute(front[0], "pool", onward), lax.ppermute(rear[1], "pool", backward))]
    )

    here, away = base_product(core, hidden_states, tile_rows(kv_weight), kv_heads * kv_width)
    there = lax.ppermute(away, "tp", swap)
    after = [arrivals[1][1][1]]
    cosine, sine, bias = tree_tables(cache_lengths, tree_parents, head_size, context, after)
    shared = (
        here,
        there,
        cosine,
        sine,
        key_gain.reshape(1, head_size),
        bias,
        queries,
        cache_keys.reshape(-1, head_size),
        cache_values.reshape(-1, head_size),
        context,
    )

    hot = (adapter_ids[None, :] == owners_here[:, None]).astype(jnp.int32)
    asked = jnp.sum(hot * jnp.arange(requests, dtype=jnp.int32)[None, :], 1)
    outputs = None
    if pool_count == requests:
        groups = [arrivals[0] + arrivals[1] + arrivals[2]] + arrivals[3:]
        at = 0
        for group in groups:
            ids = asked[at : at + len(group)]
            at += len(group)
            partial = shrink_rows(ids, hidden_states, group, tree_size, columns, cut)
            batch = (ids, partial, lax.ppermute(partial, "tp", swap), [piece[0] for piece in group])
            outputs = finish(batch, shared, outputs)
    else:
        parts = []
        for slot, piece in enumerate(sum(arrivals, [])):
            parts.append(
                shrink_rows(asked[slot : slot + 1], hidden_states, [piece], tree_size, columns, cut)
            )
        slots = jnp.sum(hot * jnp.arange(pool_count, dtype=jnp.int32)[:, None], 0)
        partial = jnp.concatenate(parts, 0)[slots]
        expands = jnp.stack([piece[0][:, :columns] for piece in sum(arrivals, [])])[slots]
        ids = jnp.arange(requests, dtype=jnp.int32)
        pieces = [expands[r] for r in range(requests)]
        outputs = finish((ids, partial, lax.ppermute(partial, "tp", swap), pieces), shared, None)
    attention, cache_rows = outputs
    tree_cache = (
        cache_rows.reshape(row_count, 2, heads_here, head_size)
        .transpose(0, 2, 1, 3)
        .reshape(row_count, heads_here, kv_width)
    )
    return attention, tree_cache


def solution(mesh):
    placed = (
        P(("grp", "pool"), "tp"),
        P("tp", None, None),
        P(("grp", "pool"), "tp", None),
        P(("grp", "pool"), None, None, None),
        P(("grp", "pool")),
        P(("grp", "pool")),
        P(("grp", "pool"), None),
        P(("grp", "pool"), "tp", None),
        P(("grp", "pool"), None, "tp", None),
        P(("grp", "pool"), None, "tp", None),
        P(),
    )
    return jax.shard_map(
        per_device,
        mesh=mesh,
        in_specs=placed,
        out_specs=(P(("grp", "pool"), "tp", None), P(("grp", "pool"), "tp", None)),
        check_vma=False,
    )
```

```python
import functools
import math

import jax
import jax.numpy as jnp
import numpy as np
from jax import lax
from jax.experimental import pallas as pl
from jax.experimental.pallas import tpu as pltpu
from jax.sharding import PartitionSpec as P

F32 = jnp.float32
BF16 = jnp.bfloat16


ANYWHERE = pl.BlockSpec(memory_space=pl.ANY)


def shapes_of(arrays):
    return [jax.ShapeDtypeStruct(array.shape, array.dtype) for array in arrays]


def ring_order(count):
    if count == 8:
        return list(range(0, count, 2)) + list(range(count - 1, 0, -2))
    return list(range(count))


def sorting_matrix(rows, columns, inner, source_inner):
    row = lax.broadcasted_iota(jnp.int32, (rows, columns), 0)
    column = lax.broadcasted_iota(jnp.int32, (rows, columns), 1)
    return (column == (row % inner) * source_inner + row // inner).astype(F32).astype(BF16)


def picking_matrix(wanted, inner, groups, first_head):
    row = lax.broadcasted_iota(jnp.int32, (wanted * inner, 256), 0)
    column = lax.broadcasted_iota(jnp.int32, (wanted * inner, 256), 1)
    group = row // inner
    source = (group % 2) * (groups // 2) + first_head + group // 2
    return (column == (row % inner) * groups + source).astype(F32).astype(BF16)


def request_at(where, slot):
    me_ref, owner_ref, adapter_ref = where
    owner = owner_ref[me_ref[0], slot]
    request = jnp.int32(0)
    for r in range(1, adapter_ref.shape[0]):
        request = jnp.where(adapter_ref[r] == owner, jnp.int32(r), request)
    return request


def slot_of(where, request):
    me_ref, owner_ref, adapter_ref = where
    adapter = adapter_ref[request]
    slot = jnp.int32(0)
    for k in range(1, owner_ref.shape[1]):
        slot = jnp.where(owner_ref[me_ref[0], k] == adapter, jnp.int32(k), slot)
    return slot


def pack_kernel(core_ref, shrink_ref, expand_ref, first_ref, second_ref, *, cut, heads_here):
    rank_size = shrink_ref.shape[0]
    groups = expand_ref.shape[0] // rank_size
    ranks = 256 // groups
    pick = picking_matrix(2 * heads_here, ranks, groups, core_ref[0] * heads_here)
    columns = 2 * heads_here * 128
    for block in range(rank_size // ranks):
        sorted_rows = jnp.dot(
            pick, expand_ref[256 * block : 256 * (block + 1), :], preferred_element_type=F32
        ).astype(BF16)
        for g in range(2 * heads_here):
            first_ref[ranks * block : ranks * (block + 1), 128 * g : 128 * (g + 1)] = sorted_rows[
                ranks * g : ranks * (g + 1), :
            ]
    first_ref[:, columns:] = shrink_ref[:, :cut]
    second_ref[...] = shrink_ref[:, cut:]


def pack(core, shrink, expand_rows, cut, heads_here):
    rank_size, half_width = shrink.shape
    columns = 2 * heads_here * 128
    return pl.pallas_call(
        functools.partial(pack_kernel, cut=cut, heads_here=heads_here),
        grid_spec=pltpu.PrefetchScalarGridSpec(
            num_scalar_prefetch=1,
            grid=(1,),
            in_specs=[
                pl.BlockSpec(shrink.shape, lambda i, c: (0, 0)),
                pl.BlockSpec(expand_rows.shape, lambda i, c: (0, 0)),
            ],
            out_specs=[
                pl.BlockSpec((rank_size, columns + cut), lambda i, c: (0, 0)),
                pl.BlockSpec((rank_size, half_width - cut), lambda i, c: (0, 0)),
            ],
        ),
        out_shape=[
            jax.ShapeDtypeStruct((rank_size, columns + cut), BF16),
            jax.ShapeDtypeStruct((rank_size, half_width - cut), BF16),
        ],
        name="pack",
    )(core, shrink, expand_rows)


def base_kernel(core_ref, hidden_ref, weight_ref, *rest, held_count):
    total_ref, wide_ref = rest[-2:]
    here_ref, away_ref = rest[-2 - held_count - 2 : -2 - held_count]
    step = pl.program_id(0)
    depth = hidden_ref.shape[1]
    groups = weight_ref.shape[0] // depth
    heads = groups // 2
    wide_ref[...] = weight_ref[...].astype(F32)
    parts = []
    for head in range(heads):
        tiles = [
            wide_ref[pl.ds(tile * heads + head, depth, stride=groups), :].astype(BF16)
            for tile in range(2)
        ]
        parts.append(
            jnp.dot(hidden_ref[...], jnp.concatenate(tiles, 1), preferred_element_type=F32)
        )
    product = jnp.concatenate(parts, 1)

    @pl.when(step == 0)
    def _():
        total_ref[...] = product

    @pl.when(step > 0)
    def _():
        total_ref[...] += product

    @pl.when(step == pl.num_programs(0) - 1)
    def _():
        columns = here_ref.shape[1]

        @pl.when(core_ref[0] == 0)
        def _():
            here_ref[...] = total_ref[:, :columns]
            away_ref[...] = total_ref[:, columns:]

        @pl.when(core_ref[0] == 1)
        def _():
            here_ref[...] = total_ref[:, columns:]
            away_ref[...] = total_ref[:, :columns]


def base_product(core, hidden_states, weight_rows, width, held):
    rows, half_width = hidden_states.shape
    groups = weight_rows.shape[0] // half_width
    depth = half_width // 2
    return pl.pallas_call(
        functools.partial(base_kernel, held_count=len(held)),
        grid_spec=pltpu.PrefetchScalarGridSpec(
            num_scalar_prefetch=1,
            grid=(half_width // depth,),
            in_specs=[
                pl.BlockSpec((rows, depth), lambda i, c: (0, i)),
                pl.BlockSpec((depth * groups, 128), lambda i, c: (i, 0)),
            ]
            + [ANYWHERE] * len(held),
            out_specs=[pl.BlockSpec((rows, width // 2), lambda i, c: (0, 0))] * 2
            + [ANYWHERE] * len(held),
            scratch_shapes=[
                pltpu.VMEM((rows, width), F32),
                pltpu.VMEM((depth * groups, 128), F32),
            ],
        ),
        out_shape=[jax.ShapeDtypeStruct((rows, width // 2), F32)] * 2 + shapes_of(held),
        input_output_aliases={3 + k: 2 + k for k in range(len(held))},
        compiler_params=pltpu.CompilerParams(vmem_limit_bytes=56 * 1024 * 1024),
        cost_estimate=pl.CostEstimate(
            flops=4_000_000_000, bytes_accessed=9_000_000, transcendentals=0
        ),
        name="base",
    )(core, hidden_states, weight_rows, *held)


def tree_kernel(length_ref, parent_ref, frequency_ref, *rest, per_group):
    table_ref, bias_ref = rest[-2:]
    requests, nodes = parent_ref.shape
    head_size = frequency_ref.shape[1]
    node = lax.broadcasted_iota(jnp.int32, (nodes, nodes), 0)
    same = node == lax.broadcasted_iota(jnp.int32, (nodes, nodes), 1)
    spread = lax.broadcasted_iota(jnp.int32, (nodes, nodes * per_group), 1) // per_group
    spread = spread == lax.broadcasted_iota(jnp.int32, (nodes, nodes * per_group), 0)
    spread = spread.astype(F32).astype(BF16)
    parents = parent_ref[...]
    below = [
        (same | (parents[r : r + 1, :] == node)).astype(F32).astype(BF16) for r in range(requests)
    ]
    reached = 1
    while reached < nodes:
        below = [
            jnp.minimum(jnp.dot(b, b, preferred_element_type=F32), 1.0).astype(BF16) for b in below
        ]
        reached = 2 * reached
    lane = lax.broadcasted_iota(jnp.int32, (nodes, head_size), 1)
    sign = jnp.where(lane < head_size // 2, -1.0, 1.0)
    ones = jnp.ones((nodes, head_size), BF16)
    for r in range(requests):
        b = below[r]
        depth = lax.dot_general(b, ones, (((0,), (0,)), ((), ())), preferred_element_type=F32)
        positions = length_ref[r].astype(F32) + depth - 1.0
        angles = positions * frequency_ref[...]
        rows = slice(nodes * r, nodes * (r + 1))
        table_ref[rows, :] = jnp.concatenate([jnp.cos(angles), jnp.sin(angles) * sign], 1)
        wide = jnp.dot(b, spread, preferred_element_type=F32)
        bias_ref[rows, :] = jnp.where(wide > 0.5, 0.0, -1e30)


def tree_tables(cache_lengths, tree_parents, head_size, per_group, after):
    requests, nodes = tree_parents.shape
    half_size = head_size // 2
    frequency = np.exp(np.arange(half_size) * (-2.0 * math.log(1000000.0) / head_size))
    frequency = np.concatenate([frequency, frequency]).reshape(1, head_size).astype(np.float32)
    whole = lambda shape: pl.BlockSpec(shape, lambda i, n: (0,) * len(shape))
    rows = requests * nodes
    shapes = [(rows, 2 * head_size), (rows, nodes * per_group)]
    return pl.pallas_call(
        functools.partial(tree_kernel, per_group=per_group),
        grid_spec=pltpu.PrefetchScalarGridSpec(
            num_scalar_prefetch=1,
            grid=(1,),
            in_specs=[whole(tree_parents.shape), whole((1, head_size))] + [ANYWHERE] * len(after),
            out_specs=[whole(shape) for shape in shapes],
        ),
        out_shape=[jax.ShapeDtypeStruct(shape, F32) for shape in shapes],
        cost_estimate=pl.CostEstimate(
            flops=1_000_000_000, bytes_accessed=8_000_000, transcendentals=0
        ),
        name="tree",
    )(cache_lengths, tree_parents, frequency, *after)


def cache_kernel(length_ref, query_ref, key_ref, value_ref, *rest, first_request, held_count, kv_heads):
    output_ref, stat_ref = rest[-2 - held_count : len(rest) - held_count]
    tree_size, heads, head_size = query_ref.shape
    context = key_ref.shape[0] // kv_heads
    per_group = heads // kv_heads
    rows = tree_size * per_group
    score_scale = math.log2(math.e) / math.sqrt(head_size)
    length = length_ref[first_request + pl.program_id(0)]
    cached = jnp.dot(
        sorting_matrix(kv_heads * context, kv_heads * context, context, kv_heads),
        jnp.concatenate([key_ref[...], value_ref[...]], 1),
        preferred_element_type=F32,
    ).astype(BF16)
    queries = query_ref[...].astype(F32)
    allowed = lax.broadcasted_iota(jnp.int32, (context, rows), 0) < length
    stats = []
    for g in range(kv_heads):
        mine = slice(context * g, context * (g + 1))
        query = queries[:, per_group * g : per_group * (g + 1), :].reshape(rows, head_size)
        scores = lax.dot_general(
            cached[mine, :head_size],
            query.astype(BF16),
            (((1,), (1,)), ((), ())),
            preferred_element_type=F32,
        )
        scores = jnp.where(allowed, scores, -1e30)
        top = jnp.max(scores, 0, keepdims=True)
        exponent = jnp.exp2((scores - top) * score_scale)
        stats += [top, jnp.sum(exponent, 0, keepdims=True)]
        output_ref[rows * g : rows * (g + 1), :] = lax.dot_general(
            exponent.astype(BF16),
            cached[mine, head_size:],
            (((0,), (0,)), ((), ())),
            preferred_element_type=F32,
        )
    stats.append(jnp.zeros((stat_ref.shape[0] - len(stats), rows), F32))
    stat_ref[...] = jnp.concatenate(stats, 0)


def cache_attention(lengths, queries, key_rows, value_rows, kv_heads, first_request, count, held, after):
    rows, heads, head_size = queries.shape
    requests = lengths.shape[0]
    tree_size = rows // requests
    cached = key_rows.shape[0] // requests
    pair_rows = tree_size * heads
    return pl.pallas_call(
        functools.partial(
            cache_kernel, first_request=first_request, held_count=len(held), kv_heads=kv_heads
        ),
        grid_spec=pltpu.PrefetchScalarGridSpec(
            num_scalar_prefetch=1,
            grid=(count,),
            in_specs=[
                pl.BlockSpec((tree_size, heads, head_size), lambda i, n: (first_request + i, 0, 0)),
                pl.BlockSpec((cached, head_size), lambda i, n: (first_request + i, 0)),
                pl.BlockSpec((cached, head_size), lambda i, n: (first_request + i, 0)),
            ]
            + [ANYWHERE] * (len(held) + len(after)),
            out_specs=[
                pl.BlockSpec((pair_rows, head_size), lambda i, n: (i, 0)),
                pl.BlockSpec((8, pair_rows // kv_heads), lambda i, n: (i, 0)),
            ]
            + [ANYWHERE] * len(held),
        ),
        out_shape=[
            jax.ShapeDtypeStruct((count * pair_rows, head_size), F32),
            jax.ShapeDtypeStruct((count * 8, pair_rows // kv_heads), F32),
        ]
        + shapes_of(held),
        input_output_aliases={4 + k: 2 + k for k in range(len(held))},
        compiler_params=pltpu.CompilerParams(vmem_limit_bytes=24 * 1024 * 1024),
        cost_estimate=pl.CostEstimate(
            flops=count * 700_000_000, bytes_accessed=count * 2_000_000, transcendentals=0
        ),
        name="cached",
    )(lengths, queries, key_rows, value_rows, *held, *after)


def shrink_kernel(me_ref, owner_ref, adapter_ref, *refs, columns, cut):
    output_ref = refs[-1]
    contract = (((1,), (1,)), ((), ()))
    for b in range(output_ref.shape[0]):
        hidden_ref, one_ref, two_ref = refs[3 * b : 3 * b + 3]
        output_ref[b] = lax.dot_general(
            hidden_ref[:, :cut], one_ref[:, columns:], contract, preferred_element_type=F32
        ) + lax.dot_general(hidden_ref[:, cut:], two_ref[...], contract, preferred_element_type=F32)


def shrink_rows(where, slot, hidden_states, pieces, tree_size, columns, cut, after):
    rank_size = pieces[0][0].shape[0]
    in_specs, operands = [], []
    for b, (one, two) in enumerate(pieces):
        in_specs += [
            pl.BlockSpec(
                (tree_size, hidden_states.shape[1]),
                lambda i, *refs, b=b: (request_at(refs, slot + b), 0),
            ),
            pl.BlockSpec(one.shape, lambda i, *refs: (0, 0)),
            pl.BlockSpec(two.shape, lambda i, *refs: (0, 0)),
        ]
        operands += [hidden_states, one, two]
    count = len(pieces)
    return pl.pallas_call(
        functools.partial(shrink_kernel, columns=columns, cut=cut),
        grid_spec=pltpu.PrefetchScalarGridSpec(
            num_scalar_prefetch=3,
            grid=(1,),
            in_specs=in_specs + [pl.BlockSpec(memory_space=pl.ANY)] * len(after),
            out_specs=pl.BlockSpec((count, tree_size, rank_size), lambda i, *refs: (0, 0, 0)),
        ),
        out_shape=jax.ShapeDtypeStruct((count, tree_size, rank_size), F32),
        compiler_params=pltpu.CompilerParams(vmem_limit_bytes=24 * 1024 * 1024),
        cost_estimate=pl.CostEstimate(
            flops=count * 300_000_000, bytes_accessed=count * 2_000_000, transcendentals=0
        ),
        name="shrink",
    )(*where, *operands, *after)


def finish_kernel(
    me_ref,
    owner_ref,
    adapter_ref,
    here_ref,
    there_ref,
    table_ref,
    bias_ref,
    query_ref,
    gain_ref,
    *rest,
    group,
    parts,
    split,
    kv_heads,
):
    cached_refs = rest[: 2 * split]
    shrunk_refs = rest[2 * split : 2 * split + 2 * parts]
    expand_refs = rest[2 * split + 2 * parts : -4]
    attention_ref, cache_ref, expand_ref, shrunk_ref = rest[-4:]
    where = (me_ref, owner_ref, adapter_ref)
    step = pl.program_id(0)
    head_size = query_ref.shape[2]
    tree_size = query_ref.shape[0] // group
    per_group = query_ref.shape[1] // kv_heads
    cache_rows = 2 * kv_heads * tree_size
    pairs = tree_size * per_group
    score_scale = math.log2(math.e) / math.sqrt(head_size)

    @pl.when(step == 0)
    def _():
        for slot, ref in enumerate(expand_refs):
            expand_ref[slot] = ref[...]
        slot = 0
        for k in range(parts):
            count = shrunk_refs[2 * k].shape[0]
            shrunk_ref[slot : slot + count] = shrunk_refs[2 * k][...] + shrunk_refs[2 * k + 1][...]
            slot += count

    gain = gain_ref[...]
    sort_new = sorting_matrix(cache_rows, cache_rows, cache_rows // tree_size, tree_size)
    for b in range(group):
        slot = slot_of(where, step * group + b)
        shrunk = shrunk_ref[slot]
        high = shrunk.astype(BF16)
        left = shrunk - high.astype(F32)
        middle = left.astype(BF16)
        low = (left - middle.astype(F32)).astype(BF16)
        terms = jnp.dot(
            jnp.concatenate([low, middle, high], 0), expand_ref[slot], preferred_element_type=F32
        )
        delta = terms[:tree_size] + terms[tree_size : 2 * tree_size] + terms[2 * tree_size :]
        rows = slice(tree_size * b, tree_size * (b + 1))
        projected = (here_ref[rows, :] + there_ref[rows, :]) + delta
        cosine = table_ref[rows, :head_size]
        sine = table_ref[rows, head_size:]
        keys, values, outputs = [], [], []
        for g in range(kv_heads):
            at = 2 * head_size * g
            key = projected[:, at : at + head_size]
            values.append(projected[:, at + head_size : at + 2 * head_size].astype(BF16))
            norm = lax.rsqrt(jnp.mean(key * key, -1, keepdims=True) + 1e-06)
            key = key * norm * gain
            keys.append((key * cosine + pltpu.roll(key, head_size // 2, 1) * sine).astype(BF16))
        queries = query_ref[rows, :, :].astype(F32)
        for g in range(kv_heads):
            query = queries[:, per_group * g : per_group * (g + 1), :].reshape(pairs, head_size)
            scores = lax.dot_general(
                keys[g], query.astype(BF16), (((1,), (1,)), ((), ())), preferred_element_type=F32
            )
            scores = scores + bias_ref[rows, :]
            top_cached = pick_half(cached_refs[1::2], step, group, b, 8, 2 * g, 1)
            sum_cached = pick_half(cached_refs[1::2], step, group, b, 8, 2 * g + 1, 1)
            top = jnp.maximum(jnp.max(scores, 0, keepdims=True), top_cached)
            exponent = jnp.exp2((scores - top) * score_scale)
            shift = jnp.exp2((top_cached - top) * score_scale)
            inverse = 1.0 / (jnp.sum(exponent, 0, keepdims=True) + shift * sum_cached)
            weights = (exponent * inverse).astype(BF16)
            output = lax.dot_general(
                weights, values[g], (((0,), (0,)), ((), ())), preferred_element_type=F32
            )
            factor = jnp.broadcast_to(shift * inverse, (8, pairs)).T[:, :1]
            old = pick_half(cached_refs[0::2], step, group, b, kv_heads * pairs, pairs * g, pairs)
            outputs.append((output + old * factor).reshape(tree_size, per_group, head_size))
        attention_ref[rows, :, :] = jnp.concatenate(outputs, 1).astype(BF16)
        cache_ref[cache_rows * b : cache_rows * (b + 1), :] = jnp.dot(
            sort_new, jnp.concatenate(keys + values, 0), preferred_element_type=F32
        ).astype(BF16)


def pick_half(refs, step, group, b, stride, start, size):
    at = stride * b + start
    rows = refs[0][at : at + size, :]
    if len(refs) == 2:
        rows = jnp.where(2 * step >= pl.num_programs(0), refs[1][at : at + size, :], rows)
    return rows


def finish(where, shared, cached, shrunk, pieces):
    gain, here, there, table, bias, queries = shared
    rows, heads, head_size = queries.shape
    requests = where[2].shape[0]
    tree_size = rows // requests
    columns = here.shape[1]
    kv_heads = columns // (2 * head_size)
    rank_size = pieces[0].shape[0]
    group = 2
    steps = requests // group
    split = len(cached)
    part = steps // split
    row_block = lambda width: pl.BlockSpec((group * tree_size, width), lambda i, *refs: (i, 0))
    whole = lambda shape: pl.BlockSpec(shape, lambda i, *refs: (0,) * len(shape))
    query_block = pl.BlockSpec((group * tree_size, heads, head_size), lambda i, *refs: (i, 0, 0))
    in_specs = [
        row_block(columns),
        row_block(columns),
        row_block(table.shape[1]),
        row_block(bias.shape[1]),
        query_block,
        whole(gain.shape),
    ]
    operands = [*where, here, there, table, bias, queries, gain]
    for k, pair in enumerate(cached):
        for array in pair:
            block = (group * (array.shape[0] * split // requests), array.shape[1])
            in_specs.append(
                pl.BlockSpec(
                    block, lambda i, *refs, k=k: (jnp.clip(i - k * part, 0, part - 1), 0)
                )
            )
            operands.append(array)
    for pair in shrunk:
        for array in pair:
            in_specs.append(whole(array.shape))
            operands.append(array)
    in_specs += [whole((rank_size, columns))] * len(pieces)
    operands += pieces
    cache_rows = 2 * kv_heads * tree_size
    return pl.pallas_call(
        functools.partial(
            finish_kernel, group=group, parts=len(shrunk), split=split, kv_heads=kv_heads
        ),
        grid_spec=pltpu.PrefetchScalarGridSpec(
            num_scalar_prefetch=3,
            grid=(steps,),
            in_specs=in_specs,
            out_specs=[
                query_block,
                pl.BlockSpec((group * cache_rows, head_size), lambda i, *refs: (i, 0)),
            ],
            scratch_shapes=[
                pltpu.VMEM((len(pieces), rank_size, columns), BF16),
                pltpu.VMEM((len(pieces), tree_size, rank_size), F32),
            ],
        ),
        out_shape=[
            jax.ShapeDtypeStruct((rows, heads, head_size), BF16),
            jax.ShapeDtypeStruct((rows * 2 * kv_heads, head_size), BF16),
        ],
        compiler_params=pltpu.CompilerParams(vmem_limit_bytes=32 * 1024 * 1024),
        cost_estimate=pl.CostEstimate(
            flops=4_000_000_000, bytes_accessed=12_000_000, transcendentals=0
        ),
        name="finish",
    )(*operands)


def per_device(
    hidden_states,
    kv_weight,
    shrink_factors,
    expand_factors,
    adapter_ids,
    cache_lengths,
    tree_parents,
    queries,
    cache_keys,
    cache_values,
    key_gain,
):
    requests, tree_size = tree_parents.shape
    row_count, half_width = hidden_states.shape
    kv_heads, kv_width = (kv_weight.shape[1], kv_weight.shape[2])
    head_size = kv_width // 2
    rank_size = shrink_factors.shape[2]
    context = cache_keys.shape[1]
    pool_count = lax.axis_size("pool")
    heads_here = kv_heads // lax.axis_size("tp")
    columns = heads_here * kv_width
    me = lax.axis_index("pool")
    core = lax.axis_index("tp").astype(jnp.int32).reshape(1)
    swap = [(0, 1), (1, 0)]

    def tile_rows(array):
        lead, heads = array.shape[0], array.shape[1]
        return array.reshape(lead, heads, 2, 128).transpose(0, 2, 1, 3).reshape(-1, 128)

    cut = (half_width + columns) // 2 - columns
    first, second = pack(
        core, shrink_factors[0].T, tile_rows(expand_factors[0]), cut, heads_here
    )

    order = ring_order(pool_count)
    onward = [(order[i], order[(i + 1) % pool_count]) for i in range(pool_count)]
    backward = [(b, a) for a, b in onward]
    half = pool_count // 2
    offsets = [[0]] + [[-step, step] for step in range(1, half)] + [[half]]
    flat_offsets = sum(offsets, [])
    owners = np.zeros((pool_count, pool_count), np.int32)
    for spot, index in enumerate(order):
        owners[index] = [order[(spot + offset) % pool_count] for offset in flat_offsets]
    where = (me.astype(jnp.int32).reshape(1), jnp.asarray(owners), adapter_ids)

    weight_rows = tile_rows(kv_weight)
    key_rows = cache_keys.reshape(-1, head_size)
    value_rows = cache_values.reshape(-1, head_size)
    halves = requests // 2

    arrivals = [(first, second)]
    front = rear = (first, second)
    cached = [None, None]
    table, bias = tree_tables(
        cache_lengths, tree_parents, head_size, queries.shape[1] // heads_here, [first]
    )
    for step in range(1, half):
        front = tuple(lax.ppermute(piece, "pool", onward) for piece in front)
        rear = tuple(lax.ppermute(piece, "pool", backward) for piece in rear)
        held = [front[1], rear[1]]
        if step == 1:
            here, away, *held = base_product(
                core, hidden_states, weight_rows, kv_heads * kv_width, held
            )
        if step == 2:
            *cached[0], front_piece, rear_piece = cache_attention(
                cache_lengths, queries, key_rows, value_rows, heads_here, 0, halves, held, []
            )
            held = [front_piece, rear_piece]
        front, rear = (front[0], held[0]), (rear[0], held[1])
        arrivals += [front, rear]
    arrivals.append(
        (lax.ppermute(front[0], "pool", onward), lax.ppermute(rear[1], "pool", backward))
    )
    there = lax.ppermute(away, "tp", swap)
    cached[1] = cache_attention(
        cache_lengths,
        queries,
        key_rows,
        value_rows,
        heads_here,
        halves,
        requests - halves,
        [],
        [arrivals[5][0]],
    )

    shrunk = []
    slot = 0
    for group in (arrivals[:-3], arrivals[-3:]):
        partial = shrink_rows(where, slot, hidden_states, group, tree_size, columns, cut, [])
        shrunk.append((partial, lax.ppermute(partial, "tp", swap)))
        slot += len(group)
    shared = (key_gain.reshape(1, head_size), here, there, table, bias, queries)
    attention, cache_rows = finish(where, shared, cached, shrunk, [piece[0] for piece in arrivals])
    tree_cache = (
        cache_rows.reshape(row_count, 2, heads_here, head_size)
        .transpose(0, 2, 1, 3)
        .reshape(row_count, heads_here, kv_width)
    )
    return attention, tree_cache


def solution(mesh):
    placed = (
        P(("grp", "pool"), "tp"),
        P("tp", None, None),
        P(("grp", "pool"), "tp", None),
        P(("grp", "pool"), None, None, None),
        P(("grp", "pool")),
        P(("grp", "pool")),
        P(("grp", "pool"), None),
        P(("grp", "pool"), "tp", None),
        P(("grp", "pool"), None, "tp", None),
        P(("grp", "pool"), None, "tp", None),
        P(),
    )
    return jax.shard_map(
        per_device,
        mesh=mesh,
        in_specs=placed,
        out_specs=(P(("grp", "pool"), "tp", None), P(("grp", "pool"), "tp", None)),
        check_vma=False,
    )
```

```python
import functools
import math

import jax
import jax.numpy as jnp
import numpy as np
from jax import lax
from jax.experimental import pallas as pl
from jax.experimental.pallas import tpu as pltpu
from jax.sharding import PartitionSpec as P

F32 = jnp.float32
BF16 = jnp.bfloat16


ANYWHERE = pl.BlockSpec(memory_space=pl.ANY)


def shapes_of(arrays):
    return [jax.ShapeDtypeStruct(array.shape, array.dtype) for array in arrays]


def ring_order(count):
    if count == 8:
        return list(range(0, count, 2)) + list(range(count - 1, 0, -2))
    return list(range(count))


def sorting_matrix(rows, columns, inner, source_inner):
    row = lax.broadcasted_iota(jnp.int32, (rows, columns), 0)
    column = lax.broadcasted_iota(jnp.int32, (rows, columns), 1)
    return (column == (row % inner) * source_inner + row // inner).astype(F32).astype(BF16)


def picking_matrix(wanted, inner, groups, first_head):
    row = lax.broadcasted_iota(jnp.int32, (wanted * inner, 256), 0)
    column = lax.broadcasted_iota(jnp.int32, (wanted * inner, 256), 1)
    group = row // inner
    source = (group % 2) * (groups // 2) + first_head + group // 2
    return (column == (row % inner) * groups + source).astype(F32).astype(BF16)


def request_at(where, slot):
    me_ref, owner_ref, adapter_ref = where
    owner = owner_ref[me_ref[0], slot]
    request = jnp.int32(0)
    for r in range(1, adapter_ref.shape[0]):
        request = jnp.where(adapter_ref[r] == owner, jnp.int32(r), request)
    return request


def pack_kernel(core_ref, shrink_ref, expand_ref, first_ref, second_ref, *, cut, heads_here):
    rank_size = shrink_ref.shape[0]
    groups = expand_ref.shape[0] // rank_size
    ranks = 256 // groups
    pick = picking_matrix(2 * heads_here, ranks, groups, core_ref[0] * heads_here)
    columns = 2 * heads_here * 128
    for block in range(rank_size // ranks):
        sorted_rows = jnp.dot(
            pick, expand_ref[256 * block : 256 * (block + 1), :], preferred_element_type=F32
        ).astype(BF16)
        for g in range(2 * heads_here):
            first_ref[ranks * block : ranks * (block + 1), 128 * g : 128 * (g + 1)] = sorted_rows[
                ranks * g : ranks * (g + 1), :
            ]
    first_ref[:, columns:] = shrink_ref[:, :cut]
    second_ref[...] = shrink_ref[:, cut:]


def pack(core, shrink, expand_rows, cut, heads_here):
    rank_size, half_width = shrink.shape
    columns = 2 * heads_here * 128
    return pl.pallas_call(
        functools.partial(pack_kernel, cut=cut, heads_here=heads_here),
        grid_spec=pltpu.PrefetchScalarGridSpec(
            num_scalar_prefetch=1,
            grid=(1,),
            in_specs=[
                pl.BlockSpec(shrink.shape, lambda i, c: (0, 0)),
                pl.BlockSpec(expand_rows.shape, lambda i, c: (0, 0)),
            ],
            out_specs=[
                pl.BlockSpec((rank_size, columns + cut), lambda i, c: (0, 0)),
                pl.BlockSpec((rank_size, half_width - cut), lambda i, c: (0, 0)),
            ],
        ),
        out_shape=[
            jax.ShapeDtypeStruct((rank_size, columns + cut), BF16),
            jax.ShapeDtypeStruct((rank_size, half_width - cut), BF16),
        ],
        name="pack",
    )(core, shrink, expand_rows)


def base_kernel(core_ref, hidden_ref, weight_ref, *rest, held_count):
    total_ref, wide_ref = rest[-2:]
    here_ref, away_ref = rest[-2 - held_count - 2 : -2 - held_count]
    step = pl.program_id(0)
    depth = hidden_ref.shape[1]
    groups = weight_ref.shape[0] // depth
    heads = groups // 2
    wide_ref[...] = weight_ref[...].astype(F32)
    parts = []
    for head in range(heads):
        tiles = [
            wide_ref[pl.ds(tile * heads + head, depth, stride=groups), :].astype(BF16)
            for tile in range(2)
        ]
        parts.append(
            jnp.dot(hidden_ref[...], jnp.concatenate(tiles, 1), preferred_element_type=F32)
        )
    product = jnp.concatenate(parts, 1)

    @pl.when(step == 0)
    def _():
        total_ref[...] = product

    @pl.when(step > 0)
    def _():
        total_ref[...] += product

    @pl.when(step == pl.num_programs(0) - 1)
    def _():
        columns = here_ref.shape[1]

        @pl.when(core_ref[0] == 0)
        def _():
            here_ref[...] = total_ref[:, :columns]
            away_ref[...] = total_ref[:, columns:]

        @pl.when(core_ref[0] == 1)
        def _():
            here_ref[...] = total_ref[:, columns:]
            away_ref[...] = total_ref[:, :columns]


def base_product(core, hidden_states, weight_rows, width, held):
    rows, half_width = hidden_states.shape
    groups = weight_rows.shape[0] // half_width
    depth = half_width // 2
    return pl.pallas_call(
        functools.partial(base_kernel, held_count=len(held)),
        grid_spec=pltpu.PrefetchScalarGridSpec(
            num_scalar_prefetch=1,
            grid=(half_width // depth,),
            in_specs=[
                pl.BlockSpec((rows, depth), lambda i, c: (0, i)),
                pl.BlockSpec((depth * groups, 128), lambda i, c: (i, 0)),
            ]
            + [ANYWHERE] * len(held),
            out_specs=[pl.BlockSpec((rows, width // 2), lambda i, c: (0, 0))] * 2
            + [ANYWHERE] * len(held),
            scratch_shapes=[
                pltpu.VMEM((rows, width), F32),
                pltpu.VMEM((depth * groups, 128), F32),
            ],
        ),
        out_shape=[jax.ShapeDtypeStruct((rows, width // 2), F32)] * 2 + shapes_of(held),
        input_output_aliases={3 + k: 2 + k for k in range(len(held))},
        compiler_params=pltpu.CompilerParams(vmem_limit_bytes=56 * 1024 * 1024),
        cost_estimate=pl.CostEstimate(
            flops=4_000_000_000, bytes_accessed=9_000_000, transcendentals=0
        ),
        name="base",
    )(core, hidden_states, weight_rows, *held)


def tree_kernel(length_ref, parent_ref, frequency_ref, *rest, kv_heads, held_count):
    table_ref = rest[len(rest) - held_count - 1]
    requests, nodes = parent_ref.shape
    head_size = frequency_ref.shape[1]
    node = lax.broadcasted_iota(jnp.int32, (nodes, nodes), 0)
    same = node == lax.broadcasted_iota(jnp.int32, (nodes, nodes), 1)
    spare = table_ref.shape[1] - 2 * head_size
    spread_node = lax.broadcasted_iota(jnp.int32, (nodes, spare), 0)
    spread_lane = lax.broadcasted_iota(jnp.int32, (nodes, spare), 1)
    spread = spread_lane == spread_node
    for g in range(1, kv_heads):
        spread = spread | (spread_lane == spread_node + nodes * g)
    spread = spread.astype(F32).astype(BF16)
    parents = parent_ref[...]
    below = [
        (same | (parents[r : r + 1, :] == node)).astype(F32).astype(BF16) for r in range(requests)
    ]
    reached = 1
    while reached < nodes:
        below = [
            jnp.minimum(jnp.dot(b, b, preferred_element_type=F32), 1.0).astype(BF16) for b in below
        ]
        reached = 2 * reached
    lane = lax.broadcasted_iota(jnp.int32, (nodes, head_size), 1)
    sign = jnp.where(lane < head_size // 2, -1.0, 1.0)
    ones = jnp.ones((nodes, head_size), BF16)
    for r in range(requests):
        b = below[r]
        depth = lax.dot_general(b, ones, (((0,), (0,)), ((), ())), preferred_element_type=F32)
        positions = length_ref[r].astype(F32) + depth - 1.0
        angles = positions * frequency_ref[...]
        rows = slice(nodes * r, nodes * (r + 1))
        wide = lax.dot_general(b, spread, (((0,), (0,)), ((), ())), preferred_element_type=F32)
        table_ref[rows, :] = jnp.concatenate(
            [jnp.cos(angles), jnp.sin(angles) * sign, jnp.where(wide > 0.5, 0.0, -1e30)], 1
        )


def tree_tables(cache_lengths, tree_parents, head_size, kv_heads, held):
    requests, nodes = tree_parents.shape
    half_size = head_size // 2
    frequency = np.exp(np.arange(half_size) * (-2.0 * math.log(1000000.0) / head_size))
    frequency = np.concatenate([frequency, frequency]).reshape(1, head_size).astype(np.float32)
    whole = lambda shape: pl.BlockSpec(shape, lambda i, n: (0,) * len(shape))
    rows = requests * nodes
    width = 2 * head_size + -(-kv_heads * nodes // 128) * 128
    return pl.pallas_call(
        functools.partial(tree_kernel, kv_heads=kv_heads, held_count=len(held)),
        grid_spec=pltpu.PrefetchScalarGridSpec(
            num_scalar_prefetch=1,
            grid=(1,),
            in_specs=[whole(tree_parents.shape), whole((1, head_size))] + [ANYWHERE] * len(held),
            out_specs=[whole((rows, width))] + [ANYWHERE] * len(held),
        ),
        out_shape=[jax.ShapeDtypeStruct((rows, width), F32)] + shapes_of(held),
        input_output_aliases={3 + k: 1 + k for k in range(len(held))},
        cost_estimate=pl.CostEstimate(
            flops=1_000_000_000, bytes_accessed=8_000_000, transcendentals=0
        ),
        name="tree",
    )(cache_lengths, tree_parents, frequency, *held)


def shrink_kernel(me_ref, owner_ref, adapter_ref, *refs, columns, cut, held_count):
    output_ref = refs[len(refs) - held_count - 1]
    contract = (((1,), (1,)), ((), ()))
    for b in range(output_ref.shape[0]):
        hidden_ref, one_ref, two_ref = refs[3 * b : 3 * b + 3]
        output_ref[b] = lax.dot_general(
            hidden_ref[:, :cut], one_ref[:, columns:], contract, preferred_element_type=F32
        ) + lax.dot_general(hidden_ref[:, cut:], two_ref[...], contract, preferred_element_type=F32)


def shrink_rows(where, slot, hidden_states, pieces, tree_size, columns, cut, after, held):
    rank_size = pieces[0][0].shape[0]
    in_specs, operands = [], []
    for b, (one, two) in enumerate(pieces):
        in_specs += [
            pl.BlockSpec(
                (tree_size, hidden_states.shape[1]),
                lambda i, *refs, b=b: (request_at(refs, slot + b), 0),
            ),
            pl.BlockSpec(one.shape, lambda i, *refs: (0, 0)),
            pl.BlockSpec(two.shape, lambda i, *refs: (0, 0)),
        ]
        operands += [hidden_states, one, two]
    count = len(pieces)
    return pl.pallas_call(
        functools.partial(shrink_kernel, columns=columns, cut=cut, held_count=len(held)),
        grid_spec=pltpu.PrefetchScalarGridSpec(
            num_scalar_prefetch=3,
            grid=(1,),
            in_specs=in_specs + [ANYWHERE] * (len(after) + len(held)),
            out_specs=[pl.BlockSpec((count, tree_size, rank_size), lambda i, *refs: (0, 0, 0))]
            + [ANYWHERE] * len(held),
        ),
        out_shape=[jax.ShapeDtypeStruct((count, tree_size, rank_size), F32)] + shapes_of(held),
        input_output_aliases={3 + len(operands) + len(after) + k: 1 + k for k in range(len(held))},
        compiler_params=pltpu.CompilerParams(vmem_limit_bytes=24 * 1024 * 1024),
        cost_estimate=pl.CostEstimate(
            flops=count * 300_000_000, bytes_accessed=count * 2_000_000, transcendentals=0
        ),
        name="shrink",
    )(*where, *operands, *after, *held)


def finish_kernel(
    me_ref,
    owner_ref,
    adapter_ref,
    length_ref,
    here_ref,
    there_ref,
    shrunk_here_ref,
    shrunk_there_ref,
    table_ref,
    gain_ref,
    query_ref,
    key_ref,
    value_ref,
    *rest,
    count,
    slot,
    kv_heads,
):
    expand_refs = rest[:count]
    attention_ref, cache_ref, expand_ref = rest[-3:]
    tree_size, heads, head_size = query_ref.shape
    cached = key_ref.shape[0]
    per_group = heads // kv_heads
    rows = tree_size * heads
    columns = kv_heads * 2 * head_size
    spare = table_ref.shape[1] - 2 * head_size
    score_scale = math.log2(math.e) / math.sqrt(head_size)
    if count == 1:
        expand = expand_refs[0][...]
    else:
        for b in range(count):

            @pl.when(pl.program_id(0) == b)
            def _():
                expand_ref[...] = expand_refs[b][...]

        expand = expand_ref[...]
    length = length_ref[request_at((me_ref, owner_ref, adapter_ref), slot + pl.program_id(0))]
    shrunk = shrunk_here_ref[0] + shrunk_there_ref[0]
    high = shrunk.astype(BF16)
    left = shrunk - high.astype(F32)
    middle = left.astype(BF16)
    low = (left - middle.astype(F32)).astype(BF16)
    terms = jnp.dot(jnp.concatenate([low, middle, high], 0), expand, preferred_element_type=F32)
    delta = terms[:tree_size] + terms[tree_size : 2 * tree_size] + terms[2 * tree_size :]
    projected = (here_ref[...] + there_ref[...]) + delta
    cosine = table_ref[:, :head_size]
    sine = table_ref[:, head_size : 2 * head_size]
    gain = gain_ref[...]
    new_keys, new_values = [], []
    for g in range(kv_heads):
        at = 2 * head_size * g
        key = projected[:, at : at + head_size]
        new_values.append(projected[:, at + head_size : at + 2 * head_size].astype(BF16))
        norm = lax.rsqrt(jnp.mean(key * key, -1, keepdims=True) + 1e-06)
        key = key * norm * gain
        new_keys.append((key * cosine + pltpu.roll(key, head_size // 2, 1) * sine).astype(BF16))
    pad = jnp.zeros((spare - kv_heads * tree_size, head_size), BF16)
    keys = jnp.concatenate([key_ref[...]] + new_keys + [pad], 0)
    values = jnp.concatenate([value_ref[...]] + new_values + [pad], 0)
    scores = lax.dot_general(
        query_ref[...].reshape(rows, head_size),
        keys,
        (((1,), (1,)), ((), ())),
        preferred_element_type=F32,
    ).reshape(tree_size, heads, cached + spare)
    lane = lax.broadcasted_iota(jnp.int32, (heads, cached), 1)
    mine = lax.broadcasted_iota(jnp.int32, (heads, cached), 0) // per_group
    allowed = (lane % kv_heads == mine) & (lane // kv_heads < length)
    cached_bias = jnp.where(allowed, 0.0, -1e30)
    lane = lax.broadcasted_iota(jnp.int32, (heads, spare), 1)
    first = lax.broadcasted_iota(jnp.int32, (heads, spare), 0) // per_group * tree_size
    head_bias = jnp.where((lane >= first) & (lane < first + tree_size), 0.0, -1e30)
    node_bias = table_ref[:, 2 * head_size :]
    cached_scores = scores[:, :, :cached] + cached_bias[None]
    tree_scores = scores[:, :, cached:] + (node_bias[:, None, :] + head_bias[None])
    top = jnp.maximum(
        jnp.max(cached_scores, -1, keepdims=True), jnp.max(tree_scores, -1, keepdims=True)
    )
    cached_exponent = jnp.exp2((cached_scores - top) * score_scale)
    tree_exponent = jnp.exp2((tree_scores - top) * score_scale)
    total = jnp.sum(cached_exponent, -1, keepdims=True) + jnp.sum(tree_exponent, -1, keepdims=True)
    exponent = jnp.concatenate([cached_exponent, tree_exponent], -1)
    output = jnp.dot(
        exponent.astype(BF16).reshape(rows, cached + spare), values, preferred_element_type=F32
    ).reshape(tree_size, heads, head_size)
    attention_ref[...] = (output * (1.0 / total)).astype(BF16)
    stacked = jnp.concatenate(new_keys + new_values, 0)
    size = stacked.shape[0]
    cache_ref[...] = jnp.dot(
        sorting_matrix(size, size, size // tree_size, tree_size),
        stacked,
        preferred_element_type=F32,
    ).astype(BF16)


def finish(where, slot, batch, there, shared, previous):
    shrunk_here, shrunk_there, pieces = batch
    lengths, gain, here, table, queries, key_rows, value_rows = shared
    spot = lambda i, refs: request_at(refs[:3], slot + i)
    count, tree_size, rank_size = shrunk_here.shape
    requests = lengths.shape[0]
    rows, heads, head_size = queries.shape
    columns = here.shape[1]
    kv_heads = columns // (2 * head_size)
    row_block = lambda width: pl.BlockSpec((tree_size, width), lambda i, *refs: (spot(i, refs), 0))
    shrunk_block = pl.BlockSpec((1, tree_size, rank_size), lambda i, *refs: (i, 0, 0))
    cached_block = pl.BlockSpec(
        (key_rows.shape[0] // requests, head_size), lambda i, *refs: (spot(i, refs), 0)
    )
    query_block = pl.BlockSpec(
        (tree_size, heads, head_size), lambda i, *refs: (spot(i, refs), 0, 0)
    )
    in_specs = [
        row_block(columns),
        row_block(columns),
        shrunk_block,
        shrunk_block,
        row_block(table.shape[1]),
        pl.BlockSpec((1, head_size), lambda i, *refs: (0, 0)),
        query_block,
        cached_block,
        cached_block,
    ] + [pl.BlockSpec((rank_size, columns), lambda i, *refs: (0, 0))] * count
    operands = [*where, lengths, here, there, shrunk_here, shrunk_there, table, gain, queries]
    operands += [key_rows, value_rows, *pieces]
    aliases = {}
    if previous is not None:
        aliases = {len(operands): 0, len(operands) + 1: 1}
        operands += list(previous)
        in_specs += [ANYWHERE] * 2
    cache_rows = 2 * kv_heads * tree_size
    return pl.pallas_call(
        functools.partial(finish_kernel, count=count, slot=slot, kv_heads=kv_heads),
        grid_spec=pltpu.PrefetchScalarGridSpec(
            num_scalar_prefetch=4,
            grid=(count,),
            in_specs=in_specs,
            out_specs=[
                query_block,
                pl.BlockSpec((cache_rows, head_size), lambda i, *refs: (spot(i, refs), 0)),
            ],
            scratch_shapes=[pltpu.VMEM((rank_size, columns), BF16)],
        ),
        out_shape=[
            jax.ShapeDtypeStruct((rows, heads, head_size), BF16),
            jax.ShapeDtypeStruct((rows * 2 * kv_heads, head_size), BF16),
        ],
        input_output_aliases=aliases,
        compiler_params=pltpu.CompilerParams(vmem_limit_bytes=24 * 1024 * 1024),
        cost_estimate=pl.CostEstimate(
            flops=count * 900_000_000, bytes_accessed=count * 3_000_000, transcendentals=0
        ),
        name="finish",
    )(*operands)


def per_device(
    hidden_states,
    kv_weight,
    shrink_factors,
    expand_factors,
    adapter_ids,
    cache_lengths,
    tree_parents,
    queries,
    cache_keys,
    cache_values,
    key_gain,
):
    requests, tree_size = tree_parents.shape
    row_count, half_width = hidden_states.shape
    kv_heads, kv_width = (kv_weight.shape[1], kv_weight.shape[2])
    head_size = kv_width // 2
    rank_size = shrink_factors.shape[2]
    context = cache_keys.shape[1]
    pool_count = lax.axis_size("pool")
    heads_here = kv_heads // lax.axis_size("tp")
    columns = heads_here * kv_width
    me = lax.axis_index("pool")
    core = lax.axis_index("tp").astype(jnp.int32).reshape(1)
    swap = [(0, 1), (1, 0)]

    def tile_rows(array):
        lead, heads = array.shape[0], array.shape[1]
        return array.reshape(lead, heads, 2, 128).transpose(0, 2, 1, 3).reshape(-1, 128)

    cut = (half_width + columns) // 2 - columns
    first, second = pack(
        core, shrink_factors[0].T, tile_rows(expand_factors[0]), cut, heads_here
    )

    order = ring_order(pool_count)
    onward = [(order[i], order[(i + 1) % pool_count]) for i in range(pool_count)]
    backward = [(b, a) for a, b in onward]
    half = pool_count // 2
    offsets = [[0]] + [[-step, step] for step in range(1, half)] + [[half]]
    flat_offsets = sum(offsets, [])
    owners = np.zeros((pool_count, pool_count), np.int32)
    for spot, index in enumerate(order):
        owners[index] = [order[(spot + offset) % pool_count] for offset in flat_offsets]
    where = (me.astype(jnp.int32).reshape(1), jnp.asarray(owners), adapter_ids)

    weight_rows = tile_rows(kv_weight)
    key_rows = cache_keys.reshape(-1, head_size)
    value_rows = cache_values.reshape(-1, head_size)

    arrivals = [(first, second)]
    front = rear = (first, second)
    for step in range(1, half):
        front = tuple(lax.ppermute(piece, "pool", onward) for piece in front)
        rear = tuple(lax.ppermute(piece, "pool", backward) for piece in rear)
        held = [front[1], rear[1]]
        if step == 1:
            here, away, *held = base_product(
                core, hidden_states, weight_rows, kv_heads * kv_width, held
            )
        if step == 2:
            table, *held = tree_tables(cache_lengths, tree_parents, head_size, heads_here, held)
        front, rear = (front[0], held[0]), (rear[0], held[1])
        arrivals += [front, rear]
    arrivals.append(
        (lax.ppermute(front[0], "pool", onward), lax.ppermute(rear[1], "pool", backward))
    )
    shared = (
        cache_lengths,
        key_gain.reshape(1, head_size),
        here,
        table,
        queries,
        key_rows,
        value_rows,
    )
    outputs = None
    if pool_count == requests:
        slot = 0
        for group in (arrivals[:-3], arrivals[-3:]):
            after = [] if outputs is None else [outputs[0]]
            held = [away] if outputs is None else []
            partial, *held = shrink_rows(
                where, slot, hidden_states, group, tree_size, columns, cut, after, held
            )
            if held:
                there = lax.ppermute(held[0], "tp", swap)
            batch = (partial, lax.ppermute(partial, "tp", swap), [piece[0] for piece in group])
            outputs = finish(where, slot, batch, there, shared, outputs)
            slot += len(group)
    else:
        parts = [
            shrink_rows(where, slot, hidden_states, [piece], tree_size, columns, cut, [], [])[0]
            for slot, piece in enumerate(arrivals)
        ]
        owners_here = lax.dynamic_index_in_dim(jnp.asarray(owners), me, 0, keepdims=False)
        hot = (adapter_ids[None, :] == owners_here[:, None]).astype(jnp.int32)
        slots = jnp.sum(hot * jnp.arange(pool_count, dtype=jnp.int32)[:, None], 0)
        partial = jnp.concatenate(parts, 0)[slots]
        expands = jnp.stack([piece[0][:, :columns] for piece in arrivals])[slots]
        every = jnp.arange(requests, dtype=jnp.int32)
        batch = (
            partial,
            lax.ppermute(partial, "tp", swap),
            [expands[r] for r in range(requests)],
        )
        there = lax.ppermute(away, "tp", swap)
        outputs = finish((every[:1], every[None, :], every), 0, batch, there, shared, None)
    attention, cache_rows = outputs
    tree_cache = (
        cache_rows.reshape(row_count, 2, heads_here, head_size)
        .transpose(0, 2, 1, 3)
        .reshape(row_count, heads_here, kv_width)
    )
    return attention, tree_cache


def solution(mesh):
    placed = (
        P(("grp", "pool"), "tp"),
        P("tp", None, None),
        P(("grp", "pool"), "tp", None),
        P(("grp", "pool"), None, None, None),
        P(("grp", "pool")),
        P(("grp", "pool")),
        P(("grp", "pool"), None),
        P(("grp", "pool"), "tp", None),
        P(("grp", "pool"), None, "tp", None),
        P(("grp", "pool"), None, "tp", None),
        P(),
    )
    return jax.shard_map(
        per_device,
        mesh=mesh,
        in_specs=placed,
        out_specs=(P(("grp", "pool"), "tp", None), P(("grp", "pool"), "tp", None)),
        check_vma=False,
    )
```

```python
import functools
import math

import jax
import jax.numpy as jnp
import numpy as np
from jax import lax
from jax.experimental import pallas as pl
from jax.experimental.pallas import tpu as pltpu
from jax.sharding import PartitionSpec as P

F32 = jnp.float32
BF16 = jnp.bfloat16


ANYWHERE = pl.BlockSpec(memory_space=pl.ANY)


def shapes_of(arrays):
    return [jax.ShapeDtypeStruct(array.shape, array.dtype) for array in arrays]


def ring_order(count):
    if count == 8:
        return list(range(0, count, 2)) + list(range(count - 1, 0, -2))
    return list(range(count))


def sorting_matrix(rows, columns, inner, source_inner):
    row = lax.broadcasted_iota(jnp.int32, (rows, columns), 0)
    column = lax.broadcasted_iota(jnp.int32, (rows, columns), 1)
    return (column == (row % inner) * source_inner + row // inner).astype(F32).astype(BF16)


def picking_matrix(wanted, inner, groups, first_head):
    row = lax.broadcasted_iota(jnp.int32, (wanted * inner, 256), 0)
    column = lax.broadcasted_iota(jnp.int32, (wanted * inner, 256), 1)
    group = row // inner
    source = (group % 2) * (groups // 2) + first_head + group // 2
    return (column == (row % inner) * groups + source).astype(F32).astype(BF16)


def request_at(where, slot):
    me_ref, owner_ref, adapter_ref = where
    owner = owner_ref[me_ref[0], slot]
    request = jnp.int32(0)
    for r in range(1, adapter_ref.shape[0]):
        request = jnp.where(adapter_ref[r] == owner, jnp.int32(r), request)
    return request


def pack_kernel(core_ref, shrink_ref, expand_ref, first_ref, second_ref, *, cut, heads_here):
    rank_size = shrink_ref.shape[0]
    groups = expand_ref.shape[0] // rank_size
    ranks = 256 // groups
    pick = picking_matrix(2 * heads_here, ranks, groups, core_ref[0] * heads_here)
    columns = 2 * heads_here * 128
    for block in range(rank_size // ranks):
        sorted_rows = jnp.dot(
            pick, expand_ref[256 * block : 256 * (block + 1), :], preferred_element_type=F32
        ).astype(BF16)
        for g in range(2 * heads_here):
            first_ref[ranks * block : ranks * (block + 1), 128 * g : 128 * (g + 1)] = sorted_rows[
                ranks * g : ranks * (g + 1), :
            ]
    first_ref[:, columns:] = shrink_ref[:, :cut]
    second_ref[...] = shrink_ref[:, cut:]


def pack(core, shrink, expand_rows, cut, heads_here):
    rank_size, half_width = shrink.shape
    columns = 2 * heads_here * 128
    return pl.pallas_call(
        functools.partial(pack_kernel, cut=cut, heads_here=heads_here),
        grid_spec=pltpu.PrefetchScalarGridSpec(
            num_scalar_prefetch=1,
            grid=(1,),
            in_specs=[
                pl.BlockSpec(shrink.shape, lambda i, c: (0, 0)),
                pl.BlockSpec(expand_rows.shape, lambda i, c: (0, 0)),
            ],
            out_specs=[
                pl.BlockSpec((rank_size, columns + cut), lambda i, c: (0, 0)),
                pl.BlockSpec((rank_size, half_width - cut), lambda i, c: (0, 0)),
            ],
        ),
        out_shape=[
            jax.ShapeDtypeStruct((rank_size, columns + cut), BF16),
            jax.ShapeDtypeStruct((rank_size, half_width - cut), BF16),
        ],
        compiler_params=pltpu.CompilerParams(vmem_limit_bytes=8 * 1024 * 1024),
        name="pack",
    )(core, shrink, expand_rows)


def base_kernel(core_ref, hidden_ref, weight_ref, *rest, held_count):
    total_ref, wide_ref = rest[-2:]
    here_ref, away_ref = rest[-2 - held_count - 2 : -2 - held_count]
    step = pl.program_id(0)
    depth = hidden_ref.shape[1]
    groups = weight_ref.shape[0] // depth
    heads = groups // 2
    wide_ref[...] = weight_ref[...].astype(F32)
    parts = []
    for head in range(heads):
        tiles = [
            wide_ref[pl.ds(tile * heads + head, depth, stride=groups), :].astype(BF16)
            for tile in range(2)
        ]
        parts.append(
            jnp.dot(hidden_ref[...], jnp.concatenate(tiles, 1), preferred_element_type=F32)
        )
    product = jnp.concatenate(parts, 1)

    @pl.when(step == 0)
    def _():
        total_ref[...] = product

    @pl.when(step > 0)
    def _():
        total_ref[...] += product

    @pl.when(step == pl.num_programs(0) - 1)
    def _():
        columns = here_ref.shape[1]

        @pl.when(core_ref[0] == 0)
        def _():
            here_ref[...] = total_ref[:, :columns]
            away_ref[...] = total_ref[:, columns:]

        @pl.when(core_ref[0] == 1)
        def _():
            here_ref[...] = total_ref[:, columns:]
            away_ref[...] = total_ref[:, :columns]


def base_product(core, hidden_states, weight_rows, width, after, held):
    rows, half_width = hidden_states.shape
    groups = weight_rows.shape[0] // half_width
    depth = half_width // 2
    return pl.pallas_call(
        functools.partial(base_kernel, held_count=len(held)),
        grid_spec=pltpu.PrefetchScalarGridSpec(
            num_scalar_prefetch=1,
            grid=(half_width // depth,),
            in_specs=[
                pl.BlockSpec((rows, depth), lambda i, c: (0, i)),
                pl.BlockSpec((depth * groups, 128), lambda i, c: (i, 0)),
            ]
            + [ANYWHERE] * (len(after) + len(held)),
            out_specs=[pl.BlockSpec((rows, width // 2), lambda i, c: (0, 0))] * 2
            + [ANYWHERE] * len(held),
            scratch_shapes=[
                pltpu.VMEM((rows, width), F32),
                pltpu.VMEM((depth * groups, 128), F32),
            ],
        ),
        out_shape=[jax.ShapeDtypeStruct((rows, width // 2), F32)] * 2 + shapes_of(held),
        input_output_aliases={3 + len(after) + k: 2 + k for k in range(len(held))},
        cost_estimate=pl.CostEstimate(
            flops=4_000_000_000, bytes_accessed=9_000_000, transcendentals=0
        ),
        compiler_params=pltpu.CompilerParams(vmem_limit_bytes=24 * 1024 * 1024),
        name="base",
    )(core, hidden_states, weight_rows, *after, *held)


def tree_kernel(length_ref, parent_ref, frequency_ref, weight_ref, *rest, kv_heads):
    table_ref, moved_ref, semaphore = rest[-3:]
    move = pltpu.make_async_copy(weight_ref, moved_ref, semaphore)
    move.start()
    requests, nodes = parent_ref.shape
    head_size = frequency_ref.shape[1]
    node = lax.broadcasted_iota(jnp.int32, (nodes, nodes), 0)
    same = node == lax.broadcasted_iota(jnp.int32, (nodes, nodes), 1)
    spare = table_ref.shape[1] - 2 * head_size
    spread_node = lax.broadcasted_iota(jnp.int32, (nodes, spare), 0)
    spread_lane = lax.broadcasted_iota(jnp.int32, (nodes, spare), 1)
    spread = spread_lane == spread_node
    for g in range(1, kv_heads):
        spread = spread | (spread_lane == spread_node + nodes * g)
    spread = spread.astype(F32).astype(BF16)
    parents = parent_ref[...]
    below = [
        (same | (parents[r : r + 1, :] == node)).astype(F32).astype(BF16) for r in range(requests)
    ]
    reached = 1
    while reached < nodes:
        below = [
            jnp.minimum(jnp.dot(b, b, preferred_element_type=F32), 1.0).astype(BF16) for b in below
        ]
        reached = 2 * reached
    lane = lax.broadcasted_iota(jnp.int32, (nodes, head_size), 1)
    sign = jnp.where(lane < head_size // 2, -1.0, 1.0)
    ones = jnp.ones((nodes, head_size), BF16)
    for r in range(requests):
        b = below[r]
        depth = lax.dot_general(b, ones, (((0,), (0,)), ((), ())), preferred_element_type=F32)
        positions = length_ref[r].astype(F32) + depth - 1.0
        angles = positions * frequency_ref[...]
        rows = slice(nodes * r, nodes * (r + 1))
        wide = lax.dot_general(b, spread, (((0,), (0,)), ((), ())), preferred_element_type=F32)
        table_ref[rows, :] = jnp.concatenate(
            [jnp.cos(angles), jnp.sin(angles) * sign, jnp.where(wide > 0.5, 0.0, -1e30)], 1
        )
    move.wait()


def tree_tables(cache_lengths, tree_parents, head_size, kv_heads, weight_rows, after):
    requests, nodes = tree_parents.shape
    half_size = head_size // 2
    frequency = np.exp(np.arange(half_size) * (-2.0 * math.log(1000000.0) / head_size))
    frequency = np.concatenate([frequency, frequency]).reshape(1, head_size).astype(np.float32)
    whole = lambda shape: pl.BlockSpec(shape, lambda i, n: (0,) * len(shape))
    rows = requests * nodes
    width = 2 * head_size + -(-kv_heads * nodes // 128) * 128
    return pl.pallas_call(
        functools.partial(tree_kernel, kv_heads=kv_heads),
        grid_spec=pltpu.PrefetchScalarGridSpec(
            num_scalar_prefetch=1,
            grid=(1,),
            in_specs=[whole(tree_parents.shape), whole((1, head_size)), pl.BlockSpec(memory_space=pltpu.HBM)]
            + [ANYWHERE] * len(after),
            out_specs=[whole((rows, width)), ANYWHERE],
            scratch_shapes=[pltpu.SemaphoreType.DMA],
        ),
        out_shape=[jax.ShapeDtypeStruct((rows, width), F32)] + shapes_of([weight_rows]),
        cost_estimate=pl.CostEstimate(
            flops=1_000_000_000, bytes_accessed=8_000_000, transcendentals=0
        ),
        compiler_params=pltpu.CompilerParams(vmem_limit_bytes=8 * 1024 * 1024),
        name="tree",
    )(cache_lengths, tree_parents, frequency, weight_rows, *after)


def shrink_kernel(me_ref, owner_ref, adapter_ref, *refs, columns, cut, held_count):
    output_ref = refs[len(refs) - held_count - 1]
    contract = (((1,), (1,)), ((), ()))
    for b in range(output_ref.shape[0]):
        hidden_ref, one_ref, two_ref = refs[3 * b : 3 * b + 3]
        output_ref[b] = lax.dot_general(
            hidden_ref[:, :cut], one_ref[:, columns:], contract, preferred_element_type=F32
        ) + lax.dot_general(hidden_ref[:, cut:], two_ref[...], contract, preferred_element_type=F32)


def shrink_rows(where, slot, hidden_states, pieces, tree_size, columns, cut, after, held):
    rank_size = pieces[0][0].shape[0]
    in_specs, operands = [], []
    for b, (one, two) in enumerate(pieces):
        in_specs += [
            pl.BlockSpec(
                (tree_size, hidden_states.shape[1]),
                lambda i, *refs, b=b: (request_at(refs, slot + b), 0),
            ),
            pl.BlockSpec(one.shape, lambda i, *refs: (0, 0)),
            pl.BlockSpec(two.shape, lambda i, *refs: (0, 0)),
        ]
        operands += [hidden_states, one, two]
    count = len(pieces)
    return pl.pallas_call(
        functools.partial(shrink_kernel, columns=columns, cut=cut, held_count=len(held)),
        grid_spec=pltpu.PrefetchScalarGridSpec(
            num_scalar_prefetch=3,
            grid=(1,),
            in_specs=in_specs + [ANYWHERE] * (len(after) + len(held)),
            out_specs=[pl.BlockSpec((count, tree_size, rank_size), lambda i, *refs: (0, 0, 0))]
            + [ANYWHERE] * len(held),
        ),
        out_shape=[jax.ShapeDtypeStruct((count, tree_size, rank_size), F32)] + shapes_of(held),
        input_output_aliases={3 + len(operands) + len(after) + k: 1 + k for k in range(len(held))},
        cost_estimate=pl.CostEstimate(
            flops=count * 300_000_000, bytes_accessed=count * 2_000_000, transcendentals=0
        ),
        compiler_params=pltpu.CompilerParams(vmem_limit_bytes=14 * 1024 * 1024),
        name="shrink",
    )(*where, *operands, *after, *held)


def finish_kernel(
    me_ref,
    owner_ref,
    adapter_ref,
    length_ref,
    here_ref,
    there_ref,
    shrunk_here_ref,
    shrunk_there_ref,
    table_ref,
    gain_ref,
    query_ref,
    key_ref,
    value_ref,
    *rest,
    count,
    slot,
    kv_heads,
):
    expand_refs = rest[:count]
    attention_ref, cache_ref, token_ref, expand_ref = rest[-4:]
    token_ref[...] = jnp.zeros_like(token_ref)
    tree_size, heads, head_size = query_ref.shape
    cached = key_ref.shape[0]
    per_group = heads // kv_heads
    rows = tree_size * heads
    columns = kv_heads * 2 * head_size
    spare = table_ref.shape[1] - 2 * head_size
    score_scale = math.log2(math.e) / math.sqrt(head_size)
    if count == 1:
        expand = expand_refs[0][...]
    else:
        for b in range(count):

            @pl.when(pl.program_id(0) == b)
            def _():
                expand_ref[...] = expand_refs[b][...]

        expand = expand_ref[...]
    length = length_ref[request_at((me_ref, owner_ref, adapter_ref), slot + pl.program_id(0))]
    shrunk = shrunk_here_ref[0] + shrunk_there_ref[0]
    high = shrunk.astype(BF16)
    left = shrunk - high.astype(F32)
    middle = left.astype(BF16)
    low = (left - middle.astype(F32)).astype(BF16)
    terms = jnp.dot(jnp.concatenate([low, middle, high], 0), expand, preferred_element_type=F32)
    delta = terms[:tree_size] + terms[tree_size : 2 * tree_size] + terms[2 * tree_size :]
    projected = (here_ref[...] + there_ref[...]) + delta
    cosine = table_ref[:, :head_size]
    sine = table_ref[:, head_size : 2 * head_size]
    gain = gain_ref[...]
    new_keys, new_values = [], []
    for g in range(kv_heads):
        at = 2 * head_size * g
        key = projected[:, at : at + head_size]
        new_values.append(projected[:, at + head_size : at + 2 * head_size].astype(BF16))
        norm = lax.rsqrt(jnp.mean(key * key, -1, keepdims=True) + 1e-06)
        key = key * norm * gain
        new_keys.append((key * cosine + pltpu.roll(key, head_size // 2, 1) * sine).astype(BF16))
    pad = jnp.zeros((spare - kv_heads * tree_size, head_size), BF16)
    keys = jnp.concatenate([key_ref[...]] + new_keys + [pad], 0)
    values = jnp.concatenate([value_ref[...]] + new_values + [pad], 0)
    scores = lax.dot_general(
        query_ref[...].reshape(rows, head_size),
        keys,
        (((1,), (1,)), ((), ())),
        preferred_element_type=F32,
    ).reshape(tree_size, heads, cached + spare)
    lane = lax.broadcasted_iota(jnp.int32, (heads, cached), 1)
    mine = lax.broadcasted_iota(jnp.int32, (heads, cached), 0) // per_group
    allowed = (lane % kv_heads == mine) & (lane // kv_heads < length)
    cached_bias = jnp.where(allowed, 0.0, -1e30)
    lane = lax.broadcasted_iota(jnp.int32, (heads, spare), 1)
    first = lax.broadcasted_iota(jnp.int32, (heads, spare), 0) // per_group * tree_size
    head_bias = jnp.where((lane >= first) & (lane < first + tree_size), 0.0, -1e30)
    node_bias = table_ref[:, 2 * head_size :]
    cached_scores = scores[:, :, :cached] + cached_bias[None]
    tree_scores = scores[:, :, cached:] + (node_bias[:, None, :] + head_bias[None])
    top = jnp.maximum(
        jnp.max(cached_scores, -1, keepdims=True), jnp.max(tree_scores, -1, keepdims=True)
    )
    cached_exponent = jnp.exp2((cached_scores - top) * score_scale)
    tree_exponent = jnp.exp2((tree_scores - top) * score_scale)
    total = jnp.sum(cached_exponent, -1, keepdims=True) + jnp.sum(tree_exponent, -1, keepdims=True)
    exponent = jnp.concatenate([cached_exponent, tree_exponent], -1)
    output = jnp.dot(
        exponent.astype(BF16).reshape(rows, cached + spare), values, preferred_element_type=F32
    ).reshape(tree_size, heads, head_size)
    attention_ref[...] = (output * (1.0 / total)).astype(BF16)
    stacked = jnp.concatenate(new_keys + new_values, 0)
    size = stacked.shape[0]
    cache_ref[...] = jnp.dot(
        sorting_matrix(size, size, size // tree_size, tree_size),
        stacked,
        preferred_element_type=F32,
    ).astype(BF16)


def finish(where, slot, batch, there, shared, previous):
    shrunk_here, shrunk_there, pieces = batch
    lengths, gain, here, table, queries, key_rows, value_rows = shared
    spot = lambda i, refs: request_at(refs[:3], slot + i)
    count, tree_size, rank_size = shrunk_here.shape
    requests = lengths.shape[0]
    rows, heads, head_size = queries.shape
    columns = here.shape[1]
    kv_heads = columns // (2 * head_size)
    row_block = lambda width: pl.BlockSpec((tree_size, width), lambda i, *refs: (spot(i, refs), 0))
    shrunk_block = pl.BlockSpec((1, tree_size, rank_size), lambda i, *refs: (i, 0, 0))
    cached_block = pl.BlockSpec(
        (key_rows.shape[0] // requests, head_size), lambda i, *refs: (spot(i, refs), 0)
    )
    query_block = pl.BlockSpec(
        (tree_size, heads, head_size), lambda i, *refs: (spot(i, refs), 0, 0)
    )
    in_specs = [
        row_block(columns),
        row_block(columns),
        shrunk_block,
        shrunk_block,
        row_block(table.shape[1]),
        pl.BlockSpec((1, head_size), lambda i, *refs: (0, 0)),
        query_block,
        cached_block,
        cached_block,
    ] + [pl.BlockSpec((rank_size, columns), lambda i, *refs: (0, 0))] * count
    operands = [*where, lengths, here, there, shrunk_here, shrunk_there, table, gain, queries]
    operands += [key_rows, value_rows, *pieces]
    aliases = {}
    if previous is not None:
        aliases = {len(operands): 0, len(operands) + 1: 1}
        operands += previous[:2]
        in_specs += [ANYWHERE] * 2
    cache_rows = 2 * kv_heads * tree_size
    return pl.pallas_call(
        functools.partial(finish_kernel, count=count, slot=slot, kv_heads=kv_heads),
        grid_spec=pltpu.PrefetchScalarGridSpec(
            num_scalar_prefetch=4,
            grid=(count,),
            in_specs=in_specs,
            out_specs=[
                query_block,
                pl.BlockSpec((cache_rows, head_size), lambda i, *refs: (spot(i, refs), 0)),
                pl.BlockSpec((8, 128), lambda i, *refs: (0, 0)),
            ],
            scratch_shapes=[pltpu.VMEM((rank_size, columns), BF16)],
        ),
        out_shape=[
            jax.ShapeDtypeStruct((rows, heads, head_size), BF16),
            jax.ShapeDtypeStruct((rows * 2 * kv_heads, head_size), BF16),
            jax.ShapeDtypeStruct((8, 128), F32),
        ],
        input_output_aliases=aliases,
        cost_estimate=pl.CostEstimate(
            flops=count * 900_000_000, bytes_accessed=count * 3_000_000, transcendentals=0
        ),
        compiler_params=pltpu.CompilerParams(vmem_limit_bytes=16 * 1024 * 1024),
        name="finish",
    )(*operands)


def per_device(
    hidden_states,
    kv_weight,
    shrink_factors,
    expand_factors,
    adapter_ids,
    cache_lengths,
    tree_parents,
    queries,
    cache_keys,
    cache_values,
    key_gain,
):
    requests, tree_size = tree_parents.shape
    row_count, half_width = hidden_states.shape
    kv_heads, kv_width = (kv_weight.shape[1], kv_weight.shape[2])
    head_size = kv_width // 2
    rank_size = shrink_factors.shape[2]
    context = cache_keys.shape[1]
    pool_count = lax.axis_size("pool")
    heads_here = kv_heads // lax.axis_size("tp")
    columns = heads_here * kv_width
    me = lax.axis_index("pool")
    core = lax.axis_index("tp").astype(jnp.int32).reshape(1)
    swap = [(0, 1), (1, 0)]

    def tile_rows(array):
        lead, heads = array.shape[0], array.shape[1]
        return array.reshape(lead, heads, 2, 128).transpose(0, 2, 1, 3).reshape(-1, 128)

    cut = (half_width + columns) // 2 - columns
    first, second = pack(
        core, shrink_factors[0].T, tile_rows(expand_factors[0]), cut, heads_here
    )

    order = ring_order(pool_count)
    onward = [(order[i], order[(i + 1) % pool_count]) for i in range(pool_count)]
    backward = [(b, a) for a, b in onward]
    half = pool_count // 2
    offsets = [[0]] + [[-step, step] for step in range(1, half)] + [[half]]
    flat_offsets = sum(offsets, [])
    owners = np.zeros((pool_count, pool_count), np.int32)
    for spot, index in enumerate(order):
        owners[index] = [order[(spot + offset) % pool_count] for offset in flat_offsets]
    where = (me.astype(jnp.int32).reshape(1), jnp.asarray(owners), adapter_ids)

    weight_rows = tile_rows(kv_weight)
    key_rows = cache_keys.reshape(-1, head_size)
    value_rows = cache_values.reshape(-1, head_size)

    arrivals = [(first, second)]
    front = rear = (first, second)
    table, weight_rows = tree_tables(
        cache_lengths, tree_parents, head_size, heads_here, weight_rows, [first]
    )
    for step in range(1, half):
        front = tuple(lax.ppermute(piece, "pool", onward) for piece in front)
        rear = tuple(lax.ppermute(piece, "pool", backward) for piece in rear)
        held = [front[1], rear[1]]
        if step == 1:
            here, away, *held = base_product(
                core, hidden_states, weight_rows, kv_heads * kv_width, [table], held
            )
        front, rear = (front[0], held[0]), (rear[0], held[1])
        arrivals += [front, rear]
    arrivals.append(
        (lax.ppermute(front[0], "pool", onward), lax.ppermute(rear[1], "pool", backward))
    )
    shared = (
        cache_lengths,
        key_gain.reshape(1, head_size),
        here,
        table,
        queries,
        key_rows,
        value_rows,
    )
    outputs = None
    if pool_count == requests:
        slot = 0
        for group in (arrivals[:-3], arrivals[-3:]):
            after = [] if outputs is None else [outputs[2]]
            held = [away] if outputs is None else []
            partial, *held = shrink_rows(
                where, slot, hidden_states, group, tree_size, columns, cut, after, held
            )
            if held:
                there = lax.ppermute(held[0], "tp", swap)
            batch = (partial, lax.ppermute(partial, "tp", swap), [piece[0] for piece in group])
            outputs = finish(where, slot, batch, there, shared, outputs)
            slot += len(group)
    else:
        parts = [
            shrink_rows(where, slot, hidden_states, [piece], tree_size, columns, cut, [], [])[0]
            for slot, piece in enumerate(arrivals)
        ]
        owners_here = lax.dynamic_index_in_dim(jnp.asarray(owners), me, 0, keepdims=False)
        hot = (adapter_ids[None, :] == owners_here[:, None]).astype(jnp.int32)
        slots = jnp.sum(hot * jnp.arange(pool_count, dtype=jnp.int32)[:, None], 0)
        partial = jnp.concatenate(parts, 0)[slots]
        expands = jnp.stack([piece[0][:, :columns] for piece in arrivals])[slots]
        every = jnp.arange(requests, dtype=jnp.int32)
        batch = (
            partial,
            lax.ppermute(partial, "tp", swap),
            [expands[r] for r in range(requests)],
        )
        there = lax.ppermute(away, "tp", swap)
        outputs = finish((every[:1], every[None, :], every), 0, batch, there, shared, None)
    attention, cache_rows, _ = outputs
    tree_cache = (
        cache_rows.reshape(row_count, 2, heads_here, head_size)
        .transpose(0, 2, 1, 3)
        .reshape(row_count, heads_here, kv_width)
    )
    return attention, tree_cache


def solution(mesh):
    placed = (
        P(("grp", "pool"), "tp"),
        P("tp", None, None),
        P(("grp", "pool"), "tp", None),
        P(("grp", "pool"), None, None, None),
        P(("grp", "pool")),
        P(("grp", "pool")),
        P(("grp", "pool"), None),
        P(("grp", "pool"), "tp", None),
        P(("grp", "pool"), None, "tp", None),
        P(("grp", "pool"), None, "tp", None),
        P(),
    )
    return jax.shard_map(
        per_device,
        mesh=mesh,
        in_specs=placed,
        out_specs=(P(("grp", "pool"), "tp", None), P(("grp", "pool"), "tp", None)),
        check_vma=False,
    )
```

```python
import functools
import math

import jax
import jax.numpy as jnp
import numpy as np
from jax import lax
from jax.experimental import pallas as pl
from jax.experimental.pallas import tpu as pltpu
from jax.sharding import PartitionSpec as P

F32 = jnp.float32
BF16 = jnp.bfloat16


ANYWHERE = pl.BlockSpec(memory_space=pl.ANY)


def shapes_of(arrays):
    return [jax.ShapeDtypeStruct(array.shape, array.dtype) for array in arrays]


def ring_order(count):
    if count == 8:
        return list(range(0, count, 2)) + list(range(count - 1, 0, -2))
    return list(range(count))


def sorting_matrix(rows, columns, inner, source_inner):
    row = lax.broadcasted_iota(jnp.int32, (rows, columns), 0)
    column = lax.broadcasted_iota(jnp.int32, (rows, columns), 1)
    return (column == (row % inner) * source_inner + row // inner).astype(F32).astype(BF16)


def picking_matrix(wanted, inner, groups, first_head):
    row = lax.broadcasted_iota(jnp.int32, (wanted * inner, 256), 0)
    column = lax.broadcasted_iota(jnp.int32, (wanted * inner, 256), 1)
    group = row // inner
    source = (group % 2) * (groups // 2) + first_head + group // 2
    return (column == (row % inner) * groups + source).astype(F32).astype(BF16)


def request_at(where, slot):
    me_ref, owner_ref, adapter_ref = where
    owner = owner_ref[me_ref[0], slot]
    request = jnp.int32(0)
    for r in range(1, adapter_ref.shape[0]):
        request = jnp.where(adapter_ref[r] == owner, jnp.int32(r), request)
    return request


def pack_kernel(core_ref, shrink_ref, expand_ref, first_ref, second_ref, *, cut, heads_here):
    rank_size = shrink_ref.shape[0]
    groups = expand_ref.shape[0] // rank_size
    ranks = 256 // groups
    pick = picking_matrix(2 * heads_here, ranks, groups, core_ref[0] * heads_here)
    columns = 2 * heads_here * 128
    for block in range(rank_size // ranks):
        sorted_rows = jnp.dot(
            pick, expand_ref[256 * block : 256 * (block + 1), :], preferred_element_type=F32
        ).astype(BF16)
        for g in range(2 * heads_here):
            first_ref[ranks * block : ranks * (block + 1), 128 * g : 128 * (g + 1)] = sorted_rows[
                ranks * g : ranks * (g + 1), :
            ]
    first_ref[:, columns:] = shrink_ref[:, :cut]
    second_ref[...] = shrink_ref[:, cut:]


def pack(core, shrink, expand_rows, cut, heads_here):
    rank_size, half_width = shrink.shape
    columns = 2 * heads_here * 128
    return pl.pallas_call(
        functools.partial(pack_kernel, cut=cut, heads_here=heads_here),
        grid_spec=pltpu.PrefetchScalarGridSpec(
            num_scalar_prefetch=1,
            grid=(1,),
            in_specs=[
                pl.BlockSpec(shrink.shape, lambda i, c: (0, 0)),
                pl.BlockSpec(expand_rows.shape, lambda i, c: (0, 0)),
            ],
            out_specs=[
                pl.BlockSpec((rank_size, columns + cut), lambda i, c: (0, 0)),
                pl.BlockSpec((rank_size, half_width - cut), lambda i, c: (0, 0)),
            ],
        ),
        out_shape=[
            jax.ShapeDtypeStruct((rank_size, columns + cut), BF16),
            jax.ShapeDtypeStruct((rank_size, half_width - cut), BF16),
        ],
        compiler_params=pltpu.CompilerParams(vmem_limit_bytes=8 * 1024 * 1024),
        name="pack",
    )(core, shrink, expand_rows)


def base_kernel(core_ref, hidden_ref, weight_ref, *rest, held_count):
    total_ref, wide_ref = rest[-2:]
    here_ref, away_ref = rest[-2 - held_count - 2 : -2 - held_count]
    step = pl.program_id(0)
    depth = hidden_ref.shape[1]
    groups = weight_ref.shape[0] // depth
    heads = groups // 2
    wide_ref[...] = weight_ref[...].astype(F32)
    parts = []
    for head in range(heads):
        tiles = [
            wide_ref[pl.ds(tile * heads + head, depth, stride=groups), :].astype(BF16)
            for tile in range(2)
        ]
        parts.append(
            jnp.dot(hidden_ref[...], jnp.concatenate(tiles, 1), preferred_element_type=F32)
        )
    product = jnp.concatenate(parts, 1)

    @pl.when(step == 0)
    def _():
        total_ref[...] = product

    @pl.when(step > 0)
    def _():
        total_ref[...] += product

    @pl.when(step == pl.num_programs(0) - 1)
    def _():
        columns = here_ref.shape[1]

        @pl.when(core_ref[0] == 0)
        def _():
            here_ref[...] = total_ref[:, :columns]
            away_ref[...] = total_ref[:, columns:]

        @pl.when(core_ref[0] == 1)
        def _():
            here_ref[...] = total_ref[:, columns:]
            away_ref[...] = total_ref[:, :columns]


def base_product(core, hidden_states, weight_rows, width, after, held):
    rows, half_width = hidden_states.shape
    groups = weight_rows.shape[0] // half_width
    depth = half_width // 2
    return pl.pallas_call(
        functools.partial(base_kernel, held_count=len(held)),
        grid_spec=pltpu.PrefetchScalarGridSpec(
            num_scalar_prefetch=1,
            grid=(half_width // depth,),
            in_specs=[
                pl.BlockSpec((rows, depth), lambda i, c: (0, i)),
                pl.BlockSpec((depth * groups, 128), lambda i, c: (i, 0)),
            ]
            + [ANYWHERE] * (len(after) + len(held)),
            out_specs=[pl.BlockSpec((rows, width // 2), lambda i, c: (0, 0))] * 2
            + [ANYWHERE] * len(held),
            scratch_shapes=[
                pltpu.VMEM((rows, width), F32),
                pltpu.VMEM((depth * groups, 128), F32),
            ],
        ),
        out_shape=[jax.ShapeDtypeStruct((rows, width // 2), F32)] * 2 + shapes_of(held),
        input_output_aliases={3 + len(after) + k: 2 + k for k in range(len(held))},
        cost_estimate=pl.CostEstimate(
            flops=4_000_000_000, bytes_accessed=9_000_000, transcendentals=0
        ),
        compiler_params=pltpu.CompilerParams(vmem_limit_bytes=24 * 1024 * 1024),
        name="base",
    )(core, hidden_states, weight_rows, *after, *held)


def tree_kernel(length_ref, parent_ref, frequency_ref, weight_ref, *rest, kv_heads):
    table_ref, moved_ref, semaphore = rest[-3:]
    move = pltpu.make_async_copy(weight_ref, moved_ref, semaphore)
    move.start()
    requests, nodes = parent_ref.shape
    head_size = frequency_ref.shape[1]
    node = lax.broadcasted_iota(jnp.int32, (nodes, nodes), 0)
    same = node == lax.broadcasted_iota(jnp.int32, (nodes, nodes), 1)
    spare = table_ref.shape[1] - 2 * head_size
    spread_node = lax.broadcasted_iota(jnp.int32, (nodes, spare), 0)
    spread_lane = lax.broadcasted_iota(jnp.int32, (nodes, spare), 1)
    spread = spread_lane == spread_node
    for g in range(1, kv_heads):
        spread = spread | (spread_lane == spread_node + nodes * g)
    spread = spread.astype(F32).astype(BF16)
    parents = parent_ref[...]
    below = [
        (same | (parents[r : r + 1, :] == node)).astype(F32).astype(BF16) for r in range(requests)
    ]
    reached = 1
    while reached < nodes:
        below = [
            jnp.minimum(jnp.dot(b, b, preferred_element_type=F32), 1.0).astype(BF16) for b in below
        ]
        reached = 2 * reached
    lane = lax.broadcasted_iota(jnp.int32, (nodes, head_size), 1)
    sign = jnp.where(lane < head_size // 2, -1.0, 1.0)
    ones = jnp.ones((nodes, head_size), BF16)
    for r in range(requests):
        b = below[r]
        depth = lax.dot_general(b, ones, (((0,), (0,)), ((), ())), preferred_element_type=F32)
        positions = length_ref[r].astype(F32) + depth - 1.0
        angles = positions * frequency_ref[...]
        rows = slice(nodes * r, nodes * (r + 1))
        wide = lax.dot_general(b, spread, (((0,), (0,)), ((), ())), preferred_element_type=F32)
        table_ref[rows, :] = jnp.concatenate(
            [jnp.cos(angles), jnp.sin(angles) * sign, jnp.where(wide > 0.5, 0.0, -1e30)], 1
        )
    move.wait()


def tree_tables(cache_lengths, tree_parents, head_size, kv_heads, weight_rows, after):
    requests, nodes = tree_parents.shape
    half_size = head_size // 2
    frequency = np.exp(np.arange(half_size) * (-2.0 * math.log(1000000.0) / head_size))
    frequency = np.concatenate([frequency, frequency]).reshape(1, head_size).astype(np.float32)
    whole = lambda shape: pl.BlockSpec(shape, lambda i, n: (0,) * len(shape))
    rows = requests * nodes
    width = 2 * head_size + -(-kv_heads * nodes // 128) * 128
    return pl.pallas_call(
        functools.partial(tree_kernel, kv_heads=kv_heads),
        grid_spec=pltpu.PrefetchScalarGridSpec(
            num_scalar_prefetch=1,
            grid=(1,),
            in_specs=[whole(tree_parents.shape), whole((1, head_size)), pl.BlockSpec(memory_space=pltpu.HBM)]
            + [ANYWHERE] * len(after),
            out_specs=[whole((rows, width)), ANYWHERE],
            scratch_shapes=[pltpu.SemaphoreType.DMA],
        ),
        out_shape=[jax.ShapeDtypeStruct((rows, width), F32)] + shapes_of([weight_rows]),
        cost_estimate=pl.CostEstimate(
            flops=1_000_000_000, bytes_accessed=8_000_000, transcendentals=0
        ),
        compiler_params=pltpu.CompilerParams(vmem_limit_bytes=8 * 1024 * 1024),
        name="tree",
    )(cache_lengths, tree_parents, frequency, weight_rows, *after)


def shrink_kernel(me_ref, owner_ref, adapter_ref, *refs, columns, cut):
    output_ref = refs[-1]
    contract = (((1,), (1,)), ((), ()))
    for b in range(output_ref.shape[0]):
        hidden_ref, away_ref, one_ref, two_ref = refs[4 * b : 4 * b + 4]
        output_ref[b, :, :columns] = away_ref[...]
        partial = lax.dot_general(
            hidden_ref[:, :cut], one_ref[:, columns:], contract, preferred_element_type=F32
        ) + lax.dot_general(hidden_ref[:, cut:], two_ref[...], contract, preferred_element_type=F32)
        output_ref[b, :, columns:] = jnp.concatenate([partial, jnp.zeros_like(partial)], 1)


def shrink_rows(where, slot, hidden_states, away, pieces, tree_size, columns, cut, after):
    rank_size = pieces[0][0].shape[0]
    in_specs, operands = [], []
    for b, (one, two) in enumerate(pieces):
        in_specs += [
            pl.BlockSpec(
                (tree_size, hidden_states.shape[1]),
                lambda i, *refs, b=b: (request_at(refs, slot + b), 0),
            ),
            pl.BlockSpec(
                (tree_size, columns), lambda i, *refs, b=b: (request_at(refs, slot + b), 0)
            ),
            pl.BlockSpec(one.shape, lambda i, *refs: (0, 0)),
            pl.BlockSpec(two.shape, lambda i, *refs: (0, 0)),
        ]
        operands += [hidden_states, away, one, two]
    count = len(pieces)
    width = columns + 2 * rank_size
    return pl.pallas_call(
        functools.partial(shrink_kernel, columns=columns, cut=cut),
        grid_spec=pltpu.PrefetchScalarGridSpec(
            num_scalar_prefetch=3,
            grid=(1,),
            in_specs=in_specs + [ANYWHERE] * len(after),
            out_specs=pl.BlockSpec((count, tree_size, width), lambda i, *refs: (0, 0, 0)),
        ),
        out_shape=jax.ShapeDtypeStruct((count, tree_size, width), F32),
        cost_estimate=pl.CostEstimate(
            flops=count * 30000000, bytes_accessed=count * 200000, transcendentals=0
        ),
        compiler_params=pltpu.CompilerParams(vmem_limit_bytes=14 * 1024 * 1024),
        name="shrink",
    )(*where, *operands, *after)


def finish_kernel(
    me_ref,
    owner_ref,
    adapter_ref,
    length_ref,
    here_ref,
    shrunk_here_ref,
    shrunk_there_ref,
    table_ref,
    gain_ref,
    query_ref,
    key_ref,
    value_ref,
    *rest,
    count,
    slot,
    kv_heads,
):
    expand_refs = rest[:count]
    attention_ref, cache_ref, token_ref, expand_ref = rest[-4:]
    token_ref[...] = jnp.zeros_like(token_ref)
    tree_size, heads, head_size = query_ref.shape
    cached = key_ref.shape[0]
    per_group = heads // kv_heads
    rows = tree_size * heads
    columns = kv_heads * 2 * head_size
    spare = table_ref.shape[1] - 2 * head_size
    score_scale = math.log2(math.e) / math.sqrt(head_size)
    if count == 1:
        expand = expand_refs[0][...]
    else:
        for b in range(count):

            @pl.when(pl.program_id(0) == b)
            def _():
                expand_ref[...] = expand_refs[b][...]

        expand = expand_ref[...]
    length = length_ref[request_at((me_ref, owner_ref, adapter_ref), slot + pl.program_id(0))]
    ranks = slice(columns, columns + expand.shape[0])
    shrunk = shrunk_here_ref[0, :, ranks] + shrunk_there_ref[0, :, ranks]
    high = shrunk.astype(BF16)
    left = shrunk - high.astype(F32)
    middle = left.astype(BF16)
    low = (left - middle.astype(F32)).astype(BF16)
    terms = jnp.dot(jnp.concatenate([low, middle, high], 0), expand, preferred_element_type=F32)
    delta = terms[:tree_size] + terms[tree_size : 2 * tree_size] + terms[2 * tree_size :]
    projected = (here_ref[...] + shrunk_there_ref[0, :, :columns]) + delta
    cosine = table_ref[:, :head_size]
    sine = table_ref[:, head_size : 2 * head_size]
    gain = gain_ref[...]
    new_keys, new_values = [], []
    for g in range(kv_heads):
        at = 2 * head_size * g
        key = projected[:, at : at + head_size]
        new_values.append(projected[:, at + head_size : at + 2 * head_size].astype(BF16))
        norm = lax.rsqrt(jnp.mean(key * key, -1, keepdims=True) + 1e-06)
        key = key * norm * gain
        new_keys.append((key * cosine + pltpu.roll(key, head_size // 2, 1) * sine).astype(BF16))
    pad = jnp.zeros((spare - kv_heads * tree_size, head_size), BF16)
    keys = jnp.concatenate([key_ref[...]] + new_keys + [pad], 0)
    values = jnp.concatenate([value_ref[...]] + new_values + [pad], 0)
    scores = lax.dot_general(
        query_ref[...].reshape(rows, head_size),
        keys,
        (((1,), (1,)), ((), ())),
        preferred_element_type=F32,
    ).reshape(tree_size, heads, cached + spare)
    lane = lax.broadcasted_iota(jnp.int32, (heads, cached), 1)
    mine = lax.broadcasted_iota(jnp.int32, (heads, cached), 0) // per_group
    allowed = (lane % kv_heads == mine) & (lane // kv_heads < length)
    cached_bias = jnp.where(allowed, 0.0, -1e30)
    lane = lax.broadcasted_iota(jnp.int32, (heads, spare), 1)
    first = lax.broadcasted_iota(jnp.int32, (heads, spare), 0) // per_group * tree_size
    head_bias = jnp.where((lane >= first) & (lane < first + tree_size), 0.0, -1e30)
    node_bias = table_ref[:, 2 * head_size :]
    cached_scores = scores[:, :, :cached] + cached_bias[None]
    tree_scores = scores[:, :, cached:] + (node_bias[:, None, :] + head_bias[None])
    top = jnp.maximum(
        jnp.max(cached_scores, -1, keepdims=True), jnp.max(tree_scores, -1, keepdims=True)
    )
    cached_exponent = jnp.exp2((cached_scores - top) * score_scale)
    tree_exponent = jnp.exp2((tree_scores - top) * score_scale)
    total = jnp.sum(cached_exponent, -1, keepdims=True) + jnp.sum(tree_exponent, -1, keepdims=True)
    exponent = jnp.concatenate([cached_exponent, tree_exponent], -1)
    output = jnp.dot(
        exponent.astype(BF16).reshape(rows, cached + spare), values, preferred_element_type=F32
    ).reshape(tree_size, heads, head_size)
    attention_ref[...] = (output * (1.0 / total)).astype(BF16)
    stacked = jnp.concatenate(new_keys + new_values, 0)
    size = stacked.shape[0]
    cache_ref[...] = jnp.dot(
        sorting_matrix(size, size, size // tree_size, tree_size),
        stacked,
        preferred_element_type=F32,
    ).astype(BF16)


def finish(where, slot, batch, shared, previous):
    shrunk_here, shrunk_there, pieces = batch
    lengths, gain, here, table, queries, key_rows, value_rows = shared
    spot = lambda i, refs: request_at(refs[:3], slot + i)
    count, tree_size, width = shrunk_here.shape
    rank_size = pieces[0].shape[0]
    requests = lengths.shape[0]
    rows, heads, head_size = queries.shape
    columns = here.shape[1]
    kv_heads = columns // (2 * head_size)
    row_block = lambda width: pl.BlockSpec((tree_size, width), lambda i, *refs: (spot(i, refs), 0))
    shrunk_block = pl.BlockSpec((1, tree_size, width), lambda i, *refs: (i, 0, 0))
    cached_block = pl.BlockSpec(
        (key_rows.shape[0] // requests, head_size), lambda i, *refs: (spot(i, refs), 0)
    )
    query_block = pl.BlockSpec(
        (tree_size, heads, head_size), lambda i, *refs: (spot(i, refs), 0, 0)
    )
    in_specs = [
        row_block(columns),
        shrunk_block,
        shrunk_block,
        row_block(table.shape[1]),
        pl.BlockSpec((1, head_size), lambda i, *refs: (0, 0)),
        query_block,
        cached_block,
        cached_block,
    ] + [pl.BlockSpec((rank_size, columns), lambda i, *refs: (0, 0))] * count
    operands = [*where, lengths, here, shrunk_here, shrunk_there, table, gain, queries]
    operands += [key_rows, value_rows, *pieces]
    aliases = {}
    if previous is not None:
        aliases = {len(operands): 0, len(operands) + 1: 1}
        operands += previous[:2]
        in_specs += [ANYWHERE] * 2
    cache_rows = 2 * kv_heads * tree_size
    return pl.pallas_call(
        functools.partial(finish_kernel, count=count, slot=slot, kv_heads=kv_heads),
        grid_spec=pltpu.PrefetchScalarGridSpec(
            num_scalar_prefetch=4,
            grid=(count,),
            in_specs=in_specs,
            out_specs=[
                query_block,
                pl.BlockSpec((cache_rows, head_size), lambda i, *refs: (spot(i, refs), 0)),
                pl.BlockSpec((8, 128), lambda i, *refs: (0, 0)),
            ],
            scratch_shapes=[pltpu.VMEM((rank_size, columns), BF16)],
        ),
        out_shape=[
            jax.ShapeDtypeStruct((rows, heads, head_size), BF16),
            jax.ShapeDtypeStruct((rows * 2 * kv_heads, head_size), BF16),
            jax.ShapeDtypeStruct((8, 128), F32),
        ],
        input_output_aliases=aliases,
        cost_estimate=pl.CostEstimate(
            flops=count * 90000000, bytes_accessed=count * 300000, transcendentals=0
        ),
        compiler_params=pltpu.CompilerParams(vmem_limit_bytes=16 * 1024 * 1024),
        name="finish",
    )(*operands)


def per_device(
    hidden_states,
    kv_weight,
    shrink_factors,
    expand_factors,
    adapter_ids,
    cache_lengths,
    tree_parents,
    queries,
    cache_keys,
    cache_values,
    key_gain,
):
    requests, tree_size = tree_parents.shape
    row_count, half_width = hidden_states.shape
    kv_heads, kv_width = (kv_weight.shape[1], kv_weight.shape[2])
    head_size = kv_width // 2
    rank_size = shrink_factors.shape[2]
    context = cache_keys.shape[1]
    pool_count = lax.axis_size("pool")
    heads_here = kv_heads // lax.axis_size("tp")
    columns = heads_here * kv_width
    me = lax.axis_index("pool")
    core = lax.axis_index("tp").astype(jnp.int32).reshape(1)
    swap = [(0, 1), (1, 0)]

    def tile_rows(array):
        lead, heads = array.shape[0], array.shape[1]
        return array.reshape(lead, heads, 2, 128).transpose(0, 2, 1, 3).reshape(-1, 128)

    cut = (half_width + columns) // 2 - columns
    first, second = pack(
        core, shrink_factors[0].T, tile_rows(expand_factors[0]), cut, heads_here
    )

    order = ring_order(pool_count)
    onward = [(order[i], order[(i + 1) % pool_count]) for i in range(pool_count)]
    backward = [(b, a) for a, b in onward]
    half = pool_count // 2
    offsets = [[0]] + [[-step, step] for step in range(1, half)] + [[half]]
    flat_offsets = sum(offsets, [])
    owners = np.zeros((pool_count, pool_count), np.int32)
    for spot, index in enumerate(order):
        owners[index] = [order[(spot + offset) % pool_count] for offset in flat_offsets]
    where = (me.astype(jnp.int32).reshape(1), jnp.asarray(owners), adapter_ids)

    weight_rows = tile_rows(kv_weight)
    key_rows = cache_keys.reshape(-1, head_size)
    value_rows = cache_values.reshape(-1, head_size)

    arrivals = [(first, second)]
    front = rear = (first, second)
    table, weight_rows = tree_tables(
        cache_lengths, tree_parents, head_size, heads_here, weight_rows, [first]
    )
    for step in range(1, half):
        front = tuple(lax.ppermute(piece, "pool", onward) for piece in front)
        rear = tuple(lax.ppermute(piece, "pool", backward) for piece in rear)
        held = [front[1], rear[1]]
        if step == 1:
            here, away, *held = base_product(
                core, hidden_states, weight_rows, kv_heads * kv_width, [table], held
            )
        front, rear = (front[0], held[0]), (rear[0], held[1])
        arrivals += [front, rear]
    arrivals.append(
        (lax.ppermute(front[0], "pool", onward), lax.ppermute(rear[1], "pool", backward))
    )
    shared = (
        cache_lengths,
        key_gain.reshape(1, head_size),
        here,
        table,
        queries,
        key_rows,
        value_rows,
    )
    outputs = None
    if pool_count == requests:
        near = 3
        groups = [
            (arrivals[:near], []),
            (arrivals[near:-3], []),
            (arrivals[-3:], []),
        ]
        slot = 0
        for group, after in groups:
            if outputs is not None:
                after = after + [outputs[2]]
            partial = shrink_rows(
                where, slot, hidden_states, away, group, tree_size, columns, cut, after
            )
            batch = (partial, lax.ppermute(partial, "tp", swap), [piece[0] for piece in group])
            outputs = finish(where, slot, batch, shared, outputs)
            slot += len(group)
    else:
        parts = [
            shrink_rows(where, slot, hidden_states, away, [piece], tree_size, columns, cut, [])
            for slot, piece in enumerate(arrivals)
        ]
        owners_here = lax.dynamic_index_in_dim(jnp.asarray(owners), me, 0, keepdims=False)
        hot = (adapter_ids[None, :] == owners_here[:, None]).astype(jnp.int32)
        slots = jnp.sum(hot * jnp.arange(pool_count, dtype=jnp.int32)[:, None], 0)
        partial = jnp.concatenate(parts, 0)[slots]
        expands = jnp.stack([piece[0][:, :columns] for piece in arrivals])[slots]
        every = jnp.arange(requests, dtype=jnp.int32)
        batch = (
            partial,
            lax.ppermute(partial, "tp", swap),
            [expands[r] for r in range(requests)],
        )
        outputs = finish((every[:1], every[None, :], every), 0, batch, shared, None)
    attention, cache_rows, _ = outputs
    tree_cache = (
        cache_rows.reshape(row_count, 2, heads_here, head_size)
        .transpose(0, 2, 1, 3)
        .reshape(row_count, heads_here, kv_width)
    )
    return attention, tree_cache


def solution(mesh):
    placed = (
        P(("grp", "pool"), "tp"),
        P("tp", None, None),
        P(("grp", "pool"), "tp", None),
        P(("grp", "pool"), None, None, None),
        P(("grp", "pool")),
        P(("grp", "pool")),
        P(("grp", "pool"), None),
        P(("grp", "pool"), "tp", None),
        P(("grp", "pool"), None, "tp", None),
        P(("grp", "pool"), None, "tp", None),
        P(),
    )
    return jax.shard_map(
        per_device,
        mesh=mesh,
        in_specs=placed,
        out_specs=(P(("grp", "pool"), "tp", None), P(("grp", "pool"), "tp", None)),
        check_vma=False,
    )
```

```python
import functools
import math

import jax
import jax.numpy as jnp
import numpy as np
from jax import lax
from jax.experimental import pallas as pl
from jax.experimental.pallas import tpu as pltpu
from jax.sharding import PartitionSpec as P

F32 = jnp.float32
BF16 = jnp.bfloat16


ANYWHERE = pl.BlockSpec(memory_space=pl.ANY)


def shapes_of(arrays):
    return [jax.ShapeDtypeStruct(array.shape, array.dtype) for array in arrays]


def ring_order(count):
    if count == 8:
        return list(range(0, count, 2)) + list(range(count - 1, 0, -2))
    return list(range(count))


def sorting_matrix(rows, columns, inner, source_inner):
    row = lax.broadcasted_iota(jnp.int32, (rows, columns), 0)
    column = lax.broadcasted_iota(jnp.int32, (rows, columns), 1)
    return (column == (row % inner) * source_inner + row // inner).astype(F32).astype(BF16)


def picking_matrix(wanted, inner, groups, first_head):
    row = lax.broadcasted_iota(jnp.int32, (wanted * inner, 256), 0)
    column = lax.broadcasted_iota(jnp.int32, (wanted * inner, 256), 1)
    group = row // inner
    source = (group % 2) * (groups // 2) + first_head + group // 2
    return (column == (row % inner) * groups + source).astype(F32).astype(BF16)


def request_at(where, slot):
    me_ref, owner_ref, adapter_ref = where
    owner = owner_ref[me_ref[0], slot]
    request = jnp.int32(0)
    for r in range(1, adapter_ref.shape[0]):
        request = jnp.where(adapter_ref[r] == owner, jnp.int32(r), request)
    return request


def pack_kernel(core_ref, shrink_ref, expand_ref, first_ref, second_ref, *, cut, heads_here):
    rank_size = shrink_ref.shape[0]
    groups = expand_ref.shape[0] // rank_size
    ranks = 256 // groups
    pick = picking_matrix(2 * heads_here, ranks, groups, core_ref[0] * heads_here)
    columns = 2 * heads_here * 128
    for block in range(rank_size // ranks):
        sorted_rows = jnp.dot(
            pick, expand_ref[256 * block : 256 * (block + 1), :], preferred_element_type=F32
        ).astype(BF16)
        for g in range(2 * heads_here):
            first_ref[ranks * block : ranks * (block + 1), 128 * g : 128 * (g + 1)] = sorted_rows[
                ranks * g : ranks * (g + 1), :
            ]
    first_ref[:, columns:] = shrink_ref[:, :cut]
    second_ref[...] = shrink_ref[:, cut:]


def pack(core, shrink, expand_rows, cut, heads_here):
    rank_size, half_width = shrink.shape
    columns = 2 * heads_here * 128
    return pl.pallas_call(
        functools.partial(pack_kernel, cut=cut, heads_here=heads_here),
        grid_spec=pltpu.PrefetchScalarGridSpec(
            num_scalar_prefetch=1,
            grid=(1,),
            in_specs=[
                pl.BlockSpec(shrink.shape, lambda i, c: (0, 0)),
                pl.BlockSpec(expand_rows.shape, lambda i, c: (0, 0)),
            ],
            out_specs=[
                pl.BlockSpec((rank_size, columns + cut), lambda i, c: (0, 0)),
                pl.BlockSpec((rank_size, half_width - cut), lambda i, c: (0, 0)),
            ],
        ),
        out_shape=[
            jax.ShapeDtypeStruct((rank_size, columns + cut), BF16),
            jax.ShapeDtypeStruct((rank_size, half_width - cut), BF16),
        ],
        compiler_params=pltpu.CompilerParams(vmem_limit_bytes=8 * 1024 * 1024),
        name="pack",
    )(core, shrink, expand_rows)


def base_kernel(core_ref, hidden_ref, weight_ref, *rest, held_count):
    total_ref, wide_ref = rest[-2:]
    here_ref, away_ref = rest[-2 - held_count - 2 : -2 - held_count]
    step = pl.program_id(0)
    depth = hidden_ref.shape[1]
    groups = weight_ref.shape[0] // depth
    heads = groups // 2
    wide_ref[...] = weight_ref[...].astype(F32)
    parts = []
    for head in range(heads):
        tiles = [
            wide_ref[pl.ds(tile * heads + head, depth, stride=groups), :].astype(BF16)
            for tile in range(2)
        ]
        parts.append(
            jnp.dot(hidden_ref[...], jnp.concatenate(tiles, 1), preferred_element_type=F32)
        )
    product = jnp.concatenate(parts, 1)

    @pl.when(step == 0)
    def _():
        total_ref[...] = product

    @pl.when(step > 0)
    def _():
        total_ref[...] += product

    @pl.when(step == pl.num_programs(0) - 1)
    def _():
        columns = here_ref.shape[1]

        @pl.when(core_ref[0] == 0)
        def _():
            here_ref[...] = total_ref[:, :columns]
            away_ref[...] = total_ref[:, columns:]

        @pl.when(core_ref[0] == 1)
        def _():
            here_ref[...] = total_ref[:, columns:]
            away_ref[...] = total_ref[:, :columns]


def base_product(core, hidden_states, weight_rows, width, after, held):
    rows, half_width = hidden_states.shape
    groups = weight_rows.shape[0] // half_width
    depth = half_width // 2
    return pl.pallas_call(
        functools.partial(base_kernel, held_count=len(held)),
        grid_spec=pltpu.PrefetchScalarGridSpec(
            num_scalar_prefetch=1,
            grid=(half_width // depth,),
            in_specs=[
                pl.BlockSpec((rows, depth), lambda i, c: (0, i)),
                pl.BlockSpec((depth * groups, 128), lambda i, c: (i, 0)),
            ]
            + [ANYWHERE] * (len(after) + len(held)),
            out_specs=[pl.BlockSpec((rows, width // 2), lambda i, c: (0, 0))] * 2
            + [ANYWHERE] * len(held),
            scratch_shapes=[
                pltpu.VMEM((rows, width), F32),
                pltpu.VMEM((depth * groups, 128), F32),
            ],
        ),
        out_shape=[jax.ShapeDtypeStruct((rows, width // 2), F32)] * 2 + shapes_of(held),
        input_output_aliases={3 + len(after) + k: 2 + k for k in range(len(held))},
        cost_estimate=pl.CostEstimate(
            flops=4_000_000_000, bytes_accessed=9_000_000, transcendentals=0
        ),
        compiler_params=pltpu.CompilerParams(vmem_limit_bytes=24 * 1024 * 1024),
        name="base",
    )(core, hidden_states, weight_rows, *after, *held)


def tree_kernel(length_ref, parent_ref, weight_ref, *rest, head_size, kv_heads):
    table_ref, moved_ref, semaphore = rest[-3:]
    move = pltpu.make_async_copy(weight_ref, moved_ref, semaphore)
    move.start()
    requests, nodes = parent_ref.shape
    node = lax.broadcasted_iota(jnp.int32, (nodes, nodes), 0)
    same = node == lax.broadcasted_iota(jnp.int32, (nodes, nodes), 1)
    spare = table_ref.shape[1] - 2 * head_size
    spread_node = lax.broadcasted_iota(jnp.int32, (nodes, spare), 0)
    spread_lane = lax.broadcasted_iota(jnp.int32, (nodes, spare), 1)
    spread = spread_lane == spread_node
    for g in range(1, kv_heads):
        spread = spread | (spread_lane == spread_node + nodes * g)
    spread = spread.astype(F32).astype(BF16)
    parents = parent_ref[...]
    below = [
        (same | (parents[r : r + 1, :] == node)).astype(F32).astype(BF16) for r in range(requests)
    ]
    reached = 1
    while reached < nodes:
        below = [
            jnp.minimum(jnp.dot(b, b, preferred_element_type=F32), 1.0).astype(BF16) for b in below
        ]
        reached = 2 * reached
    lane = lax.broadcasted_iota(jnp.int32, (nodes, head_size), 1)
    sign = jnp.where(lane < head_size // 2, -1.0, 1.0)
    power = lax.broadcasted_iota(jnp.int32, (1, head_size), 1) % (head_size // 2)
    frequency = jnp.exp(power.astype(F32) * (-2.0 * math.log(1000000.0) / head_size))
    ones = jnp.ones((nodes, head_size), BF16)
    for r in range(requests):
        b = below[r]
        depth = lax.dot_general(b, ones, (((0,), (0,)), ((), ())), preferred_element_type=F32)
        positions = length_ref[r].astype(F32) + depth - 1.0
        angles = positions * frequency
        rows = slice(nodes * r, nodes * (r + 1))
        wide = lax.dot_general(b, spread, (((0,), (0,)), ((), ())), preferred_element_type=F32)
        table_ref[rows, :] = jnp.concatenate(
            [jnp.cos(angles), jnp.sin(angles) * sign, jnp.where(wide > 0.5, 0.0, -1e30)], 1
        )
    move.wait()


def tree_tables(cache_lengths, tree_parents, head_size, kv_heads, weight_rows, after):
    requests, nodes = tree_parents.shape
    whole = lambda shape: pl.BlockSpec(shape, lambda i, n: (0,) * len(shape))
    rows = requests * nodes
    width = 2 * head_size + -(-kv_heads * nodes // 128) * 128
    return pl.pallas_call(
        functools.partial(tree_kernel, head_size=head_size, kv_heads=kv_heads),
        grid_spec=pltpu.PrefetchScalarGridSpec(
            num_scalar_prefetch=1,
            grid=(1,),
            in_specs=[whole(tree_parents.shape), ANYWHERE]
            + [ANYWHERE] * len(after),
            out_specs=[whole((rows, width)), ANYWHERE],
            scratch_shapes=[pltpu.SemaphoreType.DMA],
        ),
        out_shape=[jax.ShapeDtypeStruct((rows, width), F32)] + shapes_of([weight_rows]),
        cost_estimate=pl.CostEstimate(
            flops=1_000_000_000, bytes_accessed=8_000_000, transcendentals=0
        ),
        compiler_params=pltpu.CompilerParams(vmem_limit_bytes=8 * 1024 * 1024),
        name="tree",
    )(cache_lengths, tree_parents, weight_rows, *after)


def shrink_kernel(me_ref, owner_ref, adapter_ref, *refs, columns, cut):
    output_ref = refs[-1]
    contract = (((1,), (1,)), ((), ()))
    for b in range(output_ref.shape[0]):
        hidden_ref, away_ref, one_ref, two_ref = refs[4 * b : 4 * b + 4]
        output_ref[b, :, :columns] = away_ref[...]
        partial = lax.dot_general(
            hidden_ref[:, :cut], one_ref[:, columns:], contract, preferred_element_type=F32
        ) + lax.dot_general(hidden_ref[:, cut:], two_ref[...], contract, preferred_element_type=F32)
        output_ref[b, :, columns:] = jnp.concatenate([partial, jnp.zeros_like(partial)], 1)


def shrink_rows(where, slot, hidden_states, away, pieces, tree_size, columns, cut, after):
    rank_size = pieces[0][0].shape[0]
    in_specs, operands = [], []
    for b, (one, two) in enumerate(pieces):
        in_specs += [
            pl.BlockSpec(
                (tree_size, hidden_states.shape[1]),
                lambda i, *refs, b=b: (request_at(refs, slot + b), 0),
            ),
            pl.BlockSpec(
                (tree_size, columns), lambda i, *refs, b=b: (request_at(refs, slot + b), 0)
            ),
            pl.BlockSpec(one.shape, lambda i, *refs: (0, 0)),
            pl.BlockSpec(two.shape, lambda i, *refs: (0, 0)),
        ]
        operands += [hidden_states, away, one, two]
    count = len(pieces)
    width = columns + 2 * rank_size
    return pl.pallas_call(
        functools.partial(shrink_kernel, columns=columns, cut=cut),
        grid_spec=pltpu.PrefetchScalarGridSpec(
            num_scalar_prefetch=3,
            grid=(1,),
            in_specs=in_specs + [ANYWHERE] * len(after),
            out_specs=pl.BlockSpec((count, tree_size, width), lambda i, *refs: (0, 0, 0)),
        ),
        out_shape=jax.ShapeDtypeStruct((count, tree_size, width), F32),
        cost_estimate=pl.CostEstimate(
            flops=count * 30000000, bytes_accessed=count * 200000, transcendentals=0
        ),
        compiler_params=pltpu.CompilerParams(vmem_limit_bytes=14 * 1024 * 1024),
        name="shrink",
    )(*where, *operands, *after)


def finish_kernel(
    me_ref,
    owner_ref,
    adapter_ref,
    length_ref,
    here_ref,
    shrunk_here_ref,
    shrunk_there_ref,
    table_ref,
    gain_ref,
    query_ref,
    key_ref,
    value_ref,
    *rest,
    count,
    slot,
    kv_heads,
):
    expand_refs = rest[:count]
    attention_ref, cache_ref, token_ref, expand_ref = rest[-4:]
    token_ref[...] = jnp.zeros_like(token_ref)
    tree_size, heads, head_size = query_ref.shape
    cached = key_ref.shape[0]
    per_group = heads // kv_heads
    rows = tree_size * heads
    columns = kv_heads * 2 * head_size
    spare = table_ref.shape[1] - 2 * head_size
    score_scale = math.log2(math.e) / math.sqrt(head_size)
    if count == 1:
        expand = expand_refs[0][...]
    else:
        for b in range(count):

            @pl.when(pl.program_id(0) == b)
            def _():
                expand_ref[...] = expand_refs[b][...]

        expand = expand_ref[...]
    length = length_ref[request_at((me_ref, owner_ref, adapter_ref), slot + pl.program_id(0))]
    ranks = slice(columns, columns + expand.shape[0])
    shrunk = shrunk_here_ref[0, :, ranks] + shrunk_there_ref[0, :, ranks]
    high = shrunk.astype(BF16)
    left = shrunk - high.astype(F32)
    middle = left.astype(BF16)
    low = (left - middle.astype(F32)).astype(BF16)
    terms = jnp.dot(jnp.concatenate([low, middle, high], 0), expand, preferred_element_type=F32)
    delta = terms[:tree_size] + terms[tree_size : 2 * tree_size] + terms[2 * tree_size :]
    projected = (here_ref[...] + shrunk_there_ref[0, :, :columns]) + delta
    cosine = table_ref[:, :head_size]
    sine = table_ref[:, head_size : 2 * head_size]
    gain = gain_ref[...]
    new_keys, new_values = [], []
    for g in range(kv_heads):
        at = 2 * head_size * g
        key = projected[:, at : at + head_size]
        new_values.append(projected[:, at + head_size : at + 2 * head_size].astype(BF16))
        norm = lax.rsqrt(jnp.mean(key * key, -1, keepdims=True) + 1e-06)
        key = key * norm * gain
        new_keys.append((key * cosine + pltpu.roll(key, head_size // 2, 1) * sine).astype(BF16))
    pad = jnp.zeros((spare - kv_heads * tree_size, head_size), BF16)
    keys = jnp.concatenate([key_ref[...]] + new_keys + [pad], 0)
    values = jnp.concatenate([value_ref[...]] + new_values + [pad], 0)
    scores = lax.dot_general(
        query_ref[...].reshape(rows, head_size),
        keys,
        (((1,), (1,)), ((), ())),
        preferred_element_type=F32,
    ).reshape(tree_size, heads, cached + spare)
    lane = lax.broadcasted_iota(jnp.int32, (heads, cached), 1)
    mine = lax.broadcasted_iota(jnp.int32, (heads, cached), 0) // per_group
    allowed = (lane % kv_heads == mine) & (lane // kv_heads < length)
    cached_bias = jnp.where(allowed, 0.0, -1e30)
    lane = lax.broadcasted_iota(jnp.int32, (heads, spare), 1)
    first = lax.broadcasted_iota(jnp.int32, (heads, spare), 0) // per_group * tree_size
    head_bias = jnp.where((lane >= first) & (lane < first + tree_size), 0.0, -1e30)
    node_bias = table_ref[:, 2 * head_size :]
    cached_scores = scores[:, :, :cached] + cached_bias[None]
    tree_scores = scores[:, :, cached:] + (node_bias[:, None, :] + head_bias[None])
    top = jnp.maximum(
        jnp.max(cached_scores, -1, keepdims=True), jnp.max(tree_scores, -1, keepdims=True)
    )
    cached_exponent = jnp.exp2((cached_scores - top) * score_scale)
    tree_exponent = jnp.exp2((tree_scores - top) * score_scale)
    total = jnp.sum(cached_exponent, -1, keepdims=True) + jnp.sum(tree_exponent, -1, keepdims=True)
    exponent = jnp.concatenate([cached_exponent, tree_exponent], -1)
    output = jnp.dot(
        exponent.astype(BF16).reshape(rows, cached + spare), values, preferred_element_type=F32
    ).reshape(tree_size, heads, head_size)
    attention_ref[...] = (output * (1.0 / total)).astype(BF16)
    stacked = jnp.concatenate(new_keys + new_values, 0)
    size = stacked.shape[0]
    cache_ref[...] = jnp.dot(
        sorting_matrix(size, size, size // tree_size, tree_size),
        stacked,
        preferred_element_type=F32,
    ).astype(BF16)


def finish(where, slot, batch, shared, previous):
    shrunk_here, shrunk_there, pieces = batch
    lengths, gain, here, table, queries, key_rows, value_rows = shared
    spot = lambda i, refs: request_at(refs[:3], slot + i)
    count, tree_size, width = shrunk_here.shape
    rank_size = pieces[0].shape[0]
    requests = lengths.shape[0]
    rows, heads, head_size = queries.shape
    columns = here.shape[1]
    kv_heads = columns // (2 * head_size)
    row_block = lambda width: pl.BlockSpec((tree_size, width), lambda i, *refs: (spot(i, refs), 0))
    shrunk_block = pl.BlockSpec((1, tree_size, width), lambda i, *refs: (i, 0, 0))
    cached_block = pl.BlockSpec(
        (key_rows.shape[0] // requests, head_size), lambda i, *refs: (spot(i, refs), 0)
    )
    query_block = pl.BlockSpec(
        (tree_size, heads, head_size), lambda i, *refs: (spot(i, refs), 0, 0)
    )
    in_specs = [
        row_block(columns),
        shrunk_block,
        shrunk_block,
        row_block(table.shape[1]),
        pl.BlockSpec((1, head_size), lambda i, *refs: (0, 0)),
        query_block,
        cached_block,
        cached_block,
    ] + [pl.BlockSpec((rank_size, columns), lambda i, *refs: (0, 0))] * count
    operands = [*where, lengths, here, shrunk_here, shrunk_there, table, gain, queries]
    operands += [key_rows, value_rows, *pieces]
    aliases = {}
    if previous is not None:
        aliases = {len(operands): 0, len(operands) + 1: 1}
        operands += previous[:2]
        in_specs += [ANYWHERE] * 2
    cache_rows = 2 * kv_heads * tree_size
    return pl.pallas_call(
        functools.partial(finish_kernel, count=count, slot=slot, kv_heads=kv_heads),
        grid_spec=pltpu.PrefetchScalarGridSpec(
            num_scalar_prefetch=4,
            grid=(count,),
            in_specs=in_specs,
            out_specs=[
                query_block,
                pl.BlockSpec((cache_rows, head_size), lambda i, *refs: (spot(i, refs), 0)),
                pl.BlockSpec((8, 128), lambda i, *refs: (0, 0)),
            ],
            scratch_shapes=[pltpu.VMEM((rank_size, columns), BF16)],
        ),
        out_shape=[
            jax.ShapeDtypeStruct((rows, heads, head_size), BF16),
            jax.ShapeDtypeStruct((rows * 2 * kv_heads, head_size), BF16),
            jax.ShapeDtypeStruct((8, 128), F32),
        ],
        input_output_aliases=aliases,
        cost_estimate=pl.CostEstimate(
            flops=count * 900000000, bytes_accessed=count * 3000000, transcendentals=0
        ),
        compiler_params=pltpu.CompilerParams(vmem_limit_bytes=16 * 1024 * 1024),
        name="finish",
    )(*operands)


def per_device(
    hidden_states,
    kv_weight,
    shrink_factors,
    expand_factors,
    adapter_ids,
    cache_lengths,
    tree_parents,
    queries,
    cache_keys,
    cache_values,
    key_gain,
):
    requests, tree_size = tree_parents.shape
    row_count, half_width = hidden_states.shape
    kv_heads, kv_width = (kv_weight.shape[1], kv_weight.shape[2])
    head_size = kv_width // 2
    rank_size = shrink_factors.shape[2]
    context = cache_keys.shape[1]
    pool_count = lax.axis_size("pool")
    heads_here = kv_heads // lax.axis_size("tp")
    columns = heads_here * kv_width
    me = lax.axis_index("pool")
    core = lax.axis_index("tp").astype(jnp.int32).reshape(1)
    swap = [(0, 1), (1, 0)]

    def tile_rows(array):
        lead, heads = array.shape[0], array.shape[1]
        return array.reshape(lead, heads, 2, 128).transpose(0, 2, 1, 3).reshape(-1, 128)

    cut = (half_width + columns) // 2 - columns
    first, second = pack(
        core, shrink_factors[0].T, tile_rows(expand_factors[0]), cut, heads_here
    )

    order = ring_order(pool_count)
    onward = [(order[i], order[(i + 1) % pool_count]) for i in range(pool_count)]
    backward = [(b, a) for a, b in onward]
    half = pool_count // 2
    offsets = [[0]] + [[-step, step] for step in range(1, half)] + [[half]]
    flat_offsets = sum(offsets, [])
    owners = np.zeros((pool_count, pool_count), np.int32)
    for spot, index in enumerate(order):
        owners[index] = [order[(spot + offset) % pool_count] for offset in flat_offsets]
    where = (me.astype(jnp.int32).reshape(1), jnp.asarray(owners), adapter_ids)

    weight_rows = tile_rows(kv_weight)
    key_rows = cache_keys.reshape(-1, head_size)
    value_rows = cache_values.reshape(-1, head_size)

    arrivals = [(first, second)]
    front = rear = (first, second)
    table, weight_rows = tree_tables(
        cache_lengths, tree_parents, head_size, heads_here, weight_rows, [first]
    )
    for step in range(1, half):
        front = tuple(lax.ppermute(piece, "pool", onward) for piece in front)
        rear = tuple(lax.ppermute(piece, "pool", backward) for piece in rear)
        held = [front[1], rear[1]]
        if step == 1:
            here, away, *held = base_product(
                core, hidden_states, weight_rows, kv_heads * kv_width, [table], held
            )
        front, rear = (front[0], held[0]), (rear[0], held[1])
        arrivals += [front, rear]
    arrivals.append(
        (lax.ppermute(front[0], "pool", onward), lax.ppermute(rear[1], "pool", backward))
    )
    shared = (
        cache_lengths,
        key_gain.reshape(1, head_size),
        here,
        table,
        queries,
        key_rows,
        value_rows,
    )
    outputs = None
    if pool_count == requests:
        near = 3
        groups = [
            (arrivals[:near], []),
            (arrivals[near:-3], []),
            (arrivals[-3:], []),
        ]
        slot = 0
        for group, after in groups:
            if outputs is not None:
                after = after + [outputs[2]]
            partial = shrink_rows(
                where, slot, hidden_states, away, group, tree_size, columns, cut, after
            )
            batch = (partial, lax.ppermute(partial, "tp", swap), [piece[0] for piece in group])
            outputs = finish(where, slot, batch, shared, outputs)
            slot += len(group)
    else:
        parts = [
            shrink_rows(where, slot, hidden_states, away, [piece], tree_size, columns, cut, [])
            for slot, piece in enumerate(arrivals)
        ]
        owners_here = lax.dynamic_index_in_dim(jnp.asarray(owners), me, 0, keepdims=False)
        hot = (adapter_ids[None, :] == owners_here[:, None]).astype(jnp.int32)
        slots = jnp.sum(hot * jnp.arange(pool_count, dtype=jnp.int32)[:, None], 0)
        partial = jnp.concatenate(parts, 0)[slots]
        expands = jnp.stack([piece[0][:, :columns] for piece in arrivals])[slots]
        every = jnp.arange(requests, dtype=jnp.int32)
        batch = (
            partial,
            lax.ppermute(partial, "tp", swap),
            [expands[r] for r in range(requests)],
        )
        outputs = finish((every[:1], every[None, :], every), 0, batch, shared, None)
    attention, cache_rows, _ = outputs
    tree_cache = (
        cache_rows.reshape(row_count, 2, heads_here, head_size)
        .transpose(0, 2, 1, 3)
        .reshape(row_count, heads_here, kv_width)
    )
    return attention, tree_cache


def solution(mesh):
    placed = (
        P(("grp", "pool"), "tp"),
        P("tp", None, None),
        P(("grp", "pool"), "tp", None),
        P(("grp", "pool"), None, None, None),
        P(("grp", "pool")),
        P(("grp", "pool")),
        P(("grp", "pool"), None),
        P(("grp", "pool"), "tp", None),
        P(("grp", "pool"), None, "tp", None),
        P(("grp", "pool"), None, "tp", None),
        P(),
    )
    return jax.shard_map(
        per_device,
        mesh=mesh,
        in_specs=placed,
        out_specs=(P(("grp", "pool"), "tp", None), P(("grp", "pool"), "tp", None)),
        check_vma=False,
    )
```

```python
import functools
import math

import jax
import jax.numpy as jnp
import numpy as np
from jax import lax
from jax.experimental import pallas as pl
from jax.experimental.pallas import tpu as pltpu
from jax.sharding import PartitionSpec as P

F32 = jnp.float32
BF16 = jnp.bfloat16


ANYWHERE = pl.BlockSpec(memory_space=pl.ANY)


def shapes_of(arrays):
    return [jax.ShapeDtypeStruct(array.shape, array.dtype) for array in arrays]


def ring_order(count):
    if count == 8:
        return list(range(0, count, 2)) + list(range(count - 1, 0, -2))
    return list(range(count))


def sorting_matrix(rows, columns, inner, source_inner):
    row = lax.broadcasted_iota(jnp.int32, (rows, columns), 0)
    column = lax.broadcasted_iota(jnp.int32, (rows, columns), 1)
    return (column == (row % inner) * source_inner + row // inner).astype(F32).astype(BF16)


def picking_matrix(wanted, inner, groups, first_head):
    row = lax.broadcasted_iota(jnp.int32, (wanted * inner, 256), 0)
    column = lax.broadcasted_iota(jnp.int32, (wanted * inner, 256), 1)
    group = row // inner
    source = (group % 2) * (groups // 2) + first_head + group // 2
    return (column == (row % inner) * groups + source).astype(F32).astype(BF16)


def request_at(where, slot):
    me_ref, owner_ref, adapter_ref = where
    owner = owner_ref[me_ref[0], slot]
    request = jnp.int32(0)
    for r in range(1, adapter_ref.shape[0]):
        request = jnp.where(adapter_ref[r] == owner, jnp.int32(r), request)
    return request


def hold(array, token):
    return pl.pallas_call(
        lambda array_ref, token_ref, output_ref: None,
        in_specs=[ANYWHERE, ANYWHERE],
        out_specs=ANYWHERE,
        out_shape=jax.ShapeDtypeStruct(array.shape, array.dtype),
        input_output_aliases={0: 0},
        compiler_params=pltpu.CompilerParams(vmem_limit_bytes=4 * 1024 * 1024),
        name="hold",
    )(array, token)


def pack_kernel(core_ref, shrink_ref, expand_ref, first_ref, second_ref, *, cut, heads_here):
    rank_size = shrink_ref.shape[0]
    groups = expand_ref.shape[0] // rank_size
    ranks = 256 // groups
    pick = picking_matrix(2 * heads_here, ranks, groups, core_ref[0] * heads_here)
    columns = 2 * heads_here * 128
    for block in range(rank_size // ranks):
        sorted_rows = jnp.dot(
            pick, expand_ref[256 * block : 256 * (block + 1), :], preferred_element_type=F32
        ).astype(BF16)
        for g in range(2 * heads_here):
            first_ref[ranks * block : ranks * (block + 1), 128 * g : 128 * (g + 1)] = sorted_rows[
                ranks * g : ranks * (g + 1), :
            ]
    first_ref[:, columns:] = shrink_ref[:, :cut]
    second_ref[...] = shrink_ref[:, cut:]


def pack(core, shrink, expand_rows, cut, heads_here):
    rank_size, half_width = shrink.shape
    columns = 2 * heads_here * 128
    return pl.pallas_call(
        functools.partial(pack_kernel, cut=cut, heads_here=heads_here),
        grid_spec=pltpu.PrefetchScalarGridSpec(
            num_scalar_prefetch=1,
            grid=(1,),
            in_specs=[
                pl.BlockSpec(shrink.shape, lambda i, c: (0, 0)),
                pl.BlockSpec(expand_rows.shape, lambda i, c: (0, 0)),
            ],
            out_specs=[
                pl.BlockSpec((rank_size, columns + cut), lambda i, c: (0, 0)),
                pl.BlockSpec((rank_size, half_width - cut), lambda i, c: (0, 0)),
            ],
        ),
        out_shape=[
            jax.ShapeDtypeStruct((rank_size, columns + cut), BF16),
            jax.ShapeDtypeStruct((rank_size, half_width - cut), BF16),
        ],
        compiler_params=pltpu.CompilerParams(vmem_limit_bytes=8 * 1024 * 1024),
        name="pack",
    )(core, shrink, expand_rows)


def base_kernel(core_ref, hidden_ref, weight_ref, *rest, held_count):
    total_ref, wide_ref = rest[-2:]
    here_ref, away_ref = rest[-2 - held_count - 2 : -2 - held_count]
    step = pl.program_id(0)
    depth = hidden_ref.shape[1]
    groups = weight_ref.shape[0] // depth
    heads = groups // 2
    wide_ref[...] = weight_ref[...].astype(F32)
    parts = []
    for head in range(heads):
        tiles = [
            wide_ref[pl.ds(tile * heads + head, depth, stride=groups), :].astype(BF16)
            for tile in range(2)
        ]
        parts.append(
            jnp.dot(hidden_ref[...], jnp.concatenate(tiles, 1), preferred_element_type=F32)
        )
    product = jnp.concatenate(parts, 1)

    @pl.when(step == 0)
    def _():
        total_ref[...] = product

    @pl.when(step > 0)
    def _():
        total_ref[...] += product

    @pl.when(step == pl.num_programs(0) - 1)
    def _():
        columns = here_ref.shape[1]

        @pl.when(core_ref[0] == 0)
        def _():
            here_ref[...] = total_ref[:, :columns]
            away_ref[...] = total_ref[:, columns:]

        @pl.when(core_ref[0] == 1)
        def _():
            here_ref[...] = total_ref[:, columns:]
            away_ref[...] = total_ref[:, :columns]


def base_product(core, hidden_states, weight_rows, width, after, held):
    rows, half_width = hidden_states.shape
    groups = weight_rows.shape[0] // half_width
    depth = half_width // 2
    return pl.pallas_call(
        functools.partial(base_kernel, held_count=len(held)),
        grid_spec=pltpu.PrefetchScalarGridSpec(
            num_scalar_prefetch=1,
            grid=(half_width // depth,),
            in_specs=[
                pl.BlockSpec((rows, depth), lambda i, c: (0, i)),
                pl.BlockSpec((depth * groups, 128), lambda i, c: (i, 0)),
            ]
            + [ANYWHERE] * (len(after) + len(held)),
            out_specs=[pl.BlockSpec((rows, width // 2), lambda i, c: (0, 0))] * 2
            + [ANYWHERE] * len(held),
            scratch_shapes=[
                pltpu.VMEM((rows, width), F32),
                pltpu.VMEM((depth * groups, 128), F32),
            ],
        ),
        out_shape=[jax.ShapeDtypeStruct((rows, width // 2), F32)] * 2 + shapes_of(held),
        input_output_aliases={3 + len(after) + k: 2 + k for k in range(len(held))},
        cost_estimate=pl.CostEstimate(
            flops=4_000_000_000, bytes_accessed=9_000_000, transcendentals=0
        ),
        compiler_params=pltpu.CompilerParams(vmem_limit_bytes=24 * 1024 * 1024),
        name="base",
    )(core, hidden_states, weight_rows, *after, *held)


def tree_kernel(length_ref, parent_ref, weight_ref, *rest, head_size, kv_heads):
    table_ref, moved_ref, semaphore = rest[-3:]
    move = pltpu.make_async_copy(weight_ref, moved_ref, semaphore)
    move.start()
    requests, nodes = parent_ref.shape
    node = lax.broadcasted_iota(jnp.int32, (nodes, nodes), 0)
    same = node == lax.broadcasted_iota(jnp.int32, (nodes, nodes), 1)
    spare = table_ref.shape[1] - 2 * head_size
    spread_node = lax.broadcasted_iota(jnp.int32, (nodes, spare), 0)
    spread_lane = lax.broadcasted_iota(jnp.int32, (nodes, spare), 1)
    spread = spread_lane == spread_node
    for g in range(1, kv_heads):
        spread = spread | (spread_lane == spread_node + nodes * g)
    spread = spread.astype(F32).astype(BF16)
    parents = parent_ref[...]
    below = [
        (same | (parents[r : r + 1, :] == node)).astype(F32).astype(BF16) for r in range(requests)
    ]
    reached = 1
    while reached < nodes:
        below = [
            jnp.minimum(jnp.dot(b, b, preferred_element_type=F32), 1.0).astype(BF16) for b in below
        ]
        reached = 2 * reached
    lane = lax.broadcasted_iota(jnp.int32, (nodes, head_size), 1)
    sign = jnp.where(lane < head_size // 2, -1.0, 1.0)
    power = lax.broadcasted_iota(jnp.int32, (1, head_size), 1) % (head_size // 2)
    frequency = jnp.exp(power.astype(F32) * (-2.0 * math.log(1000000.0) / head_size))
    ones = jnp.ones((nodes, head_size), BF16)
    for r in range(requests):
        b = below[r]
        depth = lax.dot_general(b, ones, (((0,), (0,)), ((), ())), preferred_element_type=F32)
        positions = length_ref[r].astype(F32) + depth - 1.0
        angles = positions * frequency
        rows = slice(nodes * r, nodes * (r + 1))
        wide = lax.dot_general(b, spread, (((0,), (0,)), ((), ())), preferred_element_type=F32)
        table_ref[rows, :] = jnp.concatenate(
            [jnp.cos(angles), jnp.sin(angles) * sign, jnp.where(wide > 0.5, 0.0, -1e30)], 1
        )
    move.wait()


def tree_tables(cache_lengths, tree_parents, head_size, kv_heads, weight_rows, after):
    requests, nodes = tree_parents.shape
    whole = lambda shape: pl.BlockSpec(shape, lambda i, n: (0,) * len(shape))
    rows = requests * nodes
    width = 2 * head_size + -(-kv_heads * nodes // 128) * 128
    return pl.pallas_call(
        functools.partial(tree_kernel, head_size=head_size, kv_heads=kv_heads),
        grid_spec=pltpu.PrefetchScalarGridSpec(
            num_scalar_prefetch=1,
            grid=(1,),
            in_specs=[whole(tree_parents.shape), ANYWHERE]
            + [ANYWHERE] * len(after),
            out_specs=[whole((rows, width)), ANYWHERE],
            scratch_shapes=[pltpu.SemaphoreType.DMA],
        ),
        out_shape=[jax.ShapeDtypeStruct((rows, width), F32)] + shapes_of([weight_rows]),
        cost_estimate=pl.CostEstimate(
            flops=1_000_000_000, bytes_accessed=8_000_000, transcendentals=0
        ),
        compiler_params=pltpu.CompilerParams(vmem_limit_bytes=8 * 1024 * 1024),
        name="tree",
    )(cache_lengths, tree_parents, weight_rows, *after)


def shrink_kernel(me_ref, owner_ref, adapter_ref, *refs, columns, cut):
    output_ref = refs[-1]
    contract = (((1,), (1,)), ((), ()))
    for b in range(output_ref.shape[0]):
        hidden_ref, away_ref, one_ref, two_ref = refs[4 * b : 4 * b + 4]
        output_ref[b, :, :columns] = away_ref[...]
        partial = lax.dot_general(
            hidden_ref[:, :cut], one_ref[:, columns:], contract, preferred_element_type=F32
        ) + lax.dot_general(hidden_ref[:, cut:], two_ref[...], contract, preferred_element_type=F32)
        output_ref[b, :, columns:] = jnp.concatenate([partial, jnp.zeros_like(partial)], 1)


def shrink_rows(where, slot, hidden_states, away, pieces, tree_size, columns, cut, after):
    rank_size = pieces[0][0].shape[0]
    in_specs, operands = [], []
    for b, (one, two) in enumerate(pieces):
        in_specs += [
            pl.BlockSpec(
                (tree_size, hidden_states.shape[1]),
                lambda i, *refs, b=b: (request_at(refs, slot + b), 0),
            ),
            pl.BlockSpec(
                (tree_size, columns), lambda i, *refs, b=b: (request_at(refs, slot + b), 0)
            ),
            pl.BlockSpec(one.shape, lambda i, *refs: (0, 0)),
            pl.BlockSpec(two.shape, lambda i, *refs: (0, 0)),
        ]
        operands += [hidden_states, away, one, two]
    count = len(pieces)
    width = columns + 2 * rank_size
    return pl.pallas_call(
        functools.partial(shrink_kernel, columns=columns, cut=cut),
        grid_spec=pltpu.PrefetchScalarGridSpec(
            num_scalar_prefetch=3,
            grid=(1,),
            in_specs=in_specs + [ANYWHERE] * len(after),
            out_specs=pl.BlockSpec((count, tree_size, width), lambda i, *refs: (0, 0, 0)),
        ),
        out_shape=jax.ShapeDtypeStruct((count, tree_size, width), F32),
        cost_estimate=pl.CostEstimate(
            flops=count * 30000000, bytes_accessed=count * 200000, transcendentals=0
        ),
        compiler_params=pltpu.CompilerParams(vmem_limit_bytes=14 * 1024 * 1024),
        name="shrink",
    )(*where, *operands, *after)


def finish_kernel(
    me_ref,
    owner_ref,
    adapter_ref,
    length_ref,
    here_ref,
    shrunk_here_ref,
    shrunk_there_ref,
    table_ref,
    gain_ref,
    query_ref,
    key_ref,
    value_ref,
    *rest,
    count,
    slot,
    kv_heads,
):
    expand_refs = rest[:count]
    attention_ref, cache_ref, token_ref, expand_ref = rest[-4:]
    token_ref[...] = jnp.zeros_like(token_ref)
    tree_size, heads, head_size = query_ref.shape
    cached = key_ref.shape[0]
    per_group = heads // kv_heads
    rows = tree_size * heads
    columns = kv_heads * 2 * head_size
    spare = table_ref.shape[1] - 2 * head_size
    score_scale = math.log2(math.e) / math.sqrt(head_size)
    if count == 1:
        expand = expand_refs[0][...]
    else:
        for b in range(count):

            @pl.when(pl.program_id(0) == b)
            def _():
                expand_ref[...] = expand_refs[b][...]

        expand = expand_ref[...]
    length = length_ref[request_at((me_ref, owner_ref, adapter_ref), slot + pl.program_id(0))]
    ranks = slice(columns, columns + expand.shape[0])
    shrunk = shrunk_here_ref[0, :, ranks] + shrunk_there_ref[0, :, ranks]
    high = shrunk.astype(BF16)
    left = shrunk - high.astype(F32)
    middle = left.astype(BF16)
    low = (left - middle.astype(F32)).astype(BF16)
    terms = jnp.dot(jnp.concatenate([low, middle, high], 0), expand, preferred_element_type=F32)
    delta = terms[:tree_size] + terms[tree_size : 2 * tree_size] + terms[2 * tree_size :]
    projected = (here_ref[...] + shrunk_there_ref[0, :, :columns]) + delta
    cosine = table_ref[:, :head_size]
    sine = table_ref[:, head_size : 2 * head_size]
    gain = gain_ref[...]
    new_keys, new_values = [], []
    for g in range(kv_heads):
        at = 2 * head_size * g
        key = projected[:, at : at + head_size]
        new_values.append(projected[:, at + head_size : at + 2 * head_size].astype(BF16))
        norm = lax.rsqrt(jnp.mean(key * key, -1, keepdims=True) + 1e-06)
        key = key * norm * gain
        new_keys.append((key * cosine + pltpu.roll(key, head_size // 2, 1) * sine).astype(BF16))
    pad = jnp.zeros((spare - kv_heads * tree_size, head_size), BF16)
    keys = jnp.concatenate([key_ref[...]] + new_keys + [pad], 0)
    values = jnp.concatenate([value_ref[...]] + new_values + [pad], 0)
    scores = lax.dot_general(
        query_ref[...].reshape(rows, head_size),
        keys,
        (((1,), (1,)), ((), ())),
        preferred_element_type=F32,
    ).reshape(tree_size, heads, cached + spare)
    lane = lax.broadcasted_iota(jnp.int32, (heads, cached), 1)
    mine = lax.broadcasted_iota(jnp.int32, (heads, cached), 0) // per_group
    allowed = (lane % kv_heads == mine) & (lane // kv_heads < length)
    cached_bias = jnp.where(allowed, 0.0, -1e30)
    lane = lax.broadcasted_iota(jnp.int32, (heads, spare), 1)
    first = lax.broadcasted_iota(jnp.int32, (heads, spare), 0) // per_group * tree_size
    head_bias = jnp.where((lane >= first) & (lane < first + tree_size), 0.0, -1e30)
    node_bias = table_ref[:, 2 * head_size :]
    cached_scores = scores[:, :, :cached] + cached_bias[None]
    tree_scores = scores[:, :, cached:] + (node_bias[:, None, :] + head_bias[None])
    top = jnp.maximum(
        jnp.max(cached_scores, -1, keepdims=True), jnp.max(tree_scores, -1, keepdims=True)
    )
    cached_exponent = jnp.exp2((cached_scores - top) * score_scale)
    tree_exponent = jnp.exp2((tree_scores - top) * score_scale)
    total = jnp.sum(cached_exponent, -1, keepdims=True) + jnp.sum(tree_exponent, -1, keepdims=True)
    exponent = jnp.concatenate([cached_exponent, tree_exponent], -1)
    output = jnp.dot(
        exponent.astype(BF16).reshape(rows, cached + spare), values, preferred_element_type=F32
    ).reshape(tree_size, heads, head_size)
    attention_ref[...] = (output * (1.0 / total)).astype(BF16)
    stacked = jnp.concatenate(new_keys + new_values, 0)
    size = stacked.shape[0]
    cache_ref[...] = jnp.dot(
        sorting_matrix(size, size, size // tree_size, tree_size),
        stacked,
        preferred_element_type=F32,
    ).astype(BF16)


def finish(where, slot, batch, shared, previous):
    shrunk_here, shrunk_there, pieces = batch
    lengths, gain, here, table, queries, key_rows, value_rows = shared
    spot = lambda i, refs: request_at(refs[:3], slot + i)
    count, tree_size, width = shrunk_here.shape
    rank_size = pieces[0].shape[0]
    requests = lengths.shape[0]
    rows, heads, head_size = queries.shape
    columns = here.shape[1]
    kv_heads = columns // (2 * head_size)
    row_block = lambda width: pl.BlockSpec((tree_size, width), lambda i, *refs: (spot(i, refs), 0))
    shrunk_block = pl.BlockSpec((1, tree_size, width), lambda i, *refs: (i, 0, 0))
    cached_block = pl.BlockSpec(
        (key_rows.shape[0] // requests, head_size), lambda i, *refs: (spot(i, refs), 0)
    )
    query_block = pl.BlockSpec(
        (tree_size, heads, head_size), lambda i, *refs: (spot(i, refs), 0, 0)
    )
    in_specs = [
        row_block(columns),
        shrunk_block,
        shrunk_block,
        row_block(table.shape[1]),
        pl.BlockSpec((1, head_size), lambda i, *refs: (0, 0)),
        query_block,
        cached_block,
        cached_block,
    ] + [pl.BlockSpec((rank_size, columns), lambda i, *refs: (0, 0))] * count
    operands = [*where, lengths, here, shrunk_here, shrunk_there, table, gain, queries]
    operands += [key_rows, value_rows, *pieces]
    aliases = {}
    if previous is not None:
        aliases = {len(operands): 0, len(operands) + 1: 1}
        operands += previous[:2]
        in_specs += [ANYWHERE] * 2
    cache_rows = 2 * kv_heads * tree_size
    return pl.pallas_call(
        functools.partial(finish_kernel, count=count, slot=slot, kv_heads=kv_heads),
        grid_spec=pltpu.PrefetchScalarGridSpec(
            num_scalar_prefetch=4,
            grid=(count,),
            in_specs=in_specs,
            out_specs=[
                query_block,
                pl.BlockSpec((cache_rows, head_size), lambda i, *refs: (spot(i, refs), 0)),
                pl.BlockSpec((8, 128), lambda i, *refs: (0, 0)),
            ],
            scratch_shapes=[pltpu.VMEM((rank_size, columns), BF16)],
        ),
        out_shape=[
            jax.ShapeDtypeStruct((rows, heads, head_size), BF16),
            jax.ShapeDtypeStruct((rows * 2 * kv_heads, head_size), BF16),
            jax.ShapeDtypeStruct((8, 128), F32),
        ],
        input_output_aliases=aliases,
        cost_estimate=pl.CostEstimate(
            flops=count * 90000000, bytes_accessed=count * 300000, transcendentals=0
        ),
        compiler_params=pltpu.CompilerParams(vmem_limit_bytes=16 * 1024 * 1024),
        name="finish",
    )(*operands)


def per_device(
    hidden_states,
    kv_weight,
    shrink_factors,
    expand_factors,
    adapter_ids,
    cache_lengths,
    tree_parents,
    queries,
    cache_keys,
    cache_values,
    key_gain,
):
    requests, tree_size = tree_parents.shape
    row_count, half_width = hidden_states.shape
    kv_heads, kv_width = (kv_weight.shape[1], kv_weight.shape[2])
    head_size = kv_width // 2
    rank_size = shrink_factors.shape[2]
    context = cache_keys.shape[1]
    pool_count = lax.axis_size("pool")
    heads_here = kv_heads // lax.axis_size("tp")
    columns = heads_here * kv_width
    me = lax.axis_index("pool")
    core = lax.axis_index("tp").astype(jnp.int32).reshape(1)
    swap = [(0, 1), (1, 0)]

    def tile_rows(array):
        lead, heads = array.shape[0], array.shape[1]
        return array.reshape(lead, heads, 2, 128).transpose(0, 2, 1, 3).reshape(-1, 128)

    cut = (half_width + columns) // 2 - columns
    first, second = pack(
        core, shrink_factors[0].T, tile_rows(expand_factors[0]), cut, heads_here
    )

    order = ring_order(pool_count)
    onward = [(order[i], order[(i + 1) % pool_count]) for i in range(pool_count)]
    backward = [(b, a) for a, b in onward]
    half = pool_count // 2
    offsets = [[0]] + [[-step, step] for step in range(1, half)] + [[half]]
    flat_offsets = sum(offsets, [])
    owners = np.zeros((pool_count, pool_count), np.int32)
    for spot, index in enumerate(order):
        owners[index] = [order[(spot + offset) % pool_count] for offset in flat_offsets]
    where = (me.astype(jnp.int32).reshape(1), jnp.asarray(owners), adapter_ids)

    weight_rows = tile_rows(kv_weight)
    key_rows = cache_keys.reshape(-1, head_size)
    value_rows = cache_values.reshape(-1, head_size)

    arrivals = [(first, second)]
    front = rear = (first, second)
    table, weight_rows = tree_tables(
        cache_lengths, tree_parents, head_size, heads_here, weight_rows, [first]
    )
    split_batches = pool_count == requests
    near = 3
    done = [(None, 0)]
    shared = None

    def finish_batch(group):
        outputs, slot = done[-1]
        after = [] if outputs is None else [outputs[2]]
        partial = shrink_rows(
            where, slot, hidden_states, away, group, tree_size, columns, cut, after
        )
        batch = (partial, lax.ppermute(partial, "tp", swap), [piece[0] for piece in group])
        done.append((finish(where, slot, batch, shared, outputs), slot + len(group)))

    for step in range(1, half):
        front = tuple(lax.ppermute(piece, "pool", onward) for piece in front)
        rear = tuple(lax.ppermute(piece, "pool", backward) for piece in rear)
        held = [front[1], rear[1]]
        if step == 1:
            here, away, *held = base_product(
                core, hidden_states, weight_rows, kv_heads * kv_width, [table], held
            )
            shared = (
                cache_lengths,
                key_gain.reshape(1, head_size),
                here,
                table,
                queries,
                key_rows,
                value_rows,
            )
        first_front = front[0]
        if step == 2 and split_batches:
            finish_batch(arrivals[:near])
            token = done[-1][0][2]
            first_front, held[1] = hold(first_front, token), hold(held[1], token)
        front, rear = (first_front, held[0]), (rear[0], held[1])
        arrivals += [front, rear]
    arrivals.append(
        (lax.ppermute(front[0], "pool", onward), lax.ppermute(rear[1], "pool", backward))
    )
    if split_batches:
        finish_batch(arrivals[near:-3])
        finish_batch(arrivals[-3:])
        outputs = done[-1][0]
    else:
        parts = [
            shrink_rows(where, slot, hidden_states, away, [piece], tree_size, columns, cut, [])
            for slot, piece in enumerate(arrivals)
        ]
        owners_here = lax.dynamic_index_in_dim(jnp.asarray(owners), me, 0, keepdims=False)
        hot = (adapter_ids[None, :] == owners_here[:, None]).astype(jnp.int32)
        slots = jnp.sum(hot * jnp.arange(pool_count, dtype=jnp.int32)[:, None], 0)
        partial = jnp.concatenate(parts, 0)[slots]
        expands = jnp.stack([piece[0][:, :columns] for piece in arrivals])[slots]
        every = jnp.arange(requests, dtype=jnp.int32)
        batch = (
            partial,
            lax.ppermute(partial, "tp", swap),
            [expands[r] for r in range(requests)],
        )
        outputs = finish((every[:1], every[None, :], every), 0, batch, shared, None)
    attention, cache_rows, _ = outputs
    tree_cache = (
        cache_rows.reshape(row_count, 2, heads_here, head_size)
        .transpose(0, 2, 1, 3)
        .reshape(row_count, heads_here, kv_width)
    )
    return attention, tree_cache


def solution(mesh):
    placed = (
        P(("grp", "pool"), "tp"),
        P("tp", None, None),
        P(("grp", "pool"), "tp", None),
        P(("grp", "pool"), None, None, None),
        P(("grp", "pool")),
        P(("grp", "pool")),
        P(("grp", "pool"), None),
        P(("grp", "pool"), "tp", None),
        P(("grp", "pool"), None, "tp", None),
        P(("grp", "pool"), None, "tp", None),
        P(),
    )
    return jax.shard_map(
        per_device,
        mesh=mesh,
        in_specs=placed,
        out_specs=(P(("grp", "pool"), "tp", None), P(("grp", "pool"), "tp", None)),
        check_vma=False,
    )
```

```python
import functools
import math

import jax
import jax.numpy as jnp
import numpy as np
from jax import lax
from jax.experimental import pallas as pl
from jax.experimental.pallas import tpu as pltpu
from jax.sharding import PartitionSpec as P

F32 = jnp.float32
BF16 = jnp.bfloat16


ANYWHERE = pl.BlockSpec(memory_space=pl.ANY)


def shapes_of(arrays):
    return [jax.ShapeDtypeStruct(array.shape, array.dtype) for array in arrays]


def ring_order(count):
    if count == 8:
        return list(range(0, count, 2)) + list(range(count - 1, 0, -2))
    return list(range(count))


def sorting_matrix(rows, columns, inner, source_inner):
    row = lax.broadcasted_iota(jnp.int32, (rows, columns), 0)
    column = lax.broadcasted_iota(jnp.int32, (rows, columns), 1)
    return (column == (row % inner) * source_inner + row // inner).astype(F32).astype(BF16)


def picking_matrix(wanted, inner, groups, first_head):
    row = lax.broadcasted_iota(jnp.int32, (wanted * inner, 256), 0)
    column = lax.broadcasted_iota(jnp.int32, (wanted * inner, 256), 1)
    group = row // inner
    source = (group % 2) * (groups // 2) + first_head + group // 2
    return (column == (row % inner) * groups + source).astype(F32).astype(BF16)


def request_at(where, slot):
    me_ref, owner_ref, adapter_ref = where
    owner = owner_ref[me_ref[0], slot]
    request = jnp.int32(0)
    for r in range(1, adapter_ref.shape[0]):
        request = jnp.where(adapter_ref[r] == owner, jnp.int32(r), request)
    return request


def hold(array, token):
    return pl.pallas_call(
        lambda array_ref, token_ref, output_ref: None,
        in_specs=[ANYWHERE, ANYWHERE],
        out_specs=ANYWHERE,
        out_shape=jax.ShapeDtypeStruct(array.shape, array.dtype),
        input_output_aliases={0: 0},
        compiler_params=pltpu.CompilerParams(vmem_limit_bytes=4 * 1024 * 1024),
        name="hold",
    )(array, token)


def pack_kernel(core_ref, shrink_ref, expand_ref, first_ref, second_ref, *, cut, heads_here):
    rank_size = shrink_ref.shape[0]
    groups = expand_ref.shape[0] // rank_size
    ranks = 256 // groups
    pick = picking_matrix(2 * heads_here, ranks, groups, core_ref[0] * heads_here)
    columns = 2 * heads_here * 128
    for block in range(rank_size // ranks):
        sorted_rows = jnp.dot(
            pick, expand_ref[256 * block : 256 * (block + 1), :], preferred_element_type=F32
        ).astype(BF16)
        for g in range(2 * heads_here):
            first_ref[ranks * block : ranks * (block + 1), 128 * g : 128 * (g + 1)] = sorted_rows[
                ranks * g : ranks * (g + 1), :
            ]
    first_ref[:, columns:] = shrink_ref[:, :cut]
    second_ref[...] = shrink_ref[:, cut:]


def pack(core, shrink, expand_rows, cut, heads_here):
    rank_size, half_width = shrink.shape
    columns = 2 * heads_here * 128
    return pl.pallas_call(
        functools.partial(pack_kernel, cut=cut, heads_here=heads_here),
        grid_spec=pltpu.PrefetchScalarGridSpec(
            num_scalar_prefetch=1,
            grid=(1,),
            in_specs=[
                pl.BlockSpec(shrink.shape, lambda i, c: (0, 0)),
                pl.BlockSpec(expand_rows.shape, lambda i, c: (0, 0)),
            ],
            out_specs=[
                pl.BlockSpec((rank_size, columns + cut), lambda i, c: (0, 0)),
                pl.BlockSpec((rank_size, half_width - cut), lambda i, c: (0, 0)),
            ],
        ),
        out_shape=[
            jax.ShapeDtypeStruct((rank_size, columns + cut), BF16),
            jax.ShapeDtypeStruct((rank_size, half_width - cut), BF16),
        ],
        compiler_params=pltpu.CompilerParams(vmem_limit_bytes=8 * 1024 * 1024),
        name="pack",
    )(core, shrink, expand_rows)


def base_kernel(core_ref, hidden_ref, weight_ref, *rest, held_count):
    total_ref, wide_ref = rest[-2:]
    here_ref, away_ref = rest[-2 - held_count - 2 : -2 - held_count]
    step = pl.program_id(0)
    depth = hidden_ref.shape[1]
    groups = weight_ref.shape[0] // depth
    heads = groups // 2
    wide_ref[...] = weight_ref[...].astype(F32)
    parts = []
    for head in range(heads):
        tiles = [
            wide_ref[pl.ds(tile * heads + head, depth, stride=groups), :].astype(BF16)
            for tile in range(2)
        ]
        parts.append(
            jnp.dot(hidden_ref[...], jnp.concatenate(tiles, 1), preferred_element_type=F32)
        )
    product = jnp.concatenate(parts, 1)

    @pl.when(step == 0)
    def _():
        total_ref[...] = product

    @pl.when(step > 0)
    def _():
        total_ref[...] += product

    @pl.when(step == pl.num_programs(0) - 1)
    def _():
        columns = here_ref.shape[1]

        @pl.when(core_ref[0] == 0)
        def _():
            here_ref[...] = total_ref[:, :columns]
            away_ref[...] = total_ref[:, columns:]

        @pl.when(core_ref[0] == 1)
        def _():
            here_ref[...] = total_ref[:, columns:]
            away_ref[...] = total_ref[:, :columns]


def base_product(core, hidden_states, weight_rows, width, after, held):
    rows, half_width = hidden_states.shape
    groups = weight_rows.shape[0] // half_width
    depth = half_width // 2
    return pl.pallas_call(
        functools.partial(base_kernel, held_count=len(held)),
        grid_spec=pltpu.PrefetchScalarGridSpec(
            num_scalar_prefetch=1,
            grid=(half_width // depth,),
            in_specs=[
                pl.BlockSpec((rows, depth), lambda i, c: (0, i)),
                pl.BlockSpec((depth * groups, 128), lambda i, c: (i, 0)),
            ]
            + [ANYWHERE] * (len(after) + len(held)),
            out_specs=[pl.BlockSpec((rows, width // 2), lambda i, c: (0, 0))] * 2
            + [ANYWHERE] * len(held),
            scratch_shapes=[
                pltpu.VMEM((rows, width), F32),
                pltpu.VMEM((depth * groups, 128), F32),
            ],
        ),
        out_shape=[jax.ShapeDtypeStruct((rows, width // 2), F32)] * 2 + shapes_of(held),
        input_output_aliases={3 + len(after) + k: 2 + k for k in range(len(held))},
        cost_estimate=pl.CostEstimate(
            flops=4_000_000_000, bytes_accessed=9_000_000, transcendentals=0
        ),
        compiler_params=pltpu.CompilerParams(vmem_limit_bytes=24 * 1024 * 1024),
        name="base",
    )(core, hidden_states, weight_rows, *after, *held)


def tree_kernel(length_ref, parent_ref, *rest, head_size, kv_heads):
    table_ref = rest[-1]
    requests, nodes = parent_ref.shape
    node = lax.broadcasted_iota(jnp.int32, (nodes, nodes), 0)
    same = node == lax.broadcasted_iota(jnp.int32, (nodes, nodes), 1)
    spare = table_ref.shape[1] - 2 * head_size
    spread_node = lax.broadcasted_iota(jnp.int32, (nodes, spare), 0)
    spread_lane = lax.broadcasted_iota(jnp.int32, (nodes, spare), 1)
    spread = spread_lane == spread_node
    for g in range(1, kv_heads):
        spread = spread | (spread_lane == spread_node + nodes * g)
    spread = spread.astype(F32).astype(BF16)
    parents = parent_ref[...]
    below = [
        (same | (parents[r : r + 1, :] == node)).astype(F32).astype(BF16) for r in range(requests)
    ]
    reached = 1
    while reached < nodes:
        below = [
            jnp.minimum(jnp.dot(b, b, preferred_element_type=F32), 1.0).astype(BF16) for b in below
        ]
        reached = 2 * reached
    lane = lax.broadcasted_iota(jnp.int32, (nodes, head_size), 1)
    sign = jnp.where(lane < head_size // 2, -1.0, 1.0)
    power = lax.broadcasted_iota(jnp.int32, (1, head_size), 1) % (head_size // 2)
    frequency = jnp.exp(power.astype(F32) * (-2.0 * math.log(1000000.0) / head_size))
    ones = jnp.ones((nodes, head_size), BF16)
    for r in range(requests):
        b = below[r]
        depth = lax.dot_general(b, ones, (((0,), (0,)), ((), ())), preferred_element_type=F32)
        positions = length_ref[r].astype(F32) + depth - 1.0
        angles = positions * frequency
        rows = slice(nodes * r, nodes * (r + 1))
        wide = lax.dot_general(b, spread, (((0,), (0,)), ((), ())), preferred_element_type=F32)
        table_ref[rows, :] = jnp.concatenate(
            [jnp.cos(angles), jnp.sin(angles) * sign, jnp.where(wide > 0.5, 0.0, -1e30)], 1
        )


def tree_tables(cache_lengths, tree_parents, head_size, kv_heads, after):
    requests, nodes = tree_parents.shape
    whole = lambda shape: pl.BlockSpec(shape, lambda i, n: (0,) * len(shape))
    rows = requests * nodes
    width = 2 * head_size + -(-kv_heads * nodes // 128) * 128
    return pl.pallas_call(
        functools.partial(tree_kernel, head_size=head_size, kv_heads=kv_heads),
        grid_spec=pltpu.PrefetchScalarGridSpec(
            num_scalar_prefetch=1,
            grid=(1,),
            in_specs=[whole(tree_parents.shape)]
            + [ANYWHERE] * len(after),
            out_specs=whole((rows, width)),
        ),
        out_shape=jax.ShapeDtypeStruct((rows, width), F32),
        cost_estimate=pl.CostEstimate(
            flops=1_000_000_000, bytes_accessed=8_000_000, transcendentals=0
        ),
        compiler_params=pltpu.CompilerParams(vmem_limit_bytes=8 * 1024 * 1024),
        name="tree",
    )(cache_lengths, tree_parents, *after)


def shrink_kernel(me_ref, owner_ref, adapter_ref, *refs, columns, cut):
    output_ref = refs[-1]
    contract = (((1,), (1,)), ((), ()))
    for b in range(output_ref.shape[0]):
        hidden_ref, away_ref, one_ref, two_ref = refs[4 * b : 4 * b + 4]
        output_ref[b, :, :columns] = away_ref[...]
        partial = lax.dot_general(
            hidden_ref[:, :cut], one_ref[:, columns:], contract, preferred_element_type=F32
        ) + lax.dot_general(hidden_ref[:, cut:], two_ref[...], contract, preferred_element_type=F32)
        output_ref[b, :, columns:] = jnp.concatenate([partial, jnp.zeros_like(partial)], 1)


def shrink_rows(where, slot, hidden_states, away, pieces, tree_size, columns, cut, after):
    rank_size = pieces[0][0].shape[0]
    in_specs, operands = [], []
    for b, (one, two) in enumerate(pieces):
        in_specs += [
            pl.BlockSpec(
                (tree_size, hidden_states.shape[1]),
                lambda i, *refs, b=b: (request_at(refs, slot + b), 0),
            ),
            pl.BlockSpec(
                (tree_size, columns), lambda i, *refs, b=b: (request_at(refs, slot + b), 0)
            ),
            pl.BlockSpec(one.shape, lambda i, *refs: (0, 0)),
            pl.BlockSpec(two.shape, lambda i, *refs: (0, 0)),
        ]
        operands += [hidden_states, away, one, two]
    count = len(pieces)
    width = columns + 2 * rank_size
    return pl.pallas_call(
        functools.partial(shrink_kernel, columns=columns, cut=cut),
        grid_spec=pltpu.PrefetchScalarGridSpec(
            num_scalar_prefetch=3,
            grid=(1,),
            in_specs=in_specs + [ANYWHERE] * len(after),
            out_specs=pl.BlockSpec((count, tree_size, width), lambda i, *refs: (0, 0, 0)),
        ),
        out_shape=jax.ShapeDtypeStruct((count, tree_size, width), F32),
        cost_estimate=pl.CostEstimate(
            flops=count * 30000000, bytes_accessed=count * 200000, transcendentals=0
        ),
        compiler_params=pltpu.CompilerParams(vmem_limit_bytes=14 * 1024 * 1024),
        name="shrink",
    )(*where, *operands, *after)


def finish_kernel(
    me_ref,
    owner_ref,
    adapter_ref,
    length_ref,
    here_ref,
    shrunk_here_ref,
    shrunk_there_ref,
    table_ref,
    gain_ref,
    query_ref,
    key_ref,
    value_ref,
    *rest,
    count,
    slot,
    kv_heads,
):
    expand_refs = rest[:count]
    attention_ref, cache_ref, token_ref, expand_ref = rest[-4:]
    token_ref[...] = jnp.zeros_like(token_ref)
    tree_size, heads, head_size = query_ref.shape
    cached = key_ref.shape[0]
    per_group = heads // kv_heads
    rows = tree_size * heads
    columns = kv_heads * 2 * head_size
    spare = table_ref.shape[1] - 2 * head_size
    score_scale = math.log2(math.e) / math.sqrt(head_size)
    if count == 1:
        expand = expand_refs[0][...]
    else:
        for b in range(count):

            @pl.when(pl.program_id(0) == b)
            def _():
                expand_ref[...] = expand_refs[b][...]

        expand = expand_ref[...]
    length = length_ref[request_at((me_ref, owner_ref, adapter_ref), slot + pl.program_id(0))]
    ranks = slice(columns, columns + expand.shape[0])
    shrunk = shrunk_here_ref[0, :, ranks] + shrunk_there_ref[0, :, ranks]
    high = shrunk.astype(BF16)
    left = shrunk - high.astype(F32)
    middle = left.astype(BF16)
    low = (left - middle.astype(F32)).astype(BF16)
    terms = jnp.dot(jnp.concatenate([low, middle, high], 0), expand, preferred_element_type=F32)
    delta = terms[:tree_size] + terms[tree_size : 2 * tree_size] + terms[2 * tree_size :]
    projected = (here_ref[...] + shrunk_there_ref[0, :, :columns]) + delta
    cosine = table_ref[:, :head_size]
    sine = table_ref[:, head_size : 2 * head_size]
    gain = gain_ref[...]
    new_keys, new_values = [], []
    for g in range(kv_heads):
        at = 2 * head_size * g
        key = projected[:, at : at + head_size]
        new_values.append(projected[:, at + head_size : at + 2 * head_size].astype(BF16))
        norm = lax.rsqrt(jnp.mean(key * key, -1, keepdims=True) + 1e-06)
        key = key * norm * gain
        new_keys.append((key * cosine + pltpu.roll(key, head_size // 2, 1) * sine).astype(BF16))
    pad = jnp.zeros((spare - kv_heads * tree_size, head_size), BF16)
    keys = jnp.concatenate([key_ref[...]] + new_keys + [pad], 0)
    values = jnp.concatenate([value_ref[...]] + new_values + [pad], 0)
    scores = lax.dot_general(
        query_ref[...].reshape(rows, head_size),
        keys,
        (((1,), (1,)), ((), ())),
        preferred_element_type=F32,
    ).reshape(tree_size, heads, cached + spare)
    lane = lax.broadcasted_iota(jnp.int32, (heads, cached), 1)
    mine = lax.broadcasted_iota(jnp.int32, (heads, cached), 0) // per_group
    allowed = (lane % kv_heads == mine) & (lane // kv_heads < length)
    cached_bias = jnp.where(allowed, 0.0, -1e30)
    lane = lax.broadcasted_iota(jnp.int32, (heads, spare), 1)
    first = lax.broadcasted_iota(jnp.int32, (heads, spare), 0) // per_group * tree_size
    head_bias = jnp.where((lane >= first) & (lane < first + tree_size), 0.0, -1e30)
    node_bias = table_ref[:, 2 * head_size :]
    cached_scores = scores[:, :, :cached] + cached_bias[None]
    tree_scores = scores[:, :, cached:] + (node_bias[:, None, :] + head_bias[None])
    top = jnp.maximum(
        jnp.max(cached_scores, -1, keepdims=True), jnp.max(tree_scores, -1, keepdims=True)
    )
    cached_exponent = jnp.exp2((cached_scores - top) * score_scale)
    tree_exponent = jnp.exp2((tree_scores - top) * score_scale)
    total = jnp.sum(cached_exponent, -1, keepdims=True) + jnp.sum(tree_exponent, -1, keepdims=True)
    exponent = jnp.concatenate([cached_exponent, tree_exponent], -1)
    output = jnp.dot(
        exponent.astype(BF16).reshape(rows, cached + spare), values, preferred_element_type=F32
    ).reshape(tree_size, heads, head_size)
    attention_ref[...] = (output * (1.0 / total)).astype(BF16)
    stacked = jnp.concatenate(new_keys + new_values, 0)
    size = stacked.shape[0]
    cache_ref[...] = jnp.dot(
        sorting_matrix(size, size, size // tree_size, tree_size),
        stacked,
        preferred_element_type=F32,
    ).astype(BF16)


def finish(where, slot, batch, shared, previous):
    shrunk_here, shrunk_there, pieces = batch
    lengths, gain, here, table, queries, key_rows, value_rows = shared
    spot = lambda i, refs: request_at(refs[:3], slot + i)
    count, tree_size, width = shrunk_here.shape
    rank_size = pieces[0].shape[0]
    requests = lengths.shape[0]
    rows, heads, head_size = queries.shape
    columns = here.shape[1]
    kv_heads = columns // (2 * head_size)
    row_block = lambda width: pl.BlockSpec((tree_size, width), lambda i, *refs: (spot(i, refs), 0))
    shrunk_block = pl.BlockSpec((1, tree_size, width), lambda i, *refs: (i, 0, 0))
    cached_block = pl.BlockSpec(
        (key_rows.shape[0] // requests, head_size), lambda i, *refs: (spot(i, refs), 0)
    )
    query_block = pl.BlockSpec(
        (tree_size, heads, head_size), lambda i, *refs: (spot(i, refs), 0, 0)
    )
    in_specs = [
        row_block(columns),
        shrunk_block,
        shrunk_block,
        row_block(table.shape[1]),
        pl.BlockSpec((1, head_size), lambda i, *refs: (0, 0)),
        query_block,
        cached_block,
        cached_block,
    ] + [pl.BlockSpec((rank_size, columns), lambda i, *refs: (0, 0))] * count
    operands = [*where, lengths, here, shrunk_here, shrunk_there, table, gain, queries]
    operands += [key_rows, value_rows, *pieces]
    aliases = {}
    if previous is not None:
        aliases = {len(operands): 0, len(operands) + 1: 1}
        operands += previous[:2]
        in_specs += [ANYWHERE] * 2
    cache_rows = 2 * kv_heads * tree_size
    return pl.pallas_call(
        functools.partial(finish_kernel, count=count, slot=slot, kv_heads=kv_heads),
        grid_spec=pltpu.PrefetchScalarGridSpec(
            num_scalar_prefetch=4,
            grid=(count,),
            in_specs=in_specs,
            out_specs=[
                query_block,
                pl.BlockSpec((cache_rows, head_size), lambda i, *refs: (spot(i, refs), 0)),
                pl.BlockSpec((8, 128), lambda i, *refs: (0, 0)),
            ],
            scratch_shapes=[pltpu.VMEM((rank_size, columns), BF16)],
        ),
        out_shape=[
            jax.ShapeDtypeStruct((rows, heads, head_size), BF16),
            jax.ShapeDtypeStruct((rows * 2 * kv_heads, head_size), BF16),
            jax.ShapeDtypeStruct((8, 128), F32),
        ],
        input_output_aliases=aliases,
        cost_estimate=pl.CostEstimate(
            flops=count * 90000000, bytes_accessed=count * 300000, transcendentals=0
        ),
        compiler_params=pltpu.CompilerParams(vmem_limit_bytes=16 * 1024 * 1024),
        name="finish",
    )(*operands)


def per_device(
    hidden_states,
    kv_weight,
    shrink_factors,
    expand_factors,
    adapter_ids,
    cache_lengths,
    tree_parents,
    queries,
    cache_keys,
    cache_values,
    key_gain,
):
    requests, tree_size = tree_parents.shape
    row_count, half_width = hidden_states.shape
    kv_heads, kv_width = (kv_weight.shape[1], kv_weight.shape[2])
    head_size = kv_width // 2
    rank_size = shrink_factors.shape[2]
    context = cache_keys.shape[1]
    pool_count = lax.axis_size("pool")
    heads_here = kv_heads // lax.axis_size("tp")
    columns = heads_here * kv_width
    me = lax.axis_index("pool")
    core = lax.axis_index("tp").astype(jnp.int32).reshape(1)
    swap = [(0, 1), (1, 0)]

    def tile_rows(array):
        lead, heads = array.shape[0], array.shape[1]
        return array.reshape(lead, heads, 2, 128).transpose(0, 2, 1, 3).reshape(-1, 128)

    cut = (half_width + columns) // 2 - columns
    first, second = pack(
        core, shrink_factors[0].T, tile_rows(expand_factors[0]), cut, heads_here
    )

    order = ring_order(pool_count)
    onward = [(order[i], order[(i + 1) % pool_count]) for i in range(pool_count)]
    backward = [(b, a) for a, b in onward]
    half = pool_count // 2
    offsets = [[0]] + [[-step, step] for step in range(1, half)] + [[half]]
    flat_offsets = sum(offsets, [])
    owners = np.zeros((pool_count, pool_count), np.int32)
    for spot, index in enumerate(order):
        owners[index] = [order[(spot + offset) % pool_count] for offset in flat_offsets]
    where = (me.astype(jnp.int32).reshape(1), jnp.asarray(owners), adapter_ids)

    weight_rows = tile_rows(kv_weight)
    key_rows = cache_keys.reshape(-1, head_size)
    value_rows = cache_values.reshape(-1, head_size)

    arrivals = [(first, second)]
    front = rear = (first, second)
    here, away = base_product(
        core, hidden_states, weight_rows, kv_heads * kv_width, [first], []
    )
    split_batches = pool_count == requests
    near = 3
    done = [(None, 0)]
    shared = None

    def finish_batch(group, after=()):
        outputs, slot = done[-1]
        after = list(after) if outputs is None else [outputs[2]]
        partial = shrink_rows(
            where, slot, hidden_states, away, group, tree_size, columns, cut, after
        )
        batch = (partial, lax.ppermute(partial, "tp", swap), [piece[0] for piece in group])
        done.append((finish(where, slot, batch, shared, outputs), slot + len(group)))

    for step in range(1, half):
        front = tuple(lax.ppermute(piece, "pool", onward) for piece in front)
        rear = tuple(lax.ppermute(piece, "pool", backward) for piece in rear)
        held = [front[1], rear[1]]
        first_front = front[0]
        if step == 1:
            held = [hold(piece, away) for piece in held]
            table = tree_tables(
                cache_lengths, tree_parents, head_size, heads_here, [here, front[0], rear[0]]
            )
            first_front = hold(first_front, table)
            shared = (
                cache_lengths,
                key_gain.reshape(1, head_size),
                here,
                table,
                queries,
                key_rows,
                value_rows,
            )
        if step == 2 and split_batches:
            finish_batch(arrivals[:near], held)
            token = done[-1][0][2]
            first_front, held[1] = hold(first_front, token), hold(held[1], token)
        front, rear = (first_front, held[0]), (rear[0], held[1])
        arrivals += [front, rear]
    arrivals.append(
        (lax.ppermute(front[0], "pool", onward), lax.ppermute(rear[1], "pool", backward))
    )
    if split_batches:
        finish_batch(arrivals[near:-3])
        finish_batch(arrivals[-3:])
        outputs = done[-1][0]
    else:
        parts = [
            shrink_rows(where, slot, hidden_states, away, [piece], tree_size, columns, cut, [])
            for slot, piece in enumerate(arrivals)
        ]
        owners_here = lax.dynamic_index_in_dim(jnp.asarray(owners), me, 0, keepdims=False)
        hot = (adapter_ids[None, :] == owners_here[:, None]).astype(jnp.int32)
        slots = jnp.sum(hot * jnp.arange(pool_count, dtype=jnp.int32)[:, None], 0)
        partial = jnp.concatenate(parts, 0)[slots]
        expands = jnp.stack([piece[0][:, :columns] for piece in arrivals])[slots]
        every = jnp.arange(requests, dtype=jnp.int32)
        batch = (
            partial,
            lax.ppermute(partial, "tp", swap),
            [expands[r] for r in range(requests)],
        )
        outputs = finish((every[:1], every[None, :], every), 0, batch, shared, None)
    attention, cache_rows, _ = outputs
    tree_cache = (
        cache_rows.reshape(row_count, 2, heads_here, head_size)
        .transpose(0, 2, 1, 3)
        .reshape(row_count, heads_here, kv_width)
    )
    return attention, tree_cache


def solution(mesh):
    placed = (
        P(("grp", "pool"), "tp"),
        P("tp", None, None),
        P(("grp", "pool"), "tp", None),
        P(("grp", "pool"), None, None, None),
        P(("grp", "pool")),
        P(("grp", "pool")),
        P(("grp", "pool"), None),
        P(("grp", "pool"), "tp", None),
        P(("grp", "pool"), None, "tp", None),
        P(("grp", "pool"), None, "tp", None),
        P(),
    )
    return jax.shard_map(
        per_device,
        mesh=mesh,
        in_specs=placed,
        out_specs=(P(("grp", "pool"), "tp", None), P(("grp", "pool"), "tp", None)),
        check_vma=False,
    )
```

```python
import functools
import math

import jax
import jax.numpy as jnp
import numpy as np
from jax import lax
from jax.experimental import pallas as pl
from jax.experimental.pallas import tpu as pltpu
from jax.sharding import PartitionSpec as P

F32 = jnp.float32
BF16 = jnp.bfloat16


ANYWHERE = pl.BlockSpec(memory_space=pl.ANY)


def shapes_of(arrays):
    return [jax.ShapeDtypeStruct(array.shape, array.dtype) for array in arrays]


def ring_order(count):
    if count == 8:
        return list(range(0, count, 2)) + list(range(count - 1, 0, -2))
    return list(range(count))


def sorting_matrix(rows, columns, inner, source_inner):
    row = lax.broadcasted_iota(jnp.int32, (rows, columns), 0)
    column = lax.broadcasted_iota(jnp.int32, (rows, columns), 1)
    return (column == (row % inner) * source_inner + row // inner).astype(F32).astype(BF16)


def picking_matrix(wanted, inner, groups, first_head):
    row = lax.broadcasted_iota(jnp.int32, (wanted * inner, 256), 0)
    column = lax.broadcasted_iota(jnp.int32, (wanted * inner, 256), 1)
    group = row // inner
    source = (group % 2) * (groups // 2) + first_head + group // 2
    return (column == (row % inner) * groups + source).astype(F32).astype(BF16)


def request_at(where, slot):
    me_ref, owner_ref, adapter_ref = where
    owner = owner_ref[me_ref[0], slot]
    request = jnp.int32(0)
    for r in range(1, adapter_ref.shape[0]):
        request = jnp.where(adapter_ref[r] == owner, jnp.int32(r), request)
    return request


def hold(array, token):
    return pl.pallas_call(
        lambda array_ref, token_ref, output_ref: None,
        in_specs=[ANYWHERE, ANYWHERE],
        out_specs=ANYWHERE,
        out_shape=jax.ShapeDtypeStruct(array.shape, array.dtype),
        input_output_aliases={0: 0},
        compiler_params=pltpu.CompilerParams(vmem_limit_bytes=4 * 1024 * 1024),
        name="hold",
    )(array, token)


def pack_kernel(core_ref, shrink_ref, expand_ref, first_ref, second_ref, *, cut, heads_here):
    rank_size = shrink_ref.shape[0]
    groups = expand_ref.shape[0] // rank_size
    ranks = 256 // groups
    pick = picking_matrix(2 * heads_here, ranks, groups, core_ref[0] * heads_here)
    columns = 2 * heads_here * 128
    for block in range(rank_size // ranks):
        sorted_rows = jnp.dot(
            pick, expand_ref[256 * block : 256 * (block + 1), :], preferred_element_type=F32
        ).astype(BF16)
        for g in range(2 * heads_here):
            first_ref[ranks * block : ranks * (block + 1), 128 * g : 128 * (g + 1)] = sorted_rows[
                ranks * g : ranks * (g + 1), :
            ]
    first_ref[:, columns:] = shrink_ref[:, :cut]
    second_ref[...] = shrink_ref[:, cut:]


def pack(core, shrink, expand_rows, cut, heads_here):
    rank_size, half_width = shrink.shape
    columns = 2 * heads_here * 128
    return pl.pallas_call(
        functools.partial(pack_kernel, cut=cut, heads_here=heads_here),
        grid_spec=pltpu.PrefetchScalarGridSpec(
            num_scalar_prefetch=1,
            grid=(1,),
            in_specs=[
                pl.BlockSpec(shrink.shape, lambda i, c: (0, 0)),
                pl.BlockSpec(expand_rows.shape, lambda i, c: (0, 0)),
            ],
            out_specs=[
                pl.BlockSpec((rank_size, columns + cut), lambda i, c: (0, 0)),
                pl.BlockSpec((rank_size, half_width - cut), lambda i, c: (0, 0)),
            ],
        ),
        out_shape=[
            jax.ShapeDtypeStruct((rank_size, columns + cut), BF16),
            jax.ShapeDtypeStruct((rank_size, half_width - cut), BF16),
        ],
        compiler_params=pltpu.CompilerParams(vmem_limit_bytes=8 * 1024 * 1024),
        name="pack",
    )(core, shrink, expand_rows)


def base_kernel(core_ref, hidden_ref, weight_ref, *rest, held_count):
    total_ref, wide_ref = rest[-2:]
    here_ref, away_ref = rest[-2 - held_count - 2 : -2 - held_count]
    step = pl.program_id(0)
    depth = hidden_ref.shape[1]
    groups = weight_ref.shape[0] // depth
    heads = groups // 2
    wide_ref[...] = weight_ref[...].astype(F32)
    parts = []
    for head in range(heads):
        tiles = [
            wide_ref[pl.ds(tile * heads + head, depth, stride=groups), :].astype(BF16)
            for tile in range(2)
        ]
        parts.append(
            jnp.dot(hidden_ref[...], jnp.concatenate(tiles, 1), preferred_element_type=F32)
        )
    product = jnp.concatenate(parts, 1)

    @pl.when(step == 0)
    def _():
        total_ref[...] = product

    @pl.when(step > 0)
    def _():
        total_ref[...] += product

    @pl.when(step == pl.num_programs(0) - 1)
    def _():
        columns = here_ref.shape[1]

        @pl.when(core_ref[0] == 0)
        def _():
            here_ref[...] = total_ref[:, :columns]
            away_ref[...] = total_ref[:, columns:]

        @pl.when(core_ref[0] == 1)
        def _():
            here_ref[...] = total_ref[:, columns:]
            away_ref[...] = total_ref[:, :columns]


def base_product(core, hidden_states, weight_rows, width, after, held):
    rows, half_width = hidden_states.shape
    groups = weight_rows.shape[0] // half_width
    depth = half_width // 2
    return pl.pallas_call(
        functools.partial(base_kernel, held_count=len(held)),
        grid_spec=pltpu.PrefetchScalarGridSpec(
            num_scalar_prefetch=1,
            grid=(half_width // depth,),
            in_specs=[
                pl.BlockSpec((rows, depth), lambda i, c: (0, i)),
                pl.BlockSpec((depth * groups, 128), lambda i, c: (i, 0)),
            ]
            + [ANYWHERE] * (len(after) + len(held)),
            out_specs=[pl.BlockSpec((rows, width // 2), lambda i, c: (0, 0))] * 2
            + [ANYWHERE] * len(held),
            scratch_shapes=[
                pltpu.VMEM((rows, width), F32),
                pltpu.VMEM((depth * groups, 128), F32),
            ],
        ),
        out_shape=[jax.ShapeDtypeStruct((rows, width // 2), F32)] * 2 + shapes_of(held),
        input_output_aliases={3 + len(after) + k: 2 + k for k in range(len(held))},
        cost_estimate=pl.CostEstimate(
            flops=4_000_000_000, bytes_accessed=9_000_000, transcendentals=0
        ),
        compiler_params=pltpu.CompilerParams(vmem_limit_bytes=24 * 1024 * 1024),
        name="base",
    )(core, hidden_states, weight_rows, *after, *held)


def tree_kernel(length_ref, parent_ref, *rest, head_size, kv_heads):
    table_ref = rest[-1]
    requests, nodes = parent_ref.shape
    node = lax.broadcasted_iota(jnp.int32, (nodes, nodes), 0)
    same = node == lax.broadcasted_iota(jnp.int32, (nodes, nodes), 1)
    spare = table_ref.shape[1] - 2 * head_size
    spread_node = lax.broadcasted_iota(jnp.int32, (nodes, spare), 0)
    spread_lane = lax.broadcasted_iota(jnp.int32, (nodes, spare), 1)
    spread = spread_lane == spread_node
    for g in range(1, kv_heads):
        spread = spread | (spread_lane == spread_node + nodes * g)
    spread = spread.astype(F32).astype(BF16)
    parents = parent_ref[...]
    below = [
        (same | (parents[r : r + 1, :] == node)).astype(F32).astype(BF16) for r in range(requests)
    ]
    reached = 1
    while reached < nodes:
        below = [
            jnp.minimum(jnp.dot(b, b, preferred_element_type=F32), 1.0).astype(BF16) for b in below
        ]
        reached = 2 * reached
    lane = lax.broadcasted_iota(jnp.int32, (nodes, head_size), 1)
    sign = jnp.where(lane < head_size // 2, -1.0, 1.0)
    power = lax.broadcasted_iota(jnp.int32, (1, head_size), 1) % (head_size // 2)
    frequency = jnp.exp(power.astype(F32) * (-2.0 * math.log(1000000.0) / head_size))
    ones = jnp.ones((nodes, head_size), BF16)
    for r in range(requests):
        b = below[r]
        depth = lax.dot_general(b, ones, (((0,), (0,)), ((), ())), preferred_element_type=F32)
        positions = length_ref[r].astype(F32) + depth - 1.0
        angles = positions * frequency
        rows = slice(nodes * r, nodes * (r + 1))
        wide = lax.dot_general(b, spread, (((0,), (0,)), ((), ())), preferred_element_type=F32)
        table_ref[rows, :] = jnp.concatenate(
            [jnp.cos(angles), jnp.sin(angles) * sign, jnp.where(wide > 0.5, 0.0, -1e30)], 1
        )


def tree_tables(cache_lengths, tree_parents, head_size, kv_heads, after):
    requests, nodes = tree_parents.shape
    whole = lambda shape: pl.BlockSpec(shape, lambda i, n: (0,) * len(shape))
    rows = requests * nodes
    width = 2 * head_size + -(-kv_heads * nodes // 128) * 128
    return pl.pallas_call(
        functools.partial(tree_kernel, head_size=head_size, kv_heads=kv_heads),
        grid_spec=pltpu.PrefetchScalarGridSpec(
            num_scalar_prefetch=1,
            grid=(1,),
            in_specs=[whole(tree_parents.shape)]
            + [ANYWHERE] * len(after),
            out_specs=whole((rows, width)),
        ),
        out_shape=jax.ShapeDtypeStruct((rows, width), F32),
        cost_estimate=pl.CostEstimate(
            flops=1_000_000_000, bytes_accessed=8_000_000, transcendentals=0
        ),
        compiler_params=pltpu.CompilerParams(vmem_limit_bytes=8 * 1024 * 1024),
        name="tree",
    )(cache_lengths, tree_parents, *after)


def shrink_kernel(me_ref, owner_ref, adapter_ref, *refs, columns, cut):
    output_ref = refs[-1]
    contract = (((1,), (1,)), ((), ()))
    for b in range(output_ref.shape[0]):
        hidden_ref, away_ref, one_ref, two_ref = refs[4 * b : 4 * b + 4]
        output_ref[b, :, :columns] = away_ref[...]
        partial = lax.dot_general(
            hidden_ref[:, :cut], one_ref[:, columns:], contract, preferred_element_type=F32
        ) + lax.dot_general(hidden_ref[:, cut:], two_ref[...], contract, preferred_element_type=F32)
        output_ref[b, :, columns:] = jnp.concatenate([partial, jnp.zeros_like(partial)], 1)


def shrink_rows(where, slot, hidden_states, away, pieces, tree_size, columns, cut, after):
    rank_size = pieces[0][0].shape[0]
    in_specs, operands = [], []
    for b, (one, two) in enumerate(pieces):
        in_specs += [
            pl.BlockSpec(
                (tree_size, hidden_states.shape[1]),
                lambda i, *refs, b=b: (request_at(refs, slot + b), 0),
            ),
            pl.BlockSpec(
                (tree_size, columns), lambda i, *refs, b=b: (request_at(refs, slot + b), 0)
            ),
            pl.BlockSpec(one.shape, lambda i, *refs: (0, 0)),
            pl.BlockSpec(two.shape, lambda i, *refs: (0, 0)),
        ]
        operands += [hidden_states, away, one, two]
    count = len(pieces)
    width = columns + 2 * rank_size
    return pl.pallas_call(
        functools.partial(shrink_kernel, columns=columns, cut=cut),
        grid_spec=pltpu.PrefetchScalarGridSpec(
            num_scalar_prefetch=3,
            grid=(1,),
            in_specs=in_specs + [ANYWHERE] * len(after),
            out_specs=pl.BlockSpec((count, tree_size, width), lambda i, *refs: (0, 0, 0)),
        ),
        out_shape=jax.ShapeDtypeStruct((count, tree_size, width), F32),
        cost_estimate=pl.CostEstimate(
            flops=count * 30000000, bytes_accessed=count * 200000, transcendentals=0
        ),
        compiler_params=pltpu.CompilerParams(vmem_limit_bytes=14 * 1024 * 1024),
        name="shrink",
    )(*where, *operands, *after)


def finish_kernel(
    me_ref,
    owner_ref,
    adapter_ref,
    length_ref,
    here_ref,
    shrunk_here_ref,
    shrunk_there_ref,
    table_ref,
    gain_ref,
    query_ref,
    key_ref,
    value_ref,
    *rest,
    count,
    slot,
    kv_heads,
):
    expand_refs = rest[:count]
    attention_ref, cache_ref, token_ref, expand_ref = rest[-4:]
    token_ref[...] = jnp.zeros_like(token_ref)
    tree_size, heads, head_size = query_ref.shape
    cached = key_ref.shape[0]
    per_group = heads // kv_heads
    rows = tree_size * heads
    columns = kv_heads * 2 * head_size
    spare = table_ref.shape[1] - 2 * head_size
    score_scale = math.log2(math.e) / math.sqrt(head_size)
    if count == 1:
        expand = expand_refs[0][...]
    else:
        for b in range(count):

            @pl.when(pl.program_id(0) == b)
            def _():
                expand_ref[...] = expand_refs[b][...]

        expand = expand_ref[...]
    length = length_ref[request_at((me_ref, owner_ref, adapter_ref), slot + pl.program_id(0))]
    ranks = slice(columns, columns + expand.shape[0])
    shrunk = shrunk_here_ref[0, :, ranks] + shrunk_there_ref[0, :, ranks]
    high = shrunk.astype(BF16)
    left = shrunk - high.astype(F32)
    middle = left.astype(BF16)
    low = (left - middle.astype(F32)).astype(BF16)
    terms = jnp.dot(jnp.concatenate([low, middle, high], 0), expand, preferred_element_type=F32)
    delta = terms[:tree_size] + terms[tree_size : 2 * tree_size] + terms[2 * tree_size :]
    projected = (here_ref[...] + shrunk_there_ref[0, :, :columns]) + delta
    cosine = table_ref[:, :head_size]
    sine = table_ref[:, head_size : 2 * head_size]
    gain = gain_ref[...]
    new_keys, new_values = [], []
    for g in range(kv_heads):
        at = 2 * head_size * g
        key = projected[:, at : at + head_size]
        new_values.append(projected[:, at + head_size : at + 2 * head_size].astype(BF16))
        norm = lax.rsqrt(jnp.mean(key * key, -1, keepdims=True) + 1e-06)
        key = key * norm * gain
        new_keys.append((key * cosine + pltpu.roll(key, head_size // 2, 1) * sine).astype(BF16))
    pad = jnp.zeros((spare - kv_heads * tree_size, head_size), BF16)
    keys = jnp.concatenate([key_ref[...]] + new_keys + [pad], 0)
    values = jnp.concatenate([value_ref[...]] + new_values + [pad], 0)
    scores = lax.dot_general(
        query_ref[...].reshape(rows, head_size),
        keys,
        (((1,), (1,)), ((), ())),
        preferred_element_type=F32,
    ).reshape(tree_size, heads, cached + spare)
    lane = lax.broadcasted_iota(jnp.int32, (heads, cached), 1)
    mine = lax.broadcasted_iota(jnp.int32, (heads, cached), 0) // per_group
    allowed = (lane % kv_heads == mine) & (lane // kv_heads < length)
    cached_bias = jnp.where(allowed, 0.0, -1e30)
    lane = lax.broadcasted_iota(jnp.int32, (heads, spare), 1)
    first = lax.broadcasted_iota(jnp.int32, (heads, spare), 0) // per_group * tree_size
    head_bias = jnp.where((lane >= first) & (lane < first + tree_size), 0.0, -1e30)
    node_bias = table_ref[:, 2 * head_size :]
    cached_scores = scores[:, :, :cached] + cached_bias[None]
    tree_scores = scores[:, :, cached:] + (node_bias[:, None, :] + head_bias[None])
    top = jnp.maximum(
        jnp.max(cached_scores, -1, keepdims=True), jnp.max(tree_scores, -1, keepdims=True)
    )
    cached_exponent = jnp.exp2((cached_scores - top) * score_scale)
    tree_exponent = jnp.exp2((tree_scores - top) * score_scale)
    total = jnp.sum(cached_exponent, -1, keepdims=True) + jnp.sum(tree_exponent, -1, keepdims=True)
    exponent = jnp.concatenate([cached_exponent, tree_exponent], -1)
    output = jnp.dot(
        exponent.astype(BF16).reshape(rows, cached + spare), values, preferred_element_type=F32
    ).reshape(tree_size, heads, head_size)
    attention_ref[...] = (output * (1.0 / total)).astype(BF16)
    stacked = jnp.concatenate(new_keys + new_values, 0)
    size = stacked.shape[0]
    cache_ref[...] = jnp.dot(
        sorting_matrix(size, size, size // tree_size, tree_size),
        stacked,
        preferred_element_type=F32,
    ).astype(BF16)


def finish(where, slot, batch, shared, previous):
    shrunk_here, shrunk_there, pieces = batch
    lengths, gain, here, table, queries, key_rows, value_rows = shared
    spot = lambda i, refs: request_at(refs[:3], slot + i)
    count, tree_size, width = shrunk_here.shape
    rank_size = pieces[0].shape[0]
    requests = lengths.shape[0]
    rows, heads, head_size = queries.shape
    columns = here.shape[1]
    kv_heads = columns // (2 * head_size)
    row_block = lambda width: pl.BlockSpec((tree_size, width), lambda i, *refs: (spot(i, refs), 0))
    shrunk_block = pl.BlockSpec((1, tree_size, width), lambda i, *refs: (i, 0, 0))
    cached_block = pl.BlockSpec(
        (key_rows.shape[0] // requests, head_size), lambda i, *refs: (spot(i, refs), 0)
    )
    query_block = pl.BlockSpec(
        (tree_size, heads, head_size), lambda i, *refs: (spot(i, refs), 0, 0)
    )
    in_specs = [
        row_block(columns),
        shrunk_block,
        shrunk_block,
        row_block(table.shape[1]),
        pl.BlockSpec((1, head_size), lambda i, *refs: (0, 0)),
        query_block,
        cached_block,
        cached_block,
    ] + [pl.BlockSpec((rank_size, columns), lambda i, *refs: (0, 0))] * count
    operands = [*where, lengths, here, shrunk_here, shrunk_there, table, gain, queries]
    operands += [key_rows, value_rows, *pieces]
    aliases = {}
    if previous is not None:
        aliases = {len(operands): 0, len(operands) + 1: 1}
        operands += previous[:2]
        in_specs += [ANYWHERE] * 2
    cache_rows = 2 * kv_heads * tree_size
    return pl.pallas_call(
        functools.partial(finish_kernel, count=count, slot=slot, kv_heads=kv_heads),
        grid_spec=pltpu.PrefetchScalarGridSpec(
            num_scalar_prefetch=4,
            grid=(count,),
            in_specs=in_specs,
            out_specs=[
                query_block,
                pl.BlockSpec((cache_rows, head_size), lambda i, *refs: (spot(i, refs), 0)),
                pl.BlockSpec((8, 128), lambda i, *refs: (0, 0)),
            ],
            scratch_shapes=[pltpu.VMEM((rank_size, columns), BF16)],
        ),
        out_shape=[
            jax.ShapeDtypeStruct((rows, heads, head_size), BF16),
            jax.ShapeDtypeStruct((rows * 2 * kv_heads, head_size), BF16),
            jax.ShapeDtypeStruct((8, 128), F32),
        ],
        input_output_aliases=aliases,
        cost_estimate=pl.CostEstimate(
            flops=count * 90000000, bytes_accessed=count * 300000, transcendentals=0
        ),
        compiler_params=pltpu.CompilerParams(vmem_limit_bytes=16 * 1024 * 1024),
        name="finish",
    )(*operands)


def per_device(
    hidden_states,
    kv_weight,
    shrink_factors,
    expand_factors,
    adapter_ids,
    cache_lengths,
    tree_parents,
    queries,
    cache_keys,
    cache_values,
    key_gain,
):
    requests, tree_size = tree_parents.shape
    row_count, half_width = hidden_states.shape
    kv_heads, kv_width = (kv_weight.shape[1], kv_weight.shape[2])
    head_size = kv_width // 2
    rank_size = shrink_factors.shape[2]
    context = cache_keys.shape[1]
    pool_count = lax.axis_size("pool")
    heads_here = kv_heads // lax.axis_size("tp")
    columns = heads_here * kv_width
    me = lax.axis_index("pool")
    core = lax.axis_index("tp").astype(jnp.int32).reshape(1)
    swap = [(0, 1), (1, 0)]

    def tile_rows(array):
        lead, heads = array.shape[0], array.shape[1]
        return array.reshape(lead, heads, 2, 128).transpose(0, 2, 1, 3).reshape(-1, 128)

    cut = (half_width + columns) // 2 - columns
    first, second = pack(
        core, shrink_factors[0].T, tile_rows(expand_factors[0]), cut, heads_here
    )

    order = ring_order(pool_count)
    onward = [(order[i], order[(i + 1) % pool_count]) for i in range(pool_count)]
    backward = [(b, a) for a, b in onward]
    half = pool_count // 2
    offsets = [[0]] + [[-step, step] for step in range(1, half)] + [[half]]
    flat_offsets = sum(offsets, [])
    owners = np.zeros((pool_count, pool_count), np.int32)
    for spot, index in enumerate(order):
        owners[index] = [order[(spot + offset) % pool_count] for offset in flat_offsets]
    where = (me.astype(jnp.int32).reshape(1), jnp.asarray(owners), adapter_ids)

    weight_rows = tile_rows(kv_weight)
    key_rows = cache_keys.reshape(-1, head_size)
    value_rows = cache_values.reshape(-1, head_size)

    arrivals = [(first, second)]
    front = rear = (first, second)
    here, away = base_product(
        core, hidden_states, weight_rows, kv_heads * kv_width, [first], []
    )
    split_batches = pool_count == requests
    near = 3
    done = [(None, 0)]
    shared = None

    def finish_batch(group, after=()):
        outputs, slot = done[-1]
        after = list(after) if outputs is None else [outputs[2]]
        partial = shrink_rows(
            where, slot, hidden_states, away, group, tree_size, columns, cut, after
        )
        batch = (partial, lax.ppermute(partial, "tp", swap), [piece[0] for piece in group])
        done.append((finish(where, slot, batch, shared, outputs), slot + len(group)))

    for step in range(1, half):
        front = tuple(lax.ppermute(piece, "pool", onward) for piece in front)
        rear = tuple(lax.ppermute(piece, "pool", backward) for piece in rear)
        held = [front[1], rear[1]]
        first_front = front[0]
        if step == 1:
            held = [hold(piece, away) for piece in held]
            table = tree_tables(
                cache_lengths, tree_parents, head_size, heads_here, [here]
            )
            shared = (
                cache_lengths,
                key_gain.reshape(1, head_size),
                here,
                table,
                queries,
                key_rows,
                value_rows,
            )
        if step == 2 and split_batches:
            finish_batch(arrivals[:near])
            first_front, held[1] = hold(first_front, table), hold(held[1], table)
        front, rear = (first_front, held[0]), (rear[0], held[1])
        arrivals += [front, rear]
    arrivals.append(
        (lax.ppermute(front[0], "pool", onward), lax.ppermute(rear[1], "pool", backward))
    )
    if split_batches:
        finish_batch(arrivals[near:-3])
        finish_batch(arrivals[-3:])
        outputs = done[-1][0]
    else:
        parts = [
            shrink_rows(where, slot, hidden_states, away, [piece], tree_size, columns, cut, [])
            for slot, piece in enumerate(arrivals)
        ]
        owners_here = lax.dynamic_index_in_dim(jnp.asarray(owners), me, 0, keepdims=False)
        hot = (adapter_ids[None, :] == owners_here[:, None]).astype(jnp.int32)
        slots = jnp.sum(hot * jnp.arange(pool_count, dtype=jnp.int32)[:, None], 0)
        partial = jnp.concatenate(parts, 0)[slots]
        expands = jnp.stack([piece[0][:, :columns] for piece in arrivals])[slots]
        every = jnp.arange(requests, dtype=jnp.int32)
        batch = (
            partial,
            lax.ppermute(partial, "tp", swap),
            [expands[r] for r in range(requests)],
        )
        outputs = finish((every[:1], every[None, :], every), 0, batch, shared, None)
    attention, cache_rows, _ = outputs
    tree_cache = (
        cache_rows.reshape(row_count, 2, heads_here, head_size)
        .transpose(0, 2, 1, 3)
        .reshape(row_count, heads_here, kv_width)
    )
    return attention, tree_cache


def solution(mesh):
    placed = (
        P(("grp", "pool"), "tp"),
        P("tp", None, None),
        P(("grp", "pool"), "tp", None),
        P(("grp", "pool"), None, None, None),
        P(("grp", "pool")),
        P(("grp", "pool")),
        P(("grp", "pool"), None),
        P(("grp", "pool"), "tp", None),
        P(("grp", "pool"), None, "tp", None),
        P(("grp", "pool"), None, "tp", None),
        P(),
    )
    return jax.shard_map(
        per_device,
        mesh=mesh,
        in_specs=placed,
        out_specs=(P(("grp", "pool"), "tp", None), P(("grp", "pool"), "tp", None)),
        check_vma=False,
    )
```

```python
import functools
import math

import jax
import jax.numpy as jnp
import numpy as np
from jax import lax
from jax.experimental import pallas as pl
from jax.experimental.pallas import tpu as pltpu
from jax.sharding import PartitionSpec as P

F32 = jnp.float32
BF16 = jnp.bfloat16


ANYWHERE = pl.BlockSpec(memory_space=pl.ANY)


def shapes_of(arrays):
    return [jax.ShapeDtypeStruct(array.shape, array.dtype) for array in arrays]


def ring_order(count):
    if count == 8:
        return list(range(0, count, 2)) + list(range(count - 1, 0, -2))
    return list(range(count))


def sorting_matrix(rows, columns, inner, source_inner):
    row = lax.broadcasted_iota(jnp.int32, (rows, columns), 0)
    column = lax.broadcasted_iota(jnp.int32, (rows, columns), 1)
    return (column == (row % inner) * source_inner + row // inner).astype(F32).astype(BF16)


def picking_matrix(wanted, inner, groups, first_head):
    row = lax.broadcasted_iota(jnp.int32, (wanted * inner, 256), 0)
    column = lax.broadcasted_iota(jnp.int32, (wanted * inner, 256), 1)
    group = row // inner
    source = (group % 2) * (groups // 2) + first_head + group // 2
    return (column == (row % inner) * groups + source).astype(F32).astype(BF16)


def request_at(where, slot):
    me_ref, owner_ref, adapter_ref = where
    owner = owner_ref[me_ref[0], slot]
    request = jnp.int32(0)
    for r in range(1, adapter_ref.shape[0]):
        request = jnp.where(adapter_ref[r] == owner, jnp.int32(r), request)
    return request


def hold(array, token):
    return pl.pallas_call(
        lambda array_ref, token_ref, output_ref: None,
        in_specs=[ANYWHERE, ANYWHERE],
        out_specs=ANYWHERE,
        out_shape=jax.ShapeDtypeStruct(array.shape, array.dtype),
        input_output_aliases={0: 0},
        compiler_params=pltpu.CompilerParams(vmem_limit_bytes=4 * 1024 * 1024),
        name="hold",
    )(array, token)


def pack_kernel(core_ref, shrink_ref, expand_ref, first_ref, second_ref, *, cut, heads_here):
    rank_size = shrink_ref.shape[0]
    groups = expand_ref.shape[0] // rank_size
    ranks = 256 // groups
    pick = picking_matrix(2 * heads_here, ranks, groups, core_ref[0] * heads_here)
    columns = 2 * heads_here * 128
    for block in range(rank_size // ranks):
        sorted_rows = jnp.dot(
            pick, expand_ref[256 * block : 256 * (block + 1), :], preferred_element_type=F32
        ).astype(BF16)
        for g in range(2 * heads_here):
            first_ref[ranks * block : ranks * (block + 1), 128 * g : 128 * (g + 1)] = sorted_rows[
                ranks * g : ranks * (g + 1), :
            ]
    first_ref[:, columns:] = shrink_ref[:, :cut]
    second_ref[...] = shrink_ref[:, cut:]


def pack(core, shrink, expand_rows, cut, heads_here):
    rank_size, half_width = shrink.shape
    columns = 2 * heads_here * 128
    return pl.pallas_call(
        functools.partial(pack_kernel, cut=cut, heads_here=heads_here),
        grid_spec=pltpu.PrefetchScalarGridSpec(
            num_scalar_prefetch=1,
            grid=(1,),
            in_specs=[
                pl.BlockSpec(shrink.shape, lambda i, c: (0, 0)),
                pl.BlockSpec(expand_rows.shape, lambda i, c: (0, 0)),
            ],
            out_specs=[
                pl.BlockSpec((rank_size, columns + cut), lambda i, c: (0, 0)),
                pl.BlockSpec((rank_size, half_width - cut), lambda i, c: (0, 0)),
            ],
        ),
        out_shape=[
            jax.ShapeDtypeStruct((rank_size, columns + cut), BF16),
            jax.ShapeDtypeStruct((rank_size, half_width - cut), BF16),
        ],
        compiler_params=pltpu.CompilerParams(vmem_limit_bytes=8 * 1024 * 1024),
        name="pack",
    )(core, shrink, expand_rows)


def base_kernel(core_ref, hidden_ref, weight_ref, *rest, held_count):
    total_ref, wide_ref = rest[-2:]
    here_ref, away_ref = rest[-2 - held_count - 2 : -2 - held_count]
    step = pl.program_id(0)
    depth = hidden_ref.shape[1]
    groups = weight_ref.shape[0] // depth
    heads = groups // 2
    wide_ref[...] = weight_ref[...].astype(F32)
    parts = []
    for head in range(heads):
        tiles = [
            wide_ref[pl.ds(tile * heads + head, depth, stride=groups), :].astype(BF16)
            for tile in range(2)
        ]
        parts.append(
            jnp.dot(hidden_ref[...], jnp.concatenate(tiles, 1), preferred_element_type=F32)
        )
    product = jnp.concatenate(parts, 1)

    @pl.when(step == 0)
    def _():
        total_ref[...] = product

    @pl.when(step > 0)
    def _():
        total_ref[...] += product

    @pl.when(step == pl.num_programs(0) - 1)
    def _():
        columns = here_ref.shape[1]

        @pl.when(core_ref[0] == 0)
        def _():
            here_ref[...] = total_ref[:, :columns]
            away_ref[...] = total_ref[:, columns:]

        @pl.when(core_ref[0] == 1)
        def _():
            here_ref[...] = total_ref[:, columns:]
            away_ref[...] = total_ref[:, :columns]


def base_product(core, hidden_states, weight_rows, width, after, held):
    rows, half_width = hidden_states.shape
    groups = weight_rows.shape[0] // half_width
    depth = half_width // 2
    return pl.pallas_call(
        functools.partial(base_kernel, held_count=len(held)),
        grid_spec=pltpu.PrefetchScalarGridSpec(
            num_scalar_prefetch=1,
            grid=(half_width // depth,),
            in_specs=[
                pl.BlockSpec((rows, depth), lambda i, c: (0, i)),
                pl.BlockSpec((depth * groups, 128), lambda i, c: (i, 0)),
            ]
            + [ANYWHERE] * (len(after) + len(held)),
            out_specs=[pl.BlockSpec((rows, width // 2), lambda i, c: (0, 0))] * 2
            + [ANYWHERE] * len(held),
            scratch_shapes=[
                pltpu.VMEM((rows, width), F32),
                pltpu.VMEM((depth * groups, 128), F32),
            ],
        ),
        out_shape=[jax.ShapeDtypeStruct((rows, width // 2), F32)] * 2 + shapes_of(held),
        input_output_aliases={3 + len(after) + k: 2 + k for k in range(len(held))},
        cost_estimate=pl.CostEstimate(
            flops=4_000_000_000, bytes_accessed=9_000_000, transcendentals=0
        ),
        compiler_params=pltpu.CompilerParams(vmem_limit_bytes=24 * 1024 * 1024),
        name="base",
    )(core, hidden_states, weight_rows, *after, *held)


def tree_kernel(length_ref, parent_ref, *rest, head_size, kv_heads):
    table_ref = rest[-1]
    requests, nodes = parent_ref.shape
    node = lax.broadcasted_iota(jnp.int32, (nodes, nodes), 0)
    same = node == lax.broadcasted_iota(jnp.int32, (nodes, nodes), 1)
    spare = table_ref.shape[1] - 2 * head_size
    spread_node = lax.broadcasted_iota(jnp.int32, (nodes, spare), 0)
    spread_lane = lax.broadcasted_iota(jnp.int32, (nodes, spare), 1)
    spread = spread_lane == spread_node
    for g in range(1, kv_heads):
        spread = spread | (spread_lane == spread_node + nodes * g)
    spread = spread.astype(F32).astype(BF16)
    parents = parent_ref[...]
    below = [
        (same | (parents[r : r + 1, :] == node)).astype(F32).astype(BF16) for r in range(requests)
    ]
    reached = 1
    while reached < nodes:
        below = [
            jnp.minimum(jnp.dot(b, b, preferred_element_type=F32), 1.0).astype(BF16) for b in below
        ]
        reached = 2 * reached
    lane = lax.broadcasted_iota(jnp.int32, (nodes, head_size), 1)
    sign = jnp.where(lane < head_size // 2, -1.0, 1.0)
    power = lax.broadcasted_iota(jnp.int32, (1, head_size), 1) % (head_size // 2)
    frequency = jnp.exp(power.astype(F32) * (-2.0 * math.log(1000000.0) / head_size))
    ones = jnp.ones((nodes, head_size), BF16)
    for r in range(requests):
        b = below[r]
        depth = lax.dot_general(b, ones, (((0,), (0,)), ((), ())), preferred_element_type=F32)
        positions = length_ref[r].astype(F32) + depth - 1.0
        angles = positions * frequency
        rows = slice(nodes * r, nodes * (r + 1))
        wide = lax.dot_general(b, spread, (((0,), (0,)), ((), ())), preferred_element_type=F32)
        table_ref[rows, :] = jnp.concatenate(
            [jnp.cos(angles), jnp.sin(angles) * sign, jnp.where(wide > 0.5, 0.0, -1e30)], 1
        )


def tree_tables(cache_lengths, tree_parents, head_size, kv_heads, after):
    requests, nodes = tree_parents.shape
    whole = lambda shape: pl.BlockSpec(shape, lambda i, n: (0,) * len(shape))
    rows = requests * nodes
    width = 2 * head_size + -(-kv_heads * nodes // 128) * 128
    return pl.pallas_call(
        functools.partial(tree_kernel, head_size=head_size, kv_heads=kv_heads),
        grid_spec=pltpu.PrefetchScalarGridSpec(
            num_scalar_prefetch=1,
            grid=(1,),
            in_specs=[whole(tree_parents.shape)]
            + [ANYWHERE] * len(after),
            out_specs=whole((rows, width)),
        ),
        out_shape=jax.ShapeDtypeStruct((rows, width), F32),
        cost_estimate=pl.CostEstimate(
            flops=1_000_000_000, bytes_accessed=8_000_000, transcendentals=0
        ),
        compiler_params=pltpu.CompilerParams(vmem_limit_bytes=8 * 1024 * 1024),
        name="tree",
    )(cache_lengths, tree_parents, *after)


def shrink_kernel(me_ref, owner_ref, adapter_ref, *refs, columns, cut):
    output_ref = refs[-1]
    contract = (((1,), (1,)), ((), ()))
    for b in range(output_ref.shape[0]):
        hidden_ref, away_ref, one_ref, two_ref = refs[4 * b : 4 * b + 4]
        output_ref[b, :, :columns] = away_ref[...]
        partial = lax.dot_general(
            hidden_ref[:, :cut], one_ref[:, columns:], contract, preferred_element_type=F32
        ) + lax.dot_general(hidden_ref[:, cut:], two_ref[...], contract, preferred_element_type=F32)
        output_ref[b, :, columns:] = jnp.concatenate([partial, jnp.zeros_like(partial)], 1)


def shrink_rows(where, slot, hidden_states, away, pieces, tree_size, columns, cut, after):
    rank_size = pieces[0][0].shape[0]
    in_specs, operands = [], []
    for b, (one, two) in enumerate(pieces):
        in_specs += [
            pl.BlockSpec(
                (tree_size, hidden_states.shape[1]),
                lambda i, *refs, b=b: (request_at(refs, slot + b), 0),
            ),
            pl.BlockSpec(
                (tree_size, columns), lambda i, *refs, b=b: (request_at(refs, slot + b), 0)
            ),
            pl.BlockSpec(one.shape, lambda i, *refs: (0, 0)),
            pl.BlockSpec(two.shape, lambda i, *refs: (0, 0)),
        ]
        operands += [hidden_states, away, one, two]
    count = len(pieces)
    width = columns + 2 * rank_size
    return pl.pallas_call(
        functools.partial(shrink_kernel, columns=columns, cut=cut),
        grid_spec=pltpu.PrefetchScalarGridSpec(
            num_scalar_prefetch=3,
            grid=(1,),
            in_specs=in_specs + [ANYWHERE] * len(after),
            out_specs=pl.BlockSpec((count, tree_size, width), lambda i, *refs: (0, 0, 0)),
        ),
        out_shape=jax.ShapeDtypeStruct((count, tree_size, width), F32),
        cost_estimate=pl.CostEstimate(
            flops=count * 30000000, bytes_accessed=count * 200000, transcendentals=0
        ),
        compiler_params=pltpu.CompilerParams(vmem_limit_bytes=14 * 1024 * 1024),
        name="shrink",
    )(*where, *operands, *after)


def finish_kernel(
    me_ref,
    owner_ref,
    adapter_ref,
    length_ref,
    here_ref,
    shrunk_here_ref,
    shrunk_there_ref,
    table_ref,
    gain_ref,
    query_ref,
    key_ref,
    value_ref,
    *rest,
    count,
    slot,
    kv_heads,
):
    expand_refs = rest[:count]
    attention_ref, cache_ref, token_ref, expand_ref = rest[-4:]
    token_ref[...] = jnp.zeros_like(token_ref)
    tree_size, heads, head_size = query_ref.shape
    cached = key_ref.shape[0]
    per_group = heads // kv_heads
    rows = tree_size * heads
    columns = kv_heads * 2 * head_size
    spare = table_ref.shape[1] - 2 * head_size
    score_scale = math.log2(math.e) / math.sqrt(head_size)
    if count == 1:
        expand = expand_refs[0][...]
    else:
        for b in range(count):

            @pl.when(pl.program_id(0) == b)
            def _():
                expand_ref[...] = expand_refs[b][...]

        expand = expand_ref[...]
    length = length_ref[request_at((me_ref, owner_ref, adapter_ref), slot + pl.program_id(0))]
    ranks = slice(columns, columns + expand.shape[0])
    shrunk = shrunk_here_ref[0, :, ranks] + shrunk_there_ref[0, :, ranks]
    high = shrunk.astype(BF16)
    left = shrunk - high.astype(F32)
    middle = left.astype(BF16)
    low = (left - middle.astype(F32)).astype(BF16)
    terms = jnp.dot(jnp.concatenate([low, middle, high], 0), expand, preferred_element_type=F32)
    delta = terms[:tree_size] + terms[tree_size : 2 * tree_size] + terms[2 * tree_size :]
    projected = (here_ref[...] + shrunk_there_ref[0, :, :columns]) + delta
    cosine = table_ref[:, :head_size]
    sine = table_ref[:, head_size : 2 * head_size]
    gain = gain_ref[...]
    new_keys, new_values = [], []
    for g in range(kv_heads):
        at = 2 * head_size * g
        key = projected[:, at : at + head_size]
        new_values.append(projected[:, at + head_size : at + 2 * head_size].astype(BF16))
        norm = lax.rsqrt(jnp.mean(key * key, -1, keepdims=True) + 1e-06)
        key = key * norm * gain
        new_keys.append((key * cosine + pltpu.roll(key, head_size // 2, 1) * sine).astype(BF16))
    pad = jnp.zeros((spare - kv_heads * tree_size, head_size), BF16)
    keys = jnp.concatenate([key_ref[...]] + new_keys + [pad], 0)
    values = jnp.concatenate([value_ref[...]] + new_values + [pad], 0)
    scores = lax.dot_general(
        query_ref[...].reshape(rows, head_size),
        keys,
        (((1,), (1,)), ((), ())),
        preferred_element_type=F32,
    ).reshape(tree_size, heads, cached + spare)
    lane = lax.broadcasted_iota(jnp.int32, (heads, cached), 1)
    mine = lax.broadcasted_iota(jnp.int32, (heads, cached), 0) // per_group
    allowed = (lane % kv_heads == mine) & (lane // kv_heads < length)
    cached_bias = jnp.where(allowed, 0.0, -1e30)
    lane = lax.broadcasted_iota(jnp.int32, (heads, spare), 1)
    first = lax.broadcasted_iota(jnp.int32, (heads, spare), 0) // per_group * tree_size
    head_bias = jnp.where((lane >= first) & (lane < first + tree_size), 0.0, -1e30)
    node_bias = table_ref[:, 2 * head_size :]
    cached_scores = scores[:, :, :cached] + cached_bias[None]
    tree_scores = scores[:, :, cached:] + (node_bias[:, None, :] + head_bias[None])
    top = jnp.maximum(
        jnp.max(cached_scores, -1, keepdims=True), jnp.max(tree_scores, -1, keepdims=True)
    )
    cached_exponent = jnp.exp2((cached_scores - top) * score_scale)
    tree_exponent = jnp.exp2((tree_scores - top) * score_scale)
    total = jnp.sum(cached_exponent, -1, keepdims=True) + jnp.sum(tree_exponent, -1, keepdims=True)
    exponent = jnp.concatenate([cached_exponent, tree_exponent], -1)
    output = jnp.dot(
        exponent.astype(BF16).reshape(rows, cached + spare), values, preferred_element_type=F32
    ).reshape(tree_size, heads, head_size)
    attention_ref[...] = (output * (1.0 / total)).astype(BF16)
    stacked = jnp.concatenate(new_keys + new_values, 0)
    size = stacked.shape[0]
    cache_ref[...] = jnp.dot(
        sorting_matrix(size, size, size // tree_size, tree_size),
        stacked,
        preferred_element_type=F32,
    ).astype(BF16)


def finish(where, slot, batch, shared, previous):
    shrunk_here, shrunk_there, pieces = batch
    lengths, gain, here, table, queries, key_rows, value_rows = shared
    spot = lambda i, refs: request_at(refs[:3], slot + i)
    count, tree_size, width = shrunk_here.shape
    rank_size = pieces[0].shape[0]
    requests = lengths.shape[0]
    rows, heads, head_size = queries.shape
    columns = here.shape[1]
    kv_heads = columns // (2 * head_size)
    row_block = lambda width: pl.BlockSpec((tree_size, width), lambda i, *refs: (spot(i, refs), 0))
    shrunk_block = pl.BlockSpec((1, tree_size, width), lambda i, *refs: (i, 0, 0))
    cached_block = pl.BlockSpec(
        (key_rows.shape[0] // requests, head_size), lambda i, *refs: (spot(i, refs), 0)
    )
    query_block = pl.BlockSpec(
        (tree_size, heads, head_size), lambda i, *refs: (spot(i, refs), 0, 0)
    )
    in_specs = [
        row_block(columns),
        shrunk_block,
        shrunk_block,
        row_block(table.shape[1]),
        pl.BlockSpec((1, head_size), lambda i, *refs: (0, 0)),
        query_block,
        cached_block,
        cached_block,
    ] + [pl.BlockSpec((rank_size, columns), lambda i, *refs: (0, 0))] * count
    operands = [*where, lengths, here, shrunk_here, shrunk_there, table, gain, queries]
    operands += [key_rows, value_rows, *pieces]
    aliases = {}
    if previous is not None:
        aliases = {len(operands): 0, len(operands) + 1: 1}
        operands += previous[:2]
        in_specs += [ANYWHERE] * 2
    cache_rows = 2 * kv_heads * tree_size
    return pl.pallas_call(
        functools.partial(finish_kernel, count=count, slot=slot, kv_heads=kv_heads),
        grid_spec=pltpu.PrefetchScalarGridSpec(
            num_scalar_prefetch=4,
            grid=(count,),
            in_specs=in_specs,
            out_specs=[
                query_block,
                pl.BlockSpec((cache_rows, head_size), lambda i, *refs: (spot(i, refs), 0)),
                pl.BlockSpec((8, 128), lambda i, *refs: (0, 0)),
            ],
            scratch_shapes=[pltpu.VMEM((rank_size, columns), BF16)],
        ),
        out_shape=[
            jax.ShapeDtypeStruct((rows, heads, head_size), BF16),
            jax.ShapeDtypeStruct((rows * 2 * kv_heads, head_size), BF16),
            jax.ShapeDtypeStruct((8, 128), F32),
        ],
        input_output_aliases=aliases,
        cost_estimate=pl.CostEstimate(
            flops=count * 90000000, bytes_accessed=count * 300000, transcendentals=0
        ),
        compiler_params=pltpu.CompilerParams(vmem_limit_bytes=16 * 1024 * 1024),
        name="finish",
    )(*operands)


def per_device(
    hidden_states,
    kv_weight,
    shrink_factors,
    expand_factors,
    adapter_ids,
    cache_lengths,
    tree_parents,
    queries,
    cache_keys,
    cache_values,
    key_gain,
):
    requests, tree_size = tree_parents.shape
    row_count, half_width = hidden_states.shape
    kv_heads, kv_width = (kv_weight.shape[1], kv_weight.shape[2])
    head_size = kv_width // 2
    rank_size = shrink_factors.shape[2]
    context = cache_keys.shape[1]
    pool_count = lax.axis_size("pool")
    heads_here = kv_heads // lax.axis_size("tp")
    columns = heads_here * kv_width
    me = lax.axis_index("pool")
    core = lax.axis_index("tp").astype(jnp.int32).reshape(1)
    swap = [(0, 1), (1, 0)]

    def tile_rows(array):
        lead, heads = array.shape[0], array.shape[1]
        return array.reshape(lead, heads, 2, 128).transpose(0, 2, 1, 3).reshape(-1, 128)

    cut = (half_width + columns) // 2 - columns
    first, second = pack(
        core, shrink_factors[0].T, tile_rows(expand_factors[0]), cut, heads_here
    )

    order = ring_order(pool_count)
    onward = [(order[i], order[(i + 1) % pool_count]) for i in range(pool_count)]
    backward = [(b, a) for a, b in onward]
    half = pool_count // 2
    offsets = [[0]] + [[-step, step] for step in range(1, half)] + [[half]]
    flat_offsets = sum(offsets, [])
    owners = np.zeros((pool_count, pool_count), np.int32)
    for spot, index in enumerate(order):
        owners[index] = [order[(spot + offset) % pool_count] for offset in flat_offsets]
    where = (me.astype(jnp.int32).reshape(1), jnp.asarray(owners), adapter_ids)

    weight_rows = tile_rows(kv_weight)
    key_rows = cache_keys.reshape(-1, head_size)
    value_rows = cache_values.reshape(-1, head_size)

    arrivals = [(first, second)]
    front = rear = (first, second)
    here, away = base_product(
        core, hidden_states, weight_rows, kv_heads * kv_width, [first], []
    )
    split_batches = pool_count == requests
    near = 3
    done = [(None, 0)]
    shared = None

    def finish_batch(group):
        outputs, slot = done[-1]
        after = [] if len(done) < 3 else [outputs[2]]
        partial = shrink_rows(
            where, slot, hidden_states, away, group, tree_size, columns, cut, after
        )
        batch = (partial, lax.ppermute(partial, "tp", swap), [piece[0] for piece in group])
        done.append((finish(where, slot, batch, shared, outputs), slot + len(group)))

    for step in range(1, half):
        front = tuple(lax.ppermute(piece, "pool", onward) for piece in front)
        rear = tuple(lax.ppermute(piece, "pool", backward) for piece in rear)
        held = [front[1], rear[1]]
        first_front = front[0]
        if step == 1:
            held = [hold(piece, away) for piece in held]
            table = tree_tables(
                cache_lengths, tree_parents, head_size, heads_here, [here]
            )
            shared = (
                cache_lengths,
                key_gain.reshape(1, head_size),
                here,
                table,
                queries,
                key_rows,
                value_rows,
            )
        if step == 2 and split_batches:
            finish_batch(arrivals[:near])
            first_front, held[1] = hold(first_front, table), hold(held[1], table)
        front, rear = (first_front, held[0]), (rear[0], held[1])
        arrivals += [front, rear]
    arrivals.append(
        (lax.ppermute(front[0], "pool", onward), lax.ppermute(rear[1], "pool", backward))
    )
    if split_batches:
        finish_batch(arrivals[near:-3])
        finish_batch(arrivals[-3:])
        outputs = done[-1][0]
    else:
        parts = [
            shrink_rows(where, slot, hidden_states, away, [piece], tree_size, columns, cut, [])
            for slot, piece in enumerate(arrivals)
        ]
        owners_here = lax.dynamic_index_in_dim(jnp.asarray(owners), me, 0, keepdims=False)
        hot = (adapter_ids[None, :] == owners_here[:, None]).astype(jnp.int32)
        slots = jnp.sum(hot * jnp.arange(pool_count, dtype=jnp.int32)[:, None], 0)
        partial = jnp.concatenate(parts, 0)[slots]
        expands = jnp.stack([piece[0][:, :columns] for piece in arrivals])[slots]
        every = jnp.arange(requests, dtype=jnp.int32)
        batch = (
            partial,
            lax.ppermute(partial, "tp", swap),
            [expands[r] for r in range(requests)],
        )
        outputs = finish((every[:1], every[None, :], every), 0, batch, shared, None)
    attention, cache_rows, _ = outputs
    tree_cache = (
        cache_rows.reshape(row_count, 2, heads_here, head_size)
        .transpose(0, 2, 1, 3)
        .reshape(row_count, heads_here, kv_width)
    )
    return attention, tree_cache


def solution(mesh):
    placed = (
        P(("grp", "pool"), "tp"),
        P("tp", None, None),
        P(("grp", "pool"), "tp", None),
        P(("grp", "pool"), None, None, None),
        P(("grp", "pool")),
        P(("grp", "pool")),
        P(("grp", "pool"), None),
        P(("grp", "pool"), "tp", None),
        P(("grp", "pool"), None, "tp", None),
        P(("grp", "pool"), None, "tp", None),
        P(),
    )
    return jax.shard_map(
        per_device,
        mesh=mesh,
        in_specs=placed,
        out_specs=(P(("grp", "pool"), "tp", None), P(("grp", "pool"), "tp", None)),
        check_vma=False,
    )
```

```python
import functools
import math

import jax
import jax.numpy as jnp
import numpy as np
from jax import lax
from jax.experimental import pallas as pl
from jax.experimental.pallas import tpu as pltpu
from jax.sharding import PartitionSpec as P

F32 = jnp.float32
BF16 = jnp.bfloat16


ANYWHERE = pl.BlockSpec(memory_space=pl.ANY)


def shapes_of(arrays):
    return [jax.ShapeDtypeStruct(array.shape, array.dtype) for array in arrays]


def ring_order(count):
    if count == 8:
        return list(range(0, count, 2)) + list(range(count - 1, 0, -2))
    return list(range(count))


def sorting_matrix(rows, columns, inner, source_inner):
    row = lax.broadcasted_iota(jnp.int32, (rows, columns), 0)
    column = lax.broadcasted_iota(jnp.int32, (rows, columns), 1)
    return (column == (row % inner) * source_inner + row // inner).astype(F32).astype(BF16)


def picking_matrix(wanted, inner, groups, first_head):
    row = lax.broadcasted_iota(jnp.int32, (wanted * inner, 256), 0)
    column = lax.broadcasted_iota(jnp.int32, (wanted * inner, 256), 1)
    group = row // inner
    source = (group % 2) * (groups // 2) + first_head + group // 2
    return (column == (row % inner) * groups + source).astype(F32).astype(BF16)


def request_at(where, slot):
    me_ref, owner_ref, adapter_ref = where
    owner = owner_ref[me_ref[0], slot]
    request = jnp.int32(0)
    for r in range(1, adapter_ref.shape[0]):
        request = jnp.where(adapter_ref[r] == owner, jnp.int32(r), request)
    return request


def hold(array, token):
    return pl.pallas_call(
        lambda array_ref, token_ref, output_ref: None,
        in_specs=[ANYWHERE, ANYWHERE],
        out_specs=ANYWHERE,
        out_shape=jax.ShapeDtypeStruct(array.shape, array.dtype),
        input_output_aliases={0: 0},
        compiler_params=pltpu.CompilerParams(vmem_limit_bytes=4 * 1024 * 1024),
        name="hold",
    )(array, token)


def pack_kernel(core_ref, shrink_ref, expand_ref, first_ref, second_ref, *, cut, heads_here):
    rank_size = shrink_ref.shape[0]
    groups = expand_ref.shape[0] // rank_size
    ranks = 256 // groups
    pick = picking_matrix(2 * heads_here, ranks, groups, core_ref[0] * heads_here)
    columns = 2 * heads_here * 128
    for block in range(rank_size // ranks):
        sorted_rows = jnp.dot(
            pick, expand_ref[256 * block : 256 * (block + 1), :], preferred_element_type=F32
        ).astype(BF16)
        for g in range(2 * heads_here):
            first_ref[ranks * block : ranks * (block + 1), 128 * g : 128 * (g + 1)] = sorted_rows[
                ranks * g : ranks * (g + 1), :
            ]
    first_ref[:, columns:] = shrink_ref[:, :cut]
    second_ref[...] = shrink_ref[:, cut:]


def pack(core, shrink, expand_rows, cut, heads_here):
    rank_size, half_width = shrink.shape
    columns = 2 * heads_here * 128
    return pl.pallas_call(
        functools.partial(pack_kernel, cut=cut, heads_here=heads_here),
        grid_spec=pltpu.PrefetchScalarGridSpec(
            num_scalar_prefetch=1,
            grid=(1,),
            in_specs=[
                pl.BlockSpec(shrink.shape, lambda i, c: (0, 0)),
                pl.BlockSpec(expand_rows.shape, lambda i, c: (0, 0)),
            ],
            out_specs=[
                pl.BlockSpec((rank_size, columns + cut), lambda i, c: (0, 0)),
                pl.BlockSpec((rank_size, half_width - cut), lambda i, c: (0, 0)),
            ],
        ),
        out_shape=[
            jax.ShapeDtypeStruct((rank_size, columns + cut), BF16),
            jax.ShapeDtypeStruct((rank_size, half_width - cut), BF16),
        ],
        compiler_params=pltpu.CompilerParams(vmem_limit_bytes=8 * 1024 * 1024),
        name="pack",
    )(core, shrink, expand_rows)


def base_kernel(core_ref, hidden_ref, weight_ref, *rest, held_count):
    total_ref, wide_ref = rest[-2:]
    here_ref, away_ref = rest[-2 - held_count - 2 : -2 - held_count]
    step = pl.program_id(0)
    depth = hidden_ref.shape[1]
    groups = weight_ref.shape[0] // depth
    heads = groups // 2
    wide_ref[...] = weight_ref[...].astype(F32)
    parts = []
    for head in range(heads):
        tiles = [
            wide_ref[pl.ds(tile * heads + head, depth, stride=groups), :].astype(BF16)
            for tile in range(2)
        ]
        parts.append(
            jnp.dot(hidden_ref[...], jnp.concatenate(tiles, 1), preferred_element_type=F32)
        )
    product = jnp.concatenate(parts, 1)

    @pl.when(step == 0)
    def _():
        total_ref[...] = product

    @pl.when(step > 0)
    def _():
        total_ref[...] += product

    @pl.when(step == pl.num_programs(0) - 1)
    def _():
        columns = here_ref.shape[1]

        @pl.when(core_ref[0] == 0)
        def _():
            here_ref[...] = total_ref[:, :columns]
            away_ref[...] = total_ref[:, columns:]

        @pl.when(core_ref[0] == 1)
        def _():
            here_ref[...] = total_ref[:, columns:]
            away_ref[...] = total_ref[:, :columns]


def base_product(core, hidden_states, weight_rows, width, after, held):
    rows, half_width = hidden_states.shape
    groups = weight_rows.shape[0] // half_width
    depth = half_width // 2
    return pl.pallas_call(
        functools.partial(base_kernel, held_count=len(held)),
        grid_spec=pltpu.PrefetchScalarGridSpec(
            num_scalar_prefetch=1,
            grid=(half_width // depth,),
            in_specs=[
                pl.BlockSpec((rows, depth), lambda i, c: (0, i)),
                pl.BlockSpec((depth * groups, 128), lambda i, c: (i, 0)),
            ]
            + [ANYWHERE] * (len(after) + len(held)),
            out_specs=[pl.BlockSpec((rows, width // 2), lambda i, c: (0, 0))] * 2
            + [ANYWHERE] * len(held),
            scratch_shapes=[
                pltpu.VMEM((rows, width), F32),
                pltpu.VMEM((depth * groups, 128), F32),
            ],
        ),
        out_shape=[jax.ShapeDtypeStruct((rows, width // 2), F32)] * 2 + shapes_of(held),
        input_output_aliases={3 + len(after) + k: 2 + k for k in range(len(held))},
        cost_estimate=pl.CostEstimate(
            flops=4_000_000_000, bytes_accessed=9_000_000, transcendentals=0
        ),
        compiler_params=pltpu.CompilerParams(vmem_limit_bytes=24 * 1024 * 1024),
        name="base",
    )(core, hidden_states, weight_rows, *after, *held)


def tree_kernel(length_ref, parent_ref, *rest, head_size, kv_heads):
    table_ref = rest[-1]
    requests, nodes = parent_ref.shape
    node = lax.broadcasted_iota(jnp.int32, (nodes, nodes), 0)
    same = node == lax.broadcasted_iota(jnp.int32, (nodes, nodes), 1)
    spare = table_ref.shape[1] - 2 * head_size
    spread_node = lax.broadcasted_iota(jnp.int32, (nodes, spare), 0)
    spread_lane = lax.broadcasted_iota(jnp.int32, (nodes, spare), 1)
    spread = spread_lane == spread_node
    for g in range(1, kv_heads):
        spread = spread | (spread_lane == spread_node + nodes * g)
    spread = spread.astype(F32).astype(BF16)
    parents = parent_ref[...]
    below = [
        (same | (parents[r : r + 1, :] == node)).astype(F32).astype(BF16) for r in range(requests)
    ]
    reached = 1
    while reached < nodes:
        below = [
            jnp.minimum(jnp.dot(b, b, preferred_element_type=F32), 1.0).astype(BF16) for b in below
        ]
        reached = 2 * reached
    lane = lax.broadcasted_iota(jnp.int32, (nodes, head_size), 1)
    sign = jnp.where(lane < head_size // 2, -1.0, 1.0)
    power = lax.broadcasted_iota(jnp.int32, (1, head_size), 1) % (head_size // 2)
    frequency = jnp.exp(power.astype(F32) * (-2.0 * math.log(1000000.0) / head_size))
    ones = jnp.ones((nodes, head_size), BF16)
    for r in range(requests):
        b = below[r]
        depth = lax.dot_general(b, ones, (((0,), (0,)), ((), ())), preferred_element_type=F32)
        positions = length_ref[r].astype(F32) + depth - 1.0
        angles = positions * frequency
        rows = slice(nodes * r, nodes * (r + 1))
        wide = lax.dot_general(b, spread, (((0,), (0,)), ((), ())), preferred_element_type=F32)
        table_ref[rows, :] = jnp.concatenate(
            [jnp.cos(angles), jnp.sin(angles) * sign, jnp.where(wide > 0.5, 0.0, -1e30)], 1
        )


def tree_tables(cache_lengths, tree_parents, head_size, kv_heads, after):
    requests, nodes = tree_parents.shape
    whole = lambda shape: pl.BlockSpec(shape, lambda i, n: (0,) * len(shape))
    rows = requests * nodes
    width = 2 * head_size + -(-kv_heads * nodes // 128) * 128
    return pl.pallas_call(
        functools.partial(tree_kernel, head_size=head_size, kv_heads=kv_heads),
        grid_spec=pltpu.PrefetchScalarGridSpec(
            num_scalar_prefetch=1,
            grid=(1,),
            in_specs=[whole(tree_parents.shape)]
            + [ANYWHERE] * len(after),
            out_specs=whole((rows, width)),
        ),
        out_shape=jax.ShapeDtypeStruct((rows, width), F32),
        cost_estimate=pl.CostEstimate(
            flops=1_000_000_000, bytes_accessed=8_000_000, transcendentals=0
        ),
        compiler_params=pltpu.CompilerParams(vmem_limit_bytes=8 * 1024 * 1024),
        name="tree",
    )(cache_lengths, tree_parents, *after)


def shrink_kernel(me_ref, owner_ref, adapter_ref, *refs, columns, cut):
    output_ref = refs[-1]
    contract = (((1,), (1,)), ((), ()))
    for b in range(output_ref.shape[0]):
        hidden_ref, away_ref, one_ref, two_ref = refs[4 * b : 4 * b + 4]
        output_ref[b, :, :columns] = away_ref[...]
        partial = lax.dot_general(
            hidden_ref[:, :cut], one_ref[:, columns:], contract, preferred_element_type=F32
        ) + lax.dot_general(hidden_ref[:, cut:], two_ref[...], contract, preferred_element_type=F32)
        output_ref[b, :, columns:] = jnp.concatenate([partial, jnp.zeros_like(partial)], 1)


def shrink_rows(where, slot, hidden_states, away, pieces, tree_size, columns, cut, after):
    rank_size = pieces[0][0].shape[0]
    in_specs, operands = [], []
    for b, (one, two) in enumerate(pieces):
        in_specs += [
            pl.BlockSpec(
                (tree_size, hidden_states.shape[1]),
                lambda i, *refs, b=b: (request_at(refs, slot + b), 0),
            ),
            pl.BlockSpec(
                (tree_size, columns), lambda i, *refs, b=b: (request_at(refs, slot + b), 0)
            ),
            pl.BlockSpec(one.shape, lambda i, *refs: (0, 0)),
            pl.BlockSpec(two.shape, lambda i, *refs: (0, 0)),
        ]
        operands += [hidden_states, away, one, two]
    count = len(pieces)
    width = columns + 2 * rank_size
    return pl.pallas_call(
        functools.partial(shrink_kernel, columns=columns, cut=cut),
        grid_spec=pltpu.PrefetchScalarGridSpec(
            num_scalar_prefetch=3,
            grid=(1,),
            in_specs=in_specs + [ANYWHERE] * len(after),
            out_specs=pl.BlockSpec((count, tree_size, width), lambda i, *refs: (0, 0, 0)),
        ),
        out_shape=jax.ShapeDtypeStruct((count, tree_size, width), F32),
        cost_estimate=pl.CostEstimate(
            flops=count * 30000000, bytes_accessed=count * 200000, transcendentals=0
        ),
        compiler_params=pltpu.CompilerParams(vmem_limit_bytes=14 * 1024 * 1024),
        name="shrink",
    )(*where, *operands, *after)


def finish_kernel(
    me_ref,
    owner_ref,
    adapter_ref,
    length_ref,
    here_ref,
    shrunk_here_ref,
    shrunk_there_ref,
    table_ref,
    gain_ref,
    query_ref,
    key_ref,
    value_ref,
    *rest,
    count,
    slot,
    kv_heads,
):
    expand_refs = rest[:count]
    attention_ref, cache_ref, token_ref, expand_ref = rest[-4:]
    token_ref[...] = jnp.zeros_like(token_ref)
    tree_size, heads, head_size = query_ref.shape
    cached = key_ref.shape[0]
    per_group = heads // kv_heads
    rows = tree_size * heads
    columns = kv_heads * 2 * head_size
    spare = table_ref.shape[1] - 2 * head_size
    score_scale = math.log2(math.e) / math.sqrt(head_size)
    if count == 1:
        expand = expand_refs[0][...]
    else:
        for b in range(count):

            @pl.when(pl.program_id(0) == b)
            def _():
                expand_ref[...] = expand_refs[b][...]

        expand = expand_ref[...]
    length = length_ref[request_at((me_ref, owner_ref, adapter_ref), slot + pl.program_id(0))]
    ranks = slice(columns, columns + expand.shape[0])
    shrunk = shrunk_here_ref[0, :, ranks] + shrunk_there_ref[0, :, ranks]
    high = shrunk.astype(BF16)
    left = shrunk - high.astype(F32)
    middle = left.astype(BF16)
    low = (left - middle.astype(F32)).astype(BF16)
    terms = jnp.dot(jnp.concatenate([low, middle, high], 0), expand, preferred_element_type=F32)
    delta = terms[:tree_size] + terms[tree_size : 2 * tree_size] + terms[2 * tree_size :]
    projected = (here_ref[...] + shrunk_there_ref[0, :, :columns]) + delta
    cosine = table_ref[:, :head_size]
    sine = table_ref[:, head_size : 2 * head_size]
    gain = gain_ref[...]
    new_keys, new_values = [], []
    for g in range(kv_heads):
        at = 2 * head_size * g
        key = projected[:, at : at + head_size]
        new_values.append(projected[:, at + head_size : at + 2 * head_size].astype(BF16))
        norm = lax.rsqrt(jnp.mean(key * key, -1, keepdims=True) + 1e-06)
        key = key * norm * gain
        new_keys.append((key * cosine + pltpu.roll(key, head_size // 2, 1) * sine).astype(BF16))
    pad = jnp.zeros((spare - kv_heads * tree_size, head_size), BF16)
    keys = jnp.concatenate([key_ref[...]] + new_keys + [pad], 0)
    values = jnp.concatenate([value_ref[...]] + new_values + [pad], 0)
    scores = lax.dot_general(
        query_ref[...].reshape(rows, head_size),
        keys,
        (((1,), (1,)), ((), ())),
        preferred_element_type=F32,
    ).reshape(tree_size, heads, cached + spare)
    lane = lax.broadcasted_iota(jnp.int32, (heads, cached), 1)
    mine = lax.broadcasted_iota(jnp.int32, (heads, cached), 0) // per_group
    allowed = (lane % kv_heads == mine) & (lane // kv_heads < length)
    cached_bias = jnp.where(allowed, 0.0, -1e30)
    lane = lax.broadcasted_iota(jnp.int32, (heads, spare), 1)
    first = lax.broadcasted_iota(jnp.int32, (heads, spare), 0) // per_group * tree_size
    head_bias = jnp.where((lane >= first) & (lane < first + tree_size), 0.0, -1e30)
    node_bias = table_ref[:, 2 * head_size :]
    cached_scores = scores[:, :, :cached] + cached_bias[None]
    tree_scores = scores[:, :, cached:] + (node_bias[:, None, :] + head_bias[None])
    top = jnp.maximum(
        jnp.max(cached_scores, -1, keepdims=True), jnp.max(tree_scores, -1, keepdims=True)
    )
    cached_exponent = jnp.exp2((cached_scores - top) * score_scale)
    tree_exponent = jnp.exp2((tree_scores - top) * score_scale)
    total = jnp.sum(cached_exponent, -1, keepdims=True) + jnp.sum(tree_exponent, -1, keepdims=True)
    exponent = jnp.concatenate([cached_exponent, tree_exponent], -1)
    output = jnp.dot(
        exponent.astype(BF16).reshape(rows, cached + spare), values, preferred_element_type=F32
    ).reshape(tree_size, heads, head_size)
    attention_ref[...] = (output * (1.0 / total)).astype(BF16)
    stacked = jnp.concatenate(new_keys + new_values, 0)
    size = stacked.shape[0]
    cache_ref[...] = jnp.dot(
        sorting_matrix(size, size, size // tree_size, tree_size),
        stacked,
        preferred_element_type=F32,
    ).astype(BF16)


def finish(where, slot, batch, shared, previous):
    shrunk_here, shrunk_there, pieces = batch
    lengths, gain, here, table, queries, key_rows, value_rows = shared
    spot = lambda i, refs: request_at(refs[:3], slot + i)
    count, tree_size, width = shrunk_here.shape
    rank_size = pieces[0].shape[0]
    requests = lengths.shape[0]
    rows, heads, head_size = queries.shape
    columns = here.shape[1]
    kv_heads = columns // (2 * head_size)
    row_block = lambda width: pl.BlockSpec((tree_size, width), lambda i, *refs: (spot(i, refs), 0))
    shrunk_block = pl.BlockSpec((1, tree_size, width), lambda i, *refs: (i, 0, 0))
    cached_block = pl.BlockSpec(
        (key_rows.shape[0] // requests, head_size), lambda i, *refs: (spot(i, refs), 0)
    )
    query_block = pl.BlockSpec(
        (tree_size, heads, head_size), lambda i, *refs: (spot(i, refs), 0, 0)
    )
    in_specs = [
        row_block(columns),
        shrunk_block,
        shrunk_block,
        row_block(table.shape[1]),
        pl.BlockSpec((1, head_size), lambda i, *refs: (0, 0)),
        query_block,
        cached_block,
        cached_block,
    ] + [pl.BlockSpec((rank_size, columns), lambda i, *refs: (0, 0))] * count
    operands = [*where, lengths, here, shrunk_here, shrunk_there, table, gain, queries]
    operands += [key_rows, value_rows, *pieces]
    aliases = {}
    if previous is not None:
        aliases = {len(operands): 0, len(operands) + 1: 1}
        operands += previous[:2]
        in_specs += [ANYWHERE] * 2
    cache_rows = 2 * kv_heads * tree_size
    return pl.pallas_call(
        functools.partial(finish_kernel, count=count, slot=slot, kv_heads=kv_heads),
        grid_spec=pltpu.PrefetchScalarGridSpec(
            num_scalar_prefetch=4,
            grid=(count,),
            in_specs=in_specs,
            out_specs=[
                query_block,
                pl.BlockSpec((cache_rows, head_size), lambda i, *refs: (spot(i, refs), 0)),
                pl.BlockSpec((8, 128), lambda i, *refs: (0, 0)),
            ],
            scratch_shapes=[pltpu.VMEM((rank_size, columns), BF16)],
        ),
        out_shape=[
            jax.ShapeDtypeStruct((rows, heads, head_size), BF16),
            jax.ShapeDtypeStruct((rows * 2 * kv_heads, head_size), BF16),
            jax.ShapeDtypeStruct((8, 128), F32),
        ],
        input_output_aliases=aliases,
        cost_estimate=pl.CostEstimate(
            flops=count * 90000000, bytes_accessed=count * 300000, transcendentals=0
        ),
        compiler_params=pltpu.CompilerParams(vmem_limit_bytes=16 * 1024 * 1024),
        name="finish",
    )(*operands)


def per_device(
    hidden_states,
    kv_weight,
    shrink_factors,
    expand_factors,
    adapter_ids,
    cache_lengths,
    tree_parents,
    queries,
    cache_keys,
    cache_values,
    key_gain,
):
    requests, tree_size = tree_parents.shape
    row_count, half_width = hidden_states.shape
    kv_heads, kv_width = (kv_weight.shape[1], kv_weight.shape[2])
    head_size = kv_width // 2
    rank_size = shrink_factors.shape[2]
    context = cache_keys.shape[1]
    pool_count = lax.axis_size("pool")
    heads_here = kv_heads // lax.axis_size("tp")
    columns = heads_here * kv_width
    me = lax.axis_index("pool")
    core = lax.axis_index("tp").astype(jnp.int32).reshape(1)
    swap = [(0, 1), (1, 0)]

    def tile_rows(array):
        lead, heads = array.shape[0], array.shape[1]
        return array.reshape(lead, heads, 2, 128).transpose(0, 2, 1, 3).reshape(-1, 128)

    cut = (half_width + columns) // 2 - columns
    first, second = pack(
        core, shrink_factors[0].T, tile_rows(expand_factors[0]), cut, heads_here
    )

    order = ring_order(pool_count)
    onward = [(order[i], order[(i + 1) % pool_count]) for i in range(pool_count)]
    backward = [(b, a) for a, b in onward]
    half = pool_count // 2
    offsets = [[0]] + [[-step, step] for step in range(1, half)] + [[half]]
    flat_offsets = sum(offsets, [])
    owners = np.zeros((pool_count, pool_count), np.int32)
    for spot, index in enumerate(order):
        owners[index] = [order[(spot + offset) % pool_count] for offset in flat_offsets]
    where = (me.astype(jnp.int32).reshape(1), jnp.asarray(owners), adapter_ids)

    weight_rows = tile_rows(kv_weight)
    key_rows = cache_keys.reshape(-1, head_size)
    value_rows = cache_values.reshape(-1, head_size)

    arrivals = [(first, second)]
    front = rear = (first, second)
    here, away = base_product(
        core, hidden_states, weight_rows, kv_heads * kv_width, [first], []
    )
    split_batches = pool_count == requests
    near = 3
    done = [(None, 0)]
    shared = None

    def finish_batch(group, partial=None):
        outputs, slot = done[-1]
        after = [] if len(done) < 3 else [outputs[2]]
        if partial is None:
            partial = shrink_rows(
                where, slot, hidden_states, away, group, tree_size, columns, cut, after
            )
        batch = (partial, lax.ppermute(partial, "tp", swap), [piece[0] for piece in group])
        done.append((finish(where, slot, batch, shared, outputs), slot + len(group)))

    for step in range(1, half):
        front = tuple(lax.ppermute(piece, "pool", onward) for piece in front)
        rear = tuple(lax.ppermute(piece, "pool", backward) for piece in rear)
        held = [front[1], rear[1]]
        first_front = front[0]
        if step == 1:
            token = away
            if split_batches:
                token = near_partial = shrink_rows(
                    where,
                    0,
                    hidden_states,
                    away,
                    arrivals + [front, rear],
                    tree_size,
                    columns,
                    cut,
                    [],
                )
            held = [hold(piece, token) for piece in held]
            table = tree_tables(
                cache_lengths, tree_parents, head_size, heads_here, [here]
            )
            shared = (
                cache_lengths,
                key_gain.reshape(1, head_size),
                here,
                table,
                queries,
                key_rows,
                value_rows,
            )
        if step == 2 and split_batches:
            finish_batch(arrivals[:near], near_partial)
            first_front, held[1] = hold(first_front, table), hold(held[1], table)
        front, rear = (first_front, held[0]), (rear[0], held[1])
        arrivals += [front, rear]
    arrivals.append(
        (lax.ppermute(front[0], "pool", onward), lax.ppermute(rear[1], "pool", backward))
    )
    if split_batches:
        finish_batch(arrivals[near:-3])
        finish_batch(arrivals[-3:])
        outputs = done[-1][0]
    else:
        parts = [
            shrink_rows(where, slot, hidden_states, away, [piece], tree_size, columns, cut, [])
            for slot, piece in enumerate(arrivals)
        ]
        owners_here = lax.dynamic_index_in_dim(jnp.asarray(owners), me, 0, keepdims=False)
        hot = (adapter_ids[None, :] == owners_here[:, None]).astype(jnp.int32)
        slots = jnp.sum(hot * jnp.arange(pool_count, dtype=jnp.int32)[:, None], 0)
        partial = jnp.concatenate(parts, 0)[slots]
        expands = jnp.stack([piece[0][:, :columns] for piece in arrivals])[slots]
        every = jnp.arange(requests, dtype=jnp.int32)
        batch = (
            partial,
            lax.ppermute(partial, "tp", swap),
            [expands[r] for r in range(requests)],
        )
        outputs = finish((every[:1], every[None, :], every), 0, batch, shared, None)
    attention, cache_rows, _ = outputs
    tree_cache = (
        cache_rows.reshape(row_count, 2, heads_here, head_size)
        .transpose(0, 2, 1, 3)
        .reshape(row_count, heads_here, kv_width)
    )
    return attention, tree_cache


def solution(mesh):
    placed = (
        P(("grp", "pool"), "tp"),
        P("tp", None, None),
        P(("grp", "pool"), "tp", None),
        P(("grp", "pool"), None, None, None),
        P(("grp", "pool")),
        P(("grp", "pool")),
        P(("grp", "pool"), None),
        P(("grp", "pool"), "tp", None),
        P(("grp", "pool"), None, "tp", None),
        P(("grp", "pool"), None, "tp", None),
        P(),
    )
    return jax.shard_map(
        per_device,
        mesh=mesh,
        in_specs=placed,
        out_specs=(P(("grp", "pool"), "tp", None), P(("grp", "pool"), "tp", None)),
        check_vma=False,
    )
```

```python
import functools
import math

import jax
import jax.numpy as jnp
import numpy as np
from jax import lax
from jax.experimental import pallas as pl
from jax.experimental.pallas import tpu as pltpu
from jax.sharding import PartitionSpec as P

F32 = jnp.float32
BF16 = jnp.bfloat16


ANYWHERE = pl.BlockSpec(memory_space=pl.ANY)


def shapes_of(arrays):
    return [jax.ShapeDtypeStruct(array.shape, array.dtype) for array in arrays]


def ring_order(count):
    if count == 8:
        return list(range(0, count, 2)) + list(range(count - 1, 0, -2))
    return list(range(count))


def sorting_matrix(rows, columns, inner, source_inner):
    row = lax.broadcasted_iota(jnp.int32, (rows, columns), 0)
    column = lax.broadcasted_iota(jnp.int32, (rows, columns), 1)
    return (column == (row % inner) * source_inner + row // inner).astype(F32).astype(BF16)


def picking_matrix(wanted, inner, groups, first_head):
    row = lax.broadcasted_iota(jnp.int32, (wanted * inner, 256), 0)
    column = lax.broadcasted_iota(jnp.int32, (wanted * inner, 256), 1)
    group = row // inner
    source = (group % 2) * (groups // 2) + first_head + group // 2
    return (column == (row % inner) * groups + source).astype(F32).astype(BF16)


def request_at(where, slot):
    me_ref, owner_ref, adapter_ref = where
    owner = owner_ref[me_ref[0], slot]
    request = jnp.int32(0)
    for r in range(1, adapter_ref.shape[0]):
        request = jnp.where(adapter_ref[r] == owner, jnp.int32(r), request)
    return request


def hold(array, token):
    return pl.pallas_call(
        lambda array_ref, token_ref, output_ref: None,
        in_specs=[ANYWHERE, ANYWHERE],
        out_specs=ANYWHERE,
        out_shape=jax.ShapeDtypeStruct(array.shape, array.dtype),
        input_output_aliases={0: 0},
        compiler_params=pltpu.CompilerParams(vmem_limit_bytes=4 * 1024 * 1024),
        name="hold",
    )(array, token)


def pack_kernel(core_ref, shrink_ref, expand_ref, first_ref, second_ref, *, cut, heads_here):
    rank_size = shrink_ref.shape[0]
    groups = expand_ref.shape[0] // rank_size
    ranks = 256 // groups
    pick = picking_matrix(2 * heads_here, ranks, groups, core_ref[0] * heads_here)
    columns = 2 * heads_here * 128
    for block in range(rank_size // ranks):
        sorted_rows = jnp.dot(
            pick, expand_ref[256 * block : 256 * (block + 1), :], preferred_element_type=F32
        ).astype(BF16)
        for g in range(2 * heads_here):
            first_ref[ranks * block : ranks * (block + 1), 128 * g : 128 * (g + 1)] = sorted_rows[
                ranks * g : ranks * (g + 1), :
            ]
    first_ref[:, columns:] = shrink_ref[:, :cut]
    second_ref[...] = shrink_ref[:, cut:]


def pack(core, shrink, expand_rows, cut, heads_here):
    rank_size, half_width = shrink.shape
    columns = 2 * heads_here * 128
    return pl.pallas_call(
        functools.partial(pack_kernel, cut=cut, heads_here=heads_here),
        grid_spec=pltpu.PrefetchScalarGridSpec(
            num_scalar_prefetch=1,
            grid=(1,),
            in_specs=[
                pl.BlockSpec(shrink.shape, lambda i, c: (0, 0)),
                pl.BlockSpec(expand_rows.shape, lambda i, c: (0, 0)),
            ],
            out_specs=[
                pl.BlockSpec((rank_size, columns + cut), lambda i, c: (0, 0)),
                pl.BlockSpec((rank_size, half_width - cut), lambda i, c: (0, 0)),
            ],
        ),
        out_shape=[
            jax.ShapeDtypeStruct((rank_size, columns + cut), BF16),
            jax.ShapeDtypeStruct((rank_size, half_width - cut), BF16),
        ],
        compiler_params=pltpu.CompilerParams(vmem_limit_bytes=8 * 1024 * 1024),
        name="pack",
    )(core, shrink, expand_rows)


def base_kernel(core_ref, hidden_ref, weight_ref, *rest, held_count):
    total_ref, wide_ref = rest[-2:]
    here_ref, away_ref = rest[-2 - held_count - 2 : -2 - held_count]
    step = pl.program_id(0)
    depth = hidden_ref.shape[1]
    groups = weight_ref.shape[0] // depth
    heads = groups // 2
    wide_ref[...] = weight_ref[...].astype(F32)
    parts = []
    for head in range(heads):
        tiles = [
            wide_ref[pl.ds(tile * heads + head, depth, stride=groups), :].astype(BF16)
            for tile in range(2)
        ]
        parts.append(
            jnp.dot(hidden_ref[...], jnp.concatenate(tiles, 1), preferred_element_type=F32)
        )
    product = jnp.concatenate(parts, 1)

    @pl.when(step == 0)
    def _():
        total_ref[...] = product

    @pl.when(step > 0)
    def _():
        total_ref[...] += product

    @pl.when(step == pl.num_programs(0) - 1)
    def _():
        columns = here_ref.shape[1]

        @pl.when(core_ref[0] == 0)
        def _():
            here_ref[...] = total_ref[:, :columns]
            away_ref[...] = total_ref[:, columns:]

        @pl.when(core_ref[0] == 1)
        def _():
            here_ref[...] = total_ref[:, columns:]
            away_ref[...] = total_ref[:, :columns]


def base_product(core, hidden_states, weight_rows, width, after, held):
    rows, half_width = hidden_states.shape
    groups = weight_rows.shape[0] // half_width
    depth = half_width // 2
    return pl.pallas_call(
        functools.partial(base_kernel, held_count=len(held)),
        grid_spec=pltpu.PrefetchScalarGridSpec(
            num_scalar_prefetch=1,
            grid=(half_width // depth,),
            in_specs=[
                pl.BlockSpec((rows, depth), lambda i, c: (0, i)),
                pl.BlockSpec((depth * groups, 128), lambda i, c: (i, 0)),
            ]
            + [ANYWHERE] * (len(after) + len(held)),
            out_specs=[pl.BlockSpec((rows, width // 2), lambda i, c: (0, 0))] * 2
            + [ANYWHERE] * len(held),
            scratch_shapes=[
                pltpu.VMEM((rows, width), F32),
                pltpu.VMEM((depth * groups, 128), F32),
            ],
        ),
        out_shape=[jax.ShapeDtypeStruct((rows, width // 2), F32)] * 2 + shapes_of(held),
        input_output_aliases={3 + len(after) + k: 2 + k for k in range(len(held))},
        cost_estimate=pl.CostEstimate(
            flops=4_000_000_000, bytes_accessed=9_000_000, transcendentals=0
        ),
        compiler_params=pltpu.CompilerParams(vmem_limit_bytes=52 * 1024 * 1024),
        name="base",
    )(core, hidden_states, weight_rows, *after, *held)


def tree_kernel(length_ref, parent_ref, *rest, head_size, kv_heads):
    table_ref = rest[-1]
    requests, nodes = parent_ref.shape
    node = lax.broadcasted_iota(jnp.int32, (nodes, nodes), 0)
    same = node == lax.broadcasted_iota(jnp.int32, (nodes, nodes), 1)
    spare = table_ref.shape[1] - 2 * head_size
    spread_node = lax.broadcasted_iota(jnp.int32, (nodes, spare), 0)
    spread_lane = lax.broadcasted_iota(jnp.int32, (nodes, spare), 1)
    spread = spread_lane == spread_node
    for g in range(1, kv_heads):
        spread = spread | (spread_lane == spread_node + nodes * g)
    spread = spread.astype(F32).astype(BF16)
    parents = parent_ref[...]
    below = [
        (same | (parents[r : r + 1, :] == node)).astype(F32).astype(BF16) for r in range(requests)
    ]
    reached = 1
    while reached < nodes:
        below = [
            jnp.minimum(jnp.dot(b, b, preferred_element_type=F32), 1.0).astype(BF16) for b in below
        ]
        reached = 2 * reached
    lane = lax.broadcasted_iota(jnp.int32, (nodes, head_size), 1)
    sign = jnp.where(lane < head_size // 2, -1.0, 1.0)
    power = lax.broadcasted_iota(jnp.int32, (1, head_size), 1) % (head_size // 2)
    frequency = jnp.exp(power.astype(F32) * (-2.0 * math.log(1000000.0) / head_size))
    ones = jnp.ones((nodes, head_size), BF16)
    for r in range(requests):
        b = below[r]
        depth = lax.dot_general(b, ones, (((0,), (0,)), ((), ())), preferred_element_type=F32)
        positions = length_ref[r].astype(F32) + depth - 1.0
        angles = positions * frequency
        rows = slice(nodes * r, nodes * (r + 1))
        wide = lax.dot_general(b, spread, (((0,), (0,)), ((), ())), preferred_element_type=F32)
        table_ref[rows, :] = jnp.concatenate(
            [jnp.cos(angles), jnp.sin(angles) * sign, jnp.where(wide > 0.5, 0.0, -1e30)], 1
        )


def tree_tables(cache_lengths, tree_parents, head_size, kv_heads, after):
    requests, nodes = tree_parents.shape
    whole = lambda shape: pl.BlockSpec(shape, lambda i, n: (0,) * len(shape))
    rows = requests * nodes
    width = 2 * head_size + -(-kv_heads * nodes // 128) * 128
    return pl.pallas_call(
        functools.partial(tree_kernel, head_size=head_size, kv_heads=kv_heads),
        grid_spec=pltpu.PrefetchScalarGridSpec(
            num_scalar_prefetch=1,
            grid=(1,),
            in_specs=[whole(tree_parents.shape)]
            + [ANYWHERE] * len(after),
            out_specs=whole((rows, width)),
        ),
        out_shape=jax.ShapeDtypeStruct((rows, width), F32),
        cost_estimate=pl.CostEstimate(
            flops=1_000_000_000, bytes_accessed=8_000_000, transcendentals=0
        ),
        compiler_params=pltpu.CompilerParams(vmem_limit_bytes=8 * 1024 * 1024),
        name="tree",
    )(cache_lengths, tree_parents, *after)


def shrink_kernel(me_ref, owner_ref, adapter_ref, *refs, columns, cut):
    output_ref = refs[-1]
    contract = (((1,), (1,)), ((), ()))
    for b in range(output_ref.shape[0]):
        hidden_ref, away_ref, one_ref, two_ref = refs[4 * b : 4 * b + 4]
        output_ref[b, :, :columns] = away_ref[...]
        partial = lax.dot_general(
            hidden_ref[:, :cut], one_ref[:, columns:], contract, preferred_element_type=F32
        ) + lax.dot_general(hidden_ref[:, cut:], two_ref[...], contract, preferred_element_type=F32)
        output_ref[b, :, columns:] = jnp.concatenate([partial, jnp.zeros_like(partial)], 1)


def shrink_rows(where, slot, hidden_states, away, pieces, tree_size, columns, cut, after):
    rank_size = pieces[0][0].shape[0]
    in_specs, operands = [], []
    for b, (one, two) in enumerate(pieces):
        in_specs += [
            pl.BlockSpec(
                (tree_size, hidden_states.shape[1]),
                lambda i, *refs, b=b: (request_at(refs, slot + b), 0),
            ),
            pl.BlockSpec(
                (tree_size, columns), lambda i, *refs, b=b: (request_at(refs, slot + b), 0)
            ),
            pl.BlockSpec(one.shape, lambda i, *refs: (0, 0)),
            pl.BlockSpec(two.shape, lambda i, *refs: (0, 0)),
        ]
        operands += [hidden_states, away, one, two]
    count = len(pieces)
    width = columns + 2 * rank_size
    return pl.pallas_call(
        functools.partial(shrink_kernel, columns=columns, cut=cut),
        grid_spec=pltpu.PrefetchScalarGridSpec(
            num_scalar_prefetch=3,
            grid=(1,),
            in_specs=in_specs + [ANYWHERE] * len(after),
            out_specs=pl.BlockSpec((count, tree_size, width), lambda i, *refs: (0, 0, 0)),
        ),
        out_shape=jax.ShapeDtypeStruct((count, tree_size, width), F32),
        cost_estimate=pl.CostEstimate(
            flops=count * 30000000, bytes_accessed=count * 200000, transcendentals=0
        ),
        compiler_params=pltpu.CompilerParams(vmem_limit_bytes=14 * 1024 * 1024),
        name="shrink",
    )(*where, *operands, *after)


def finish_kernel(
    me_ref,
    owner_ref,
    adapter_ref,
    length_ref,
    here_ref,
    shrunk_here_ref,
    shrunk_there_ref,
    table_ref,
    gain_ref,
    query_ref,
    key_ref,
    value_ref,
    *rest,
    count,
    slot,
    kv_heads,
):
    expand_refs = rest[:count]
    attention_ref, cache_ref, token_ref, expand_ref = rest[-4:]
    token_ref[...] = jnp.zeros_like(token_ref)
    tree_size, heads, head_size = query_ref.shape
    cached = key_ref.shape[0]
    per_group = heads // kv_heads
    rows = tree_size * heads
    columns = kv_heads * 2 * head_size
    spare = table_ref.shape[1] - 2 * head_size
    score_scale = math.log2(math.e) / math.sqrt(head_size)
    if count == 1:
        expand = expand_refs[0][...]
    else:
        for b in range(count):

            @pl.when(pl.program_id(0) == b)
            def _():
                expand_ref[...] = expand_refs[b][...]

        expand = expand_ref[...]
    length = length_ref[request_at((me_ref, owner_ref, adapter_ref), slot + pl.program_id(0))]
    ranks = slice(columns, columns + expand.shape[0])
    shrunk = shrunk_here_ref[0, :, ranks] + shrunk_there_ref[0, :, ranks]
    high = shrunk.astype(BF16)
    left = shrunk - high.astype(F32)
    middle = left.astype(BF16)
    low = (left - middle.astype(F32)).astype(BF16)
    terms = jnp.dot(jnp.concatenate([low, middle, high], 0), expand, preferred_element_type=F32)
    delta = terms[:tree_size] + terms[tree_size : 2 * tree_size] + terms[2 * tree_size :]
    projected = (here_ref[...] + shrunk_there_ref[0, :, :columns]) + delta
    cosine = table_ref[:, :head_size]
    sine = table_ref[:, head_size : 2 * head_size]
    gain = gain_ref[...]
    new_keys, new_values = [], []
    for g in range(kv_heads):
        at = 2 * head_size * g
        key = projected[:, at : at + head_size]
        new_values.append(projected[:, at + head_size : at + 2 * head_size].astype(BF16))
        norm = lax.rsqrt(jnp.mean(key * key, -1, keepdims=True) + 1e-06)
        key = key * norm * gain
        new_keys.append((key * cosine + pltpu.roll(key, head_size // 2, 1) * sine).astype(BF16))
    pad = jnp.zeros((spare - kv_heads * tree_size, head_size), BF16)
    keys = jnp.concatenate([key_ref[...]] + new_keys + [pad], 0)
    values = jnp.concatenate([value_ref[...]] + new_values + [pad], 0)
    scores = lax.dot_general(
        query_ref[...].reshape(rows, head_size),
        keys,
        (((1,), (1,)), ((), ())),
        preferred_element_type=F32,
    ).reshape(tree_size, heads, cached + spare)
    lane = lax.broadcasted_iota(jnp.int32, (heads, cached), 1)
    mine = lax.broadcasted_iota(jnp.int32, (heads, cached), 0) // per_group
    allowed = (lane % kv_heads == mine) & (lane // kv_heads < length)
    cached_bias = jnp.where(allowed, 0.0, -1e30)
    lane = lax.broadcasted_iota(jnp.int32, (heads, spare), 1)
    first = lax.broadcasted_iota(jnp.int32, (heads, spare), 0) // per_group * tree_size
    head_bias = jnp.where((lane >= first) & (lane < first + tree_size), 0.0, -1e30)
    node_bias = table_ref[:, 2 * head_size :]
    cached_scores = scores[:, :, :cached] + cached_bias[None]
    tree_scores = scores[:, :, cached:] + (node_bias[:, None, :] + head_bias[None])
    top = jnp.maximum(
        jnp.max(cached_scores, -1, keepdims=True), jnp.max(tree_scores, -1, keepdims=True)
    )
    cached_exponent = jnp.exp2((cached_scores - top) * score_scale)
    tree_exponent = jnp.exp2((tree_scores - top) * score_scale)
    total = jnp.sum(cached_exponent, -1, keepdims=True) + jnp.sum(tree_exponent, -1, keepdims=True)
    exponent = jnp.concatenate([cached_exponent, tree_exponent], -1)
    output = jnp.dot(
        exponent.astype(BF16).reshape(rows, cached + spare), values, preferred_element_type=F32
    ).reshape(tree_size, heads, head_size)
    attention_ref[...] = (output * (1.0 / total)).astype(BF16)
    stacked = jnp.concatenate(new_keys + new_values, 0)
    size = stacked.shape[0]
    cache_ref[...] = jnp.dot(
        sorting_matrix(size, size, size // tree_size, tree_size),
        stacked,
        preferred_element_type=F32,
    ).astype(BF16)


def finish(where, slot, batch, shared, previous):
    shrunk_here, shrunk_there, pieces = batch
    lengths, gain, here, table, queries, key_rows, value_rows = shared
    spot = lambda i, refs: request_at(refs[:3], slot + i)
    count, tree_size, width = shrunk_here.shape
    rank_size = pieces[0].shape[0]
    requests = lengths.shape[0]
    rows, heads, head_size = queries.shape
    columns = here.shape[1]
    kv_heads = columns // (2 * head_size)
    row_block = lambda width: pl.BlockSpec((tree_size, width), lambda i, *refs: (spot(i, refs), 0))
    shrunk_block = pl.BlockSpec((1, tree_size, width), lambda i, *refs: (i, 0, 0))
    cached_block = pl.BlockSpec(
        (key_rows.shape[0] // requests, head_size), lambda i, *refs: (spot(i, refs), 0)
    )
    query_block = pl.BlockSpec(
        (tree_size, heads, head_size), lambda i, *refs: (spot(i, refs), 0, 0)
    )
    in_specs = [
        row_block(columns),
        shrunk_block,
        shrunk_block,
        row_block(table.shape[1]),
        pl.BlockSpec((1, head_size), lambda i, *refs: (0, 0)),
        query_block,
        cached_block,
        cached_block,
    ] + [pl.BlockSpec((rank_size, columns), lambda i, *refs: (0, 0))] * count
    operands = [*where, lengths, here, shrunk_here, shrunk_there, table, gain, queries]
    operands += [key_rows, value_rows, *pieces]
    aliases = {}
    if previous is not None:
        aliases = {len(operands): 0, len(operands) + 1: 1}
        operands += previous[:2]
        in_specs += [ANYWHERE] * 2
    cache_rows = 2 * kv_heads * tree_size
    return pl.pallas_call(
        functools.partial(finish_kernel, count=count, slot=slot, kv_heads=kv_heads),
        grid_spec=pltpu.PrefetchScalarGridSpec(
            num_scalar_prefetch=4,
            grid=(count,),
            in_specs=in_specs,
            out_specs=[
                query_block,
                pl.BlockSpec((cache_rows, head_size), lambda i, *refs: (spot(i, refs), 0)),
                pl.BlockSpec((8, 128), lambda i, *refs: (0, 0)),
            ],
            scratch_shapes=[pltpu.VMEM((rank_size, columns), BF16)],
        ),
        out_shape=[
            jax.ShapeDtypeStruct((rows, heads, head_size), BF16),
            jax.ShapeDtypeStruct((rows * 2 * kv_heads, head_size), BF16),
            jax.ShapeDtypeStruct((8, 128), F32),
        ],
        input_output_aliases=aliases,
        cost_estimate=pl.CostEstimate(
            flops=count * 90000000, bytes_accessed=count * 300000, transcendentals=0
        ),
        compiler_params=pltpu.CompilerParams(vmem_limit_bytes=16 * 1024 * 1024),
        name="finish",
    )(*operands)


def per_device(
    hidden_states,
    kv_weight,
    shrink_factors,
    expand_factors,
    adapter_ids,
    cache_lengths,
    tree_parents,
    queries,
    cache_keys,
    cache_values,
    key_gain,
):
    requests, tree_size = tree_parents.shape
    row_count, half_width = hidden_states.shape
    kv_heads, kv_width = (kv_weight.shape[1], kv_weight.shape[2])
    head_size = kv_width // 2
    rank_size = shrink_factors.shape[2]
    context = cache_keys.shape[1]
    pool_count = lax.axis_size("pool")
    heads_here = kv_heads // lax.axis_size("tp")
    columns = heads_here * kv_width
    me = lax.axis_index("pool")
    core = lax.axis_index("tp").astype(jnp.int32).reshape(1)
    swap = [(0, 1), (1, 0)]

    def tile_rows(array):
        lead, heads = array.shape[0], array.shape[1]
        return array.reshape(lead, heads, 2, 128).transpose(0, 2, 1, 3).reshape(-1, 128)

    cut = (half_width + columns) // 2 - columns
    first, second = pack(
        core, shrink_factors[0].T, tile_rows(expand_factors[0]), cut, heads_here
    )

    order = ring_order(pool_count)
    onward = [(order[i], order[(i + 1) % pool_count]) for i in range(pool_count)]
    backward = [(b, a) for a, b in onward]
    half = pool_count // 2
    offsets = [[0]] + [[-step, step] for step in range(1, half)] + [[half]]
    flat_offsets = sum(offsets, [])
    owners = np.zeros((pool_count, pool_count), np.int32)
    for spot, index in enumerate(order):
        owners[index] = [order[(spot + offset) % pool_count] for offset in flat_offsets]
    where = (me.astype(jnp.int32).reshape(1), jnp.asarray(owners), adapter_ids)

    weight_rows = tile_rows(kv_weight)
    key_rows = cache_keys.reshape(-1, head_size)
    value_rows = cache_values.reshape(-1, head_size)

    arrivals = [(first, second)]
    front = rear = (first, second)
    here, away = base_product(
        core, hidden_states, weight_rows, kv_heads * kv_width, [first], []
    )
    split_batches = pool_count == requests
    near = 3
    done = [(None, 0)]
    shared = None

    def finish_batch(group, partial=None):
        outputs, slot = done[-1]
        after = [] if len(done) < 3 else [outputs[2]]
        if partial is None:
            partial = shrink_rows(
                where, slot, hidden_states, away, group, tree_size, columns, cut, after
            )
        batch = (partial, lax.ppermute(partial, "tp", swap), [piece[0] for piece in group])
        done.append((finish(where, slot, batch, shared, outputs), slot + len(group)))

    for step in range(1, half):
        front = tuple(lax.ppermute(piece, "pool", onward) for piece in front)
        rear = tuple(lax.ppermute(piece, "pool", backward) for piece in rear)
        held = [front[1], rear[1]]
        first_front = front[0]
        if step == 1:
            token = away
            if split_batches:
                token = near_partial = shrink_rows(
                    where,
                    0,
                    hidden_states,
                    away,
                    arrivals + [front, rear],
                    tree_size,
                    columns,
                    cut,
                    [],
                )
            held = [hold(piece, token) for piece in held]
            table = tree_tables(
                cache_lengths, tree_parents, head_size, heads_here, [here]
            )
            shared = (
                cache_lengths,
                key_gain.reshape(1, head_size),
                here,
                table,
                queries,
                key_rows,
                value_rows,
            )
        if step == 2 and split_batches:
            finish_batch(arrivals[:near], near_partial)
            first_front, held[1] = hold(first_front, table), hold(held[1], table)
        front, rear = (first_front, held[0]), (rear[0], held[1])
        arrivals += [front, rear]
    arrivals.append(
        (lax.ppermute(front[0], "pool", onward), lax.ppermute(rear[1], "pool", backward))
    )
    if split_batches:
        finish_batch(arrivals[near:-3])
        finish_batch(arrivals[-3:])
        outputs = done[-1][0]
    else:
        parts = [
            shrink_rows(where, slot, hidden_states, away, [piece], tree_size, columns, cut, [])
            for slot, piece in enumerate(arrivals)
        ]
        owners_here = lax.dynamic_index_in_dim(jnp.asarray(owners), me, 0, keepdims=False)
        hot = (adapter_ids[None, :] == owners_here[:, None]).astype(jnp.int32)
        slots = jnp.sum(hot * jnp.arange(pool_count, dtype=jnp.int32)[:, None], 0)
        partial = jnp.concatenate(parts, 0)[slots]
        expands = jnp.stack([piece[0][:, :columns] for piece in arrivals])[slots]
        every = jnp.arange(requests, dtype=jnp.int32)
        batch = (
            partial,
            lax.ppermute(partial, "tp", swap),
            [expands[r] for r in range(requests)],
        )
        outputs = finish((every[:1], every[None, :], every), 0, batch, shared, None)
    attention, cache_rows, _ = outputs
    tree_cache = (
        cache_rows.reshape(row_count, 2, heads_here, head_size)
        .transpose(0, 2, 1, 3)
        .reshape(row_count, heads_here, kv_width)
    )
    return attention, tree_cache


def solution(mesh):
    placed = (
        P(("grp", "pool"), "tp"),
        P("tp", None, None),
        P(("grp", "pool"), "tp", None),
        P(("grp", "pool"), None, None, None),
        P(("grp", "pool")),
        P(("grp", "pool")),
        P(("grp", "pool"), None),
        P(("grp", "pool"), "tp", None),
        P(("grp", "pool"), None, "tp", None),
        P(("grp", "pool"), None, "tp", None),
        P(),
    )
    return jax.shard_map(
        per_device,
        mesh=mesh,
        in_specs=placed,
        out_specs=(P(("grp", "pool"), "tp", None), P(("grp", "pool"), "tp", None)),
        check_vma=False,
    )
```
